128 devices in a mesh: dom: 32 (over y, x, core), band: 4 (over z).
Axes of the slice: x: 4, y: 4, z: 4, core: 2. Of those that a mesh axis runs over, the one named last changes fastest.
Arguments:
- block: float32 [64, 442368], P('band', 'dom')
- stiffness: float32 [343, 343], replicated
- cell_scale: float32 [2048], P('dom'), may hold values from 0.3 to 3
- potential: float32 [343, 2048], P(None, 'dom'), may hold values from 0.1 to 2
- cell_dofs: int32 [343, 2048], P(None, 'dom'), may hold values from 0 to 17919, as said below
- cell_count: int32 [32], P('dom'), may hold values from 32 to 64, as said below
- hang_rows: int32 [27648], P('dom'), may hold values from 0 to 13823, as said below
- hang_masters: int32 [4, 27648], P(None, 'dom'), may hold values from 0 to 13823, as said below
- hang_weights: float32 [4, 27648], P(None, 'dom'), may hold values from 0.1 to 0.6
Outputs:
- basis: float32 [64, 442368], P('band', 'dom')
The draws below stay inside these ranges and needn't reach their ends.
Inputs may be any that keep to these rules, and one draw needn't show every extreme that they name: `cell_dofs`: each cell's 343 rows are distinct and lie within a window of 686 rows of the extended vector of 17920 rows. `cell_count`: every shard has at least 32 live cells; some shard has exactly 64. `hang_rows`: within a shard the hanging rows are distinct and none of them is a master. `hang_masters`: masters are owned rows of the same shard.
All inputs are finite; a program needn't handle non-finite values.
Results may differ from the reference program's by a relative error of at most 0.00026.
Values sent between devices are 32-bit elements; how exact they have to be, the bound alone decides.
No kernel may reach another device: no remote copies, remote signals or barrier semaphores. Data moves between devices by JAX's collectives and lax.ppermute only.
A program may use at most 192 MiB of HBM per device.

```python
import math
import jax
import jax.numpy as jnp
from jax import lax

NSTATE = 64
NODES = 343
CELLS = 64
LOC = 13824
RIM = 2048
HANG = 864
MASTERS = 4
NDOF = 442368
CELLS_ALL = 2048
HANG_ALL = 27648
N_DOM = 32


def hanging_tables(key):
    shards = NDOF // LOC
    keys = jax.random.split(jax.random.fold_in(key, 71), shards)
    orders = jax.vmap(lambda k: jax.random.permutation(k, LOC))(keys)
    picks = jax.random.randint(jax.random.fold_in(key, 72), (shards, MASTERS, HANG), HANG, LOC)
    masters = jnp.take_along_axis(jnp.broadcast_to(orders[:, None, :], (shards, MASTERS, LOC)), picks, axis=2)
    rows = orders[:, :HANG].reshape(-1).astype(jnp.int32)
    masters = jnp.transpose(masters, (1, 0, 2)).reshape(MASTERS, -1).astype(jnp.int32)
    return (rows, masters)


def draw_hang_rows(key, part):
    rows, masters = hanging_tables(key)
    return rows


def draw_hang_masters(key, part):
    rows, masters = hanging_tables(key)
    return masters


def draw_cell_dofs(key, part):
    key = jax.random.fold_in(key, 5)
    k1, k2 = jax.random.split(key)
    top_base = LOC + 2 * RIM - 2 * NODES
    base = jax.random.randint(k1, (1, CELLS_ALL), 0, top_base + 1)
    slot = (jnp.arange(CELLS_ALL) % CELLS)[None, :]
    base = jnp.where(slot == 0, 0, jnp.where(slot == 1, top_base, base))
    offsets = 2 * jnp.arange(NODES, dtype=jnp.int32)[:, None] + jax.random.randint(k2, (NODES, CELLS_ALL), 0, 2)
    return (base + offsets).astype(jnp.int32)


def draw_cell_count(key, part):
    key = jax.random.fold_in(key, 9)
    k1, k2 = jax.random.split(key)
    shards = NDOF // LOC
    counts = jax.random.randint(k1, (shards,), CELLS // 2, CELLS + 1)
    full = jax.random.randint(k2, (), 0, shards)
    return counts.at[full].set(CELLS).astype(jnp.int32)


def draw_stiffness(key, part):
    key = jax.random.fold_in(key, 13)
    k1, k2 = jax.random.split(key)
    diag = jax.random.uniform(k1, (NODES,), jnp.float32, 1.0, 2.0)
    off = jax.random.uniform(k2, (NODES, NODES), jnp.float32, -1.0, 1.0) / NODES
    off = 0.5 * (off + off.T)
    off = off * (1.0 - jnp.eye(NODES, dtype=jnp.float32))
    return jnp.diag(diag) + off


def draw_block(key, part):
    key = jax.random.fold_in(key, 17)
    k1, k2, k3, k4 = jax.random.split(key, 4)
    shards = NDOF // LOC
    rise = (jnp.arange(NDOF) // LOC).astype(jnp.float32) / max(shards - 1, 1)
    noise = jax.random.normal(k1, (NSTATE, NDOF), jnp.float32)
    share = jax.random.uniform(k3, (NSTATE, 1), jnp.float32, 0.3, 0.8)
    factor = jnp.exp(rise * jnp.log(3.0))
    common = jax.random.normal(k2, (1, NDOF), jnp.float32)
    scales = jnp.exp(jax.random.uniform(k4, (NSTATE, 1), jnp.float32, 0.0, jnp.log(10.0)))
    return scales * (noise + share * common) * factor[None, :] * 0.3


def block_scale(own_key, shape, pieces, low, top_value):
    def one(position, shards_of):
        draws = jax.random.uniform(jax.random.fold_in(jax.random.fold_in(own_key, 6), position), (shards_of,), jnp.float32, low / len(pieces), top_value / len(pieces))
        return jnp.repeat(jnp.exp(draws), shape[position] // shards_of).reshape((-1,) + (1,) * (len(shape) - position - 1))

    factor_of = one(*pieces[0])
    for cut in pieces[1:]:
        factor_of = factor_of * one(*cut)
    return factor_of


def setup_inputs(seed: int = 0) -> dict:
    key_list = jax.random.split(jax.random.key(seed), 10)
    return {
        "block": draw_block(jax.random.fold_in(key_list[9], 71), 0),
        "stiffness": draw_stiffness(jax.random.fold_in(key_list[9], 71), 0),
        "cell_scale": jnp.clip(jnp.exp(math.log(3.0) - 2.3025851 * jax.random.uniform(key_list[2], (CELLS_ALL,), jnp.float32) ** block_scale(key_list[2], (CELLS_ALL,), ((0, 32),), -0.2, 0.2)), 0.3, 3.0),
        "potential": jnp.clip(jnp.exp(math.log(2.0) - 2.9957323 * jax.random.uniform(key_list[3], (NODES, CELLS_ALL), jnp.float32) ** block_scale(key_list[3], (NODES, CELLS_ALL), ((1, 32),), -0.2, 0.2)), 0.1, 2.0),
        "cell_dofs": draw_cell_dofs(jax.random.fold_in(key_list[9], 71), 0),
        "cell_count": draw_cell_count(jax.random.fold_in(key_list[9], 71), 0),
        "hang_rows": draw_hang_rows(jax.random.fold_in(key_list[9], 71), 0),
        "hang_masters": draw_hang_masters(jax.random.fold_in(key_list[9], 71), 0),
        "hang_weights": jnp.clip(0.1 + 0.5 * jax.random.uniform(key_list[8], (MASTERS, HANG_ALL), jnp.float32) ** block_scale(key_list[8], (MASTERS, HANG_ALL), ((1, 32),), -0.2, 0.2), 0.1, 0.6),
    }


def distribute(v, hang_g, masters_g, hang_weights):
    vals = lax.optimization_barrier(jnp.sum(hang_weights[None] * v[:, masters_g], axis=1))
    return v.at[:, hang_g].set(vals)

def condense(y, hang_g, masters_g, hang_weights):
    states = y.shape[0]
    contrib = hang_weights[None] * y[:, hang_g][:, None, :]
    y = y.at[:, masters_g.reshape(-1)].add(contrib.reshape(states, -1))
    return y.at[:, hang_g].set(jnp.zeros((states, hang_g.shape[0]), jnp.float32))

def reference(block, stiffness, cell_scale, potential, cell_dofs, cell_count, hang_rows, hang_masters, hang_weights):
    states, total = block.shape
    shard_of = (jnp.arange(HANG_ALL) // HANG).astype(jnp.int32)
    hang_g = hang_rows + shard_of * LOC
    masters_g = hang_masters + shard_of[None, :] * LOC

    def apply(v):
        u = distribute(v, hang_g, masters_g, hang_weights)
        padded = jnp.pad(u, ((0, 0), (RIM, RIM)))

        def shard_step(d, acc):
            start = (d * CELLS).astype(jnp.int32)
            dofs = lax.dynamic_slice_in_dim(cell_dofs, start, CELLS, 1) + d * LOC
            scales = lax.dynamic_slice_in_dim(cell_scale, start, CELLS, 0)
            pots = lax.dynamic_slice_in_dim(potential, start, CELLS, 1)
            alive = (jnp.arange(CELLS) < cell_count[d]).astype(jnp.float32)
            gathered = padded[:, dofs]
            prod = jnp.einsum('ij,sjc->sic', stiffness, gathered, precision=lax.Precision.HIGHEST)
            out = (scales[None, None, :] * prod + pots[None] * gathered) * alive[None, None, :]
            return acc.at[:, dofs].add(out)
        acc = lax.fori_loop(0, N_DOM, shard_step, jnp.zeros_like(padded))
        return condense(acc[:, RIM:RIM + total], hang_g, masters_g, hang_weights)
    centre = 4.5
    half = 3.5
    first = (apply(block) - centre * block) / half
    second = 2.0 * (apply(first) - centre * first) / half - block
    third = 2.0 * (apply(second) - centre * second) / half - first
    filtered = distribute(third, hang_g, masters_g, hang_weights)
    intersection = jnp.dot(filtered, filtered.T, precision=lax.Precision.HIGHEST)
    factor = jnp.linalg.cholesky(intersection)
    inverse = lax.linalg.triangular_solve(factor, jnp.eye(states, dtype=jnp.float32), left_side=True, lower=True)
    basis = jnp.dot(inverse, filtered, precision=lax.Precision.HIGHEST)
    return basis * jnp.sqrt(jnp.float32(total))
```

```python
import functools
import jax
import jax.numpy as jnp
from jax import lax
from jax.experimental import pallas as pl
from jax.experimental.pallas import tpu as pltpu
from jax.sharding import PartitionSpec as P

RIM = 2048
NODES = 343
HANG = 864
MASTERS = 4
LOC = 13824
CELLS = 64
S = 16
L = 128
EXT = LOC + 2 * RIM
NB = LOC // L
RB = RIM // L
NPAD = 384
NJ = NPAD // L
WB = 7
TOPB = EXT // L - WB
SLOTS = 3 * CELLS
GROUP = 16
HPAD = 896
HB = HPAD // L
ME = MASTERS * HPAD
HE = 1024
E = ME + HE
QLO = 256
QHI = 18
BIG = 1 << 20
CENTRE = 4.5
HALF = 3.5
F32 = jnp.float32
BF16 = jnp.bfloat16
I32 = jnp.int32
VLIM = 40 * 1024 * 1024

VM = pl.BlockSpec(memory_space=pltpu.VMEM)
SM = pl.BlockSpec(memory_space=pltpu.SMEM)
NT = (((1,), (1,)), ((), ()))


def iota(shape, dim):
    return lax.broadcasted_iota(I32, shape, dim)


def lanes(x, idx):
    return jnp.take_along_axis(x, idx, axis=1, mode="promise_in_bounds")


def nn(a, b):
    return jnp.dot(a, b, preferred_element_type=F32)


def nt(a, b):
    return lax.dot_general(a, b, NT, preferred_element_type=F32)


def split(x):
    hi = x.astype(BF16)
    return hi, (x - hi.astype(F32)).astype(BF16)


def at(b):
    return pl.ds(pl.multiple_of(b * L, L), L)


def hang_tables(ent_ref, a_ref, b_ref, lhs_ref, oh_ref, pe_ref, src_ref, posr_ref, hq_ref, start_ref):
    for i in range(E // L):
        col = slice(i * L, (i + 1) * L)
        row = jnp.broadcast_to(ent_ref[0:1, col], (L, L))
        it = iota((L, L), 0)
        a_ref[:, col] = (it == (row >> 7)).astype(F32).astype(BF16)
        b_ref[:, col] = (((row & 127) == it) & (row >= 0)).astype(F32).astype(BF16)
    flag = nt(a_ref[...], b_ref[...]) > 0.5
    flagb = flag.astype(F32).astype(BF16)
    tri = (iota((L, L), 0) < iota((L, L), 1)).astype(F32).astype(BF16)
    low = (iota((L, L), 1) < iota((L, L), 0)).astype(F32).astype(BF16)
    ones = jnp.ones((L, L), BF16)
    total = nn(flagb, ones)
    pos = nn(flagb, tri) + nn(low, total.astype(BF16))
    pos = pos.astype(I32)
    posr_ref[...] = jnp.where(flag, pos, -1)
    totrow = nt(jnp.ones((8, L), BF16), flagb)
    start_ref[...] = nn(totrow.astype(BF16), tri).astype(I32)
    ph = (pos >> 8).astype(F32).astype(BF16)
    plo = (pos & 255).astype(F32).astype(BF16)
    for i in range(E // L):
        col = slice(i * L, (i + 1) * L)
        ent = ent_ref[0:1, col]
        mask = a_ref[:, col].astype(F32)
        b = b_ref[:, col]
        hi = jnp.sum(nn(ph, b) * mask, axis=0, keepdims=True)
        lo = jnp.sum(nn(plo, b) * mask, axis=0, keepdims=True)
        pe = jnp.where(ent >= 0, hi.astype(I32) * QLO + lo.astype(I32), BIG)
        pe_ref[0:1, col] = pe
        good = jnp.broadcast_to(pe, (QLO, L))
        oh_ref[:, col] = ((good & 255) == iota((QLO, L), 0)).astype(F32).astype(BF16)
        qm = (jnp.broadcast_to(pe >> 8, (24, L)) == iota((24, L), 0)).astype(F32)
        lhs_ref[0:24, col] = qm.astype(BF16)
        lhs_ref[24:48, col] = (qm * (ent >> 7).astype(F32)).astype(BF16)
        lhs_ref[48:72, col] = (qm * (ent & 127).astype(F32)).astype(BF16)
        lhs_ref[72:96, col] = (qm if i >= ME // L else jnp.zeros_like(qm)).astype(BF16)
    res = nt(lhs_ref[...], oh_ref[...])
    cnt = res[0:24]
    den = jnp.maximum(cnt, 1.0)
    blk = (res[24:48] / den + 0.5).astype(I32)
    lo = (res[48:72] / den + 0.5).astype(I32)
    src = jnp.where(cnt > 0.5, blk * L + lo, -1)
    for q in range(24):
        src_ref[2 * q : 2 * q + 1, :] = src[q : q + 1, 0:L]
        src_ref[2 * q + 1 : 2 * q + 2, :] = src[q : q + 1, L : 2 * L]
    hq_ref[...] = res[72:96]


def zat(c):
    return pl.ds(pl.multiple_of((c >> 1) * S, S), S), pl.ds(pl.multiple_of((c & 1) * L, L), L)


def compress(y_ref, yoff, z_ref, src_ref, start_ref):
    z_ref[...] = jnp.zeros_like(z_ref)

    def step(b, _):
        y = y_ref[:, at(b + yoff)]
        c0 = start_ref[0, b] >> 7
        for t in range(2):
            c = c0 + t
            row = jnp.broadcast_to(src_ref[pl.ds(c, 1), :], (S, L))
            r, l = zat(c)
            z_ref[r, l] = jnp.where((row >> 7) == b, lanes(y, row & 127), z_ref[r, l])
        return 0

    lax.fori_loop(0, NB, step, 0, unroll=6)


def expand(b, y, z_ref, posr_ref, start_ref):
    row = jnp.broadcast_to(posr_ref[pl.ds(b, 1), :], (S, L))
    c0 = start_ref[0, b] >> 7
    for t in range(2):
        c = c0 + t
        r, l = zat(c)
        y = jnp.where((row >> 7) == c, lanes(z_ref[r, l], row & 127), y)
    return y


def gather_entries(z_ref, oh_ref, pe_ref, g_ref, first, last):
    zh, zl = split(z_ref[...])
    for i in range(first // QLO, last // QLO):
        col = slice(i * QLO, (i + 1) * QLO)
        oh = oh_ref[:, col]
        g = nn(zh, oh) + nn(zl, oh)
        q = jnp.broadcast_to(pe_ref[0:1, col] >> 8, (S, QLO))
        acc = jnp.zeros((S, QLO), F32)
        for h in range(QHI):
            acc = jnp.where(q == h, g[h * S : (h + 1) * S], acc)
        g_ref[:, col] = acc


def scatter_entries(g_ref, oh_ref, pe_ref, lh_ref, ll_ref, first, last):
    for i in range(first // L, last // L):
        col = slice(i * L, (i + 1) * L)
        g = g_ref[:, col]
        hi = g.astype(BF16).astype(F32)
        lo = g - hi
        q = jnp.broadcast_to(pe_ref[0:1, col] >> 8, (S, L))
        for h in range(QHI):
            m = q == h
            lh_ref[h * S : (h + 1) * S, col] = jnp.where(m, hi, 0.0).astype(BF16)
            ll_ref[h * S : (h + 1) * S, col] = jnp.where(m, lo, 0.0).astype(BF16)
    oh = oh_ref[:, first:last]
    return nt(lh_ref[:, first:last], oh) + nt(ll_ref[:, first:last], oh)


def hanging_values(z_ref, oh_ref, pe_ref, w_ref, g_ref, lh_ref, ll_ref, hq_ref):
    gather_entries(z_ref, oh_ref, pe_ref, g_ref, 0, ME)
    g_ref[:, ME + HPAD :] = jnp.zeros((S, HE - HPAD), F32)
    for j in range(HB):
        acc = jnp.zeros((S, L), F32)
        for k in range(MASTERS):
            col = slice(k * HPAD + j * L, k * HPAD + (j + 1) * L)
            acc = acc + g_ref[:, col] * w_ref[0:1, col]
        g_ref[:, ME + j * L : ME + (j + 1) * L] = acc
    cz = scatter_entries(g_ref, oh_ref, pe_ref, lh_ref, ll_ref, ME, E)
    for h in range(QHI):
        r = slice(h * S, (h + 1) * S)
        m = jnp.broadcast_to(hq_ref[h : h + 1, :], (S, QLO)) > 0.5
        z_ref[r, :] = jnp.where(m, cz[r], z_ref[r, :])


def add_to_masters(z_ref, oh_ref, pe_ref, w_ref, g_ref, lh_ref, ll_ref):
    gather_entries(z_ref, oh_ref, pe_ref, g_ref, ME, E)
    for j in range(HB):
        y = g_ref[:, ME + j * L : ME + (j + 1) * L]
        for k in range(MASTERS):
            col = slice(k * HPAD + j * L, k * HPAD + (j + 1) * L)
            g_ref[:, col] = y * w_ref[0:1, col]
    z_ref[...] += scatter_entries(g_ref, oh_ref, pe_ref, lh_ref, ll_ref, 0, ME)


def prepare_kernel(
    ent_ref, w_ref, block_ref,
    oh_ref, pe_ref, src_ref, posr_ref, hq_ref, start_ref, u_ref, left_ref, right_ref,
    a_ref, b_ref, lhs_ref, z_ref, g_ref, lh_ref, ll_ref, start_s, sem,
):
    hang_tables(ent_ref, a_ref, b_ref, lhs_ref, oh_ref, pe_ref, src_ref, posr_ref, hq_ref, start_ref)
    copy = pltpu.make_async_copy(start_ref, start_s, sem)
    copy.start()
    copy.wait()
    compress(block_ref, 0, z_ref, src_ref, start_s)
    hanging_values(z_ref, oh_ref, pe_ref, w_ref, g_ref, lh_ref, ll_ref, hq_ref)

    def step(b, _):
        u_ref[:, at(b)] = expand(b, block_ref[:, at(b)], z_ref, posr_ref, start_s)
        return 0

    lax.fori_loop(0, NB, step, 0, unroll=6)
    left_ref[...] = u_ref[:, 0:RIM]
    right_ref[...] = u_ref[:, LOC - RIM :]


def sds(shape, dtype=F32):
    return jax.ShapeDtypeStruct(shape, dtype)


HANG_SCRATCH = [
    pltpu.VMEM((QHI * S, QLO), F32),
    pltpu.VMEM((S, E), F32),
    pltpu.VMEM((QHI * S, E), BF16),
    pltpu.VMEM((QHI * S, E), BF16),
]


def prepare(ent, w, block):
    return pl.pallas_call(
        prepare_kernel,
        out_shape=(
            sds((QLO, E), BF16),
            sds((1, E), I32),
            sds((48, L), I32),
            sds((L, L), I32),
            sds((24, QLO)),
            sds((8, L), I32),
            sds((S, LOC)),
            sds((S, RIM)),
            sds((S, RIM)),
        ),
        in_specs=[VM] * 3,
        out_specs=(VM,) * 9,
        scratch_shapes=[
            pltpu.VMEM((L, E), BF16),
            pltpu.VMEM((L, E), BF16),
            pltpu.VMEM((96, E), BF16),
            *HANG_SCRATCH,
            pltpu.SMEM((8, L), I32),
            pltpu.SemaphoreType.DMA,
        ],
        compiler_params=pltpu.CompilerParams(vmem_limit_bytes=VLIM),
        name="prepare",
    )(ent, w, block)


def cells_kernel(own_ref, left_ref, right_ref, tab_ref, pot_ref, b0_ref, all_ref, meta_ref, meta_s, list_s, sem):
    for i, (ref, shift) in enumerate(((own_ref, 0), (left_ref, -LOC), (right_ref, LOC))):
        r = slice(i * CELLS, (i + 1) * CELLS)
        dofs = ref[:, 0:NPAD].astype(I32) + shift
        real = iota((CELLS, NPAD), 1) < NODES
        all_ref[r, 0:NPAD] = jnp.where(real, dofs, BIG).astype(F32)
        all_ref[r, NPAD:] = ref[:, NPAD:]
        low = jnp.min(jnp.where(real, dofs, BIG).astype(F32), axis=1, keepdims=True)
        top = jnp.max(jnp.where(real, dofs, -BIG).astype(F32), axis=1, keepdims=True)
        live = ref[:, 2 * NPAD + 1 : 2 * NPAD + 2] > 0.5
        used = live & (top >= RIM) & (low < RIM + LOC)
        base = jnp.clip(low.astype(I32) >> 7, 0, TOPB)
        meta_ref[r, :] = jnp.broadcast_to(jnp.where(used, base, -1), (CELLS, L))
    copy = pltpu.make_async_copy(meta_ref, meta_s, sem)
    copy.start()
    copy.wait()

    def scan(c, n):
        b = meta_s[c, 0]
        list_s[n] = c
        b0_ref[n] = b
        return n + jnp.where(b >= 0, 1, 0)

    n = lax.fori_loop(0, SLOTS, scan, 0, unroll=4)

    def blank(i, _):
        list_s[n + i] = 0
        b0_ref[n + i] = 0
        return 0

    lax.fori_loop(0, GROUP, blank, 0)
    groups = (n + GROUP - 1) // GROUP
    b0_ref[SLOTS + 2 * GROUP - 1] = groups

    def one(slot):
        c = list_s[slot]
        b0 = b0_ref[slot]
        valid = slot < n
        vals = all_ref[pl.ds(c, 1), :]
        rel = vals[:, 0:NPAD].astype(I32) - b0 * L
        rel = jnp.where(valid & (rel < WB * L), rel, BIG)
        hi = rel >> 7
        lo = rel & 127
        it = iota((L, NPAD), 0)
        oh = ((jnp.broadcast_to(lo, (L, NPAD)) == it)).astype(F32).astype(BF16)
        node = iota((8, NPAD), 1)
        m = jnp.broadcast_to(hi, (8, NPAD)) == iota((8, NPAD), 0)
        first = jnp.where(m, (node >> 7) + 1, 0).astype(F32)
        second = jnp.where(m, node & 127, 0).astype(F32)
        res = nt(jnp.concatenate([first, second], 0).astype(BF16), oh)
        nh = res[0:8].astype(I32)
        inv = jnp.where(nh > 0, (nh - 1) * L + res[8:16].astype(I32), BIG)
        tab_ref[slot, 8:16, :] = inv
        for j in range(NJ):
            tab_ref[slot, j : j + 1, :] = rel[:, j * L : (j + 1) * L]
            pot_ref[slot, j : j + 1, :] = vals[:, NPAD + j * L : NPAD + (j + 1) * L]
        pot_ref[slot, 3:4, :] = jnp.broadcast_to(vals[:, 2 * NPAD : 2 * NPAD + 1], (1, L))

    def four(i, _):
        for k in range(4):
            one(i * 4 + k)
        return 0

    lax.fori_loop(0, groups * (GROUP // 4), four, 0)


def cell_tables(own, left, right):
    return pl.pallas_call(
        cells_kernel,
        out_shape=(sds((SLOTS, 16, L), I32), sds((SLOTS, 8, L)), sds((SLOTS + 2 * GROUP,), I32)),
        in_specs=[VM] * 3,
        out_specs=(VM, VM, SM),
        scratch_shapes=[
            pltpu.VMEM((SLOTS, 7 * L), F32),
            pltpu.VMEM((SLOTS, L), I32),
            pltpu.SMEM((SLOTS, L), I32),
            pltpu.SMEM((SLOTS + 2 * GROUP,), I32),
            pltpu.SemaphoreType.DMA,
        ],
        compiler_params=pltpu.CompilerParams(vmem_limit_bytes=VLIM),
        name="cell_tables",
    )(own, left, right)


def step_kernel(number, *refs):
    (u_ref, gl_ref, gr_ref, prev_ref, tab_ref, pot_ref, kt_ref,
     oh_ref, pe_ref, src_ref, posr_ref, hq_ref, w_ref, b0_ref, start_ref, me_ref) = refs[:16]
    outs = refs[16 : 16 + (4 if number == 3 else 3)]
    ext_ref, acc_ref, x_ref, p_ref, kh_ref, kl_ref, z_ref, g_ref, lh_ref, ll_ref = refs[16 + len(outs) :]
    kh_ref[...], kl_ref[...] = split(kt_ref[...])
    ext_ref[:, 0:RIM] = gl_ref[...]
    ext_ref[:, RIM : RIM + LOC] = u_ref[...]
    ext_ref[:, RIM + LOC :] = gr_ref[...]
    acc_ref[...] = jnp.zeros_like(acc_ref)
    groups = b0_ref[SLOTS + 2 * GROUP - 1]

    def load(slot):
        b0 = b0_ref[slot]
        for j in range(NJ):
            row = jnp.broadcast_to(tab_ref[slot, j : j + 1, :], (8, L))
            lo, hi = row & 127, row >> 7
            for s in range(2):
                acc = jnp.zeros((8, L), F32)
                for k in range(WB):
                    acc = jnp.where(hi == k, lanes(ext_ref[8 * s : 8 * s + 8, at(b0 + k)], lo), acc)
                x_ref[pl.ds(slot * S + 8 * s, 8), j * L : (j + 1) * L] = acc

    def loads(i, _):
        for k in range(4):
            load(i * 4 + k)
        return 0

    lax.fori_loop(0, groups * (GROUP // 4), loads, 0)

    def product(i, _):
        r = pl.ds(pl.multiple_of(i * (GROUP * S), GROUP * S), GROUP * S)
        xh, xl = split(x_ref[r, :])
        kh, kl = kh_ref[...], kl_ref[...]
        p_ref[r, :] = nn(xh, kh) + (nn(xl, kh) + nn(xh, kl))
        return 0

    lax.fori_loop(0, groups, product, 0)

    def store(slot):
        b0 = b0_ref[slot]
        scale = jnp.broadcast_to(pot_ref[slot, 3:4, :], (8, L))
        vals = []
        for s in range(2):
            r = pl.ds(slot * S + 8 * s, 8)
            vals.append([])
            for j in range(NJ):
                col = slice(j * L, (j + 1) * L)
                pot = jnp.broadcast_to(pot_ref[slot, j : j + 1, :], (8, L))
                vals[s].append(scale * p_ref[r, col] + pot * x_ref[r, col])
        for k in range(WB):
            row = jnp.broadcast_to(tab_ref[slot, 8 + k : 9 + k, :], (8, L))
            lo, hi = row & 127, row >> 7
            for s in range(2):
                acc = jnp.zeros((8, L), F32)
                for j in range(NJ):
                    acc = jnp.where(hi == j, lanes(vals[s][j], lo), acc)
                acc_ref[8 * s : 8 * s + 8, at(b0 + k)] += acc

    def stores(i, _):
        for k in range(4):
            store(i * 4 + k)
        return 0

    lax.fori_loop(0, groups * (GROUP // 4), stores, 0)

    compress(acc_ref, RB, z_ref, src_ref, start_ref)
    add_to_masters(z_ref, oh_ref, pe_ref, w_ref, g_ref, lh_ref, ll_ref)
    hanging_values(z_ref, oh_ref, pe_ref, w_ref, g_ref, lh_ref, ll_ref, hq_ref)
    new_ref = outs[0] if number < 3 else ext_ref

    def finish(b, _):
        t = expand(b, acc_ref[:, at(b + RB)], z_ref, posr_ref, start_ref)
        r = (t - CENTRE * u_ref[:, at(b)]) * ((1.0 if number == 1 else 2.0) / HALF)
        if number > 1:
            r = r - prev_ref[:, at(b)]
        new_ref[:, at(b)] = r
        return 0

    lax.fori_loop(0, NB, finish, 0, unroll=6)
    if number < 3:
        outs[1][...] = new_ref[:, 0:RIM]
        outs[2][...] = new_ref[:, LOC - RIM :]
    else:
        me = me_ref[0]
        q = LOC // 4
        for k in range(4):
            outs[k][...] = new_ref[:, pl.ds(pl.multiple_of(((me + k) & 3) * q, L), q)]


def apply_step(number, u, gl, gr, prev, tab, pot, b0, kt, hang, w, start, me):
    oh, pe, src, posr, hq = hang
    if number == 3:
        shapes = (sds((S, LOC // 4)),) * 4
    else:
        shapes = (sds((S, LOC)), sds((S, RIM)), sds((S, RIM)))
    return pl.pallas_call(
        functools.partial(step_kernel, number),
        out_shape=shapes,
        in_specs=[VM] * 13 + [SM] * 3,
        out_specs=(VM,) * len(shapes),
        scratch_shapes=[
            pltpu.VMEM((S, EXT), F32),
            pltpu.VMEM((S, EXT), F32),
            pltpu.VMEM((SLOTS * S, NPAD), F32),
            pltpu.VMEM((SLOTS * S, NPAD), F32),
            pltpu.VMEM((NPAD, NPAD), BF16),
            pltpu.VMEM((NPAD, NPAD), BF16),
            *HANG_SCRATCH,
        ],
        compiler_params=pltpu.CompilerParams(vmem_limit_bytes=VLIM),
        name=f"step{number}",
    )(u, gl, gr, prev, tab, pot, kt, oh, pe, src, posr, hq, w, b0, start, me)


def gram_kernel(q0_ref, q1_ref, q2_ref, q3_ref, me_ref, gram_ref, all_ref):
    me = me_ref[0]
    for k, ref in enumerate((q0_ref, q1_ref, q2_ref, q3_ref)):
        all_ref[pl.ds(pl.multiple_of(((me - k) & 3) * S, S), S), :] = ref[...]
    a = all_ref[...]
    gram_ref[...] = lax.dot_general(a, a, NT, preferred_element_type=F32, precision=lax.Precision.HIGHEST)


def gram_of(qs, me):
    n = qs[0].shape[1]
    return pl.pallas_call(
        gram_kernel,
        out_shape=(sds((4 * S, 4 * S)), sds((4 * S, n))),
        in_specs=[VM] * 4 + [SM],
        out_specs=(VM, VM),
        compiler_params=pltpu.CompilerParams(vmem_limit_bytes=VLIM),
        name="gram",
    )(*qs, me)


def basis_kernel(total, gram_ref, all_ref, me_ref, o0_ref, o1_ref, o2_ref, o3_ref, m_ref, r_ref):
    n = 4 * S
    eye = (iota((n, n), 0) == iota((n, n), 1)).astype(F32)
    m_ref[...] = jnp.concatenate([gram_ref[...], eye], 1)
    row_id = iota((n, 2 * n), 0)

    m = m_ref[...]
    diag = jnp.zeros((n, 1), F32)
    for j in range(n):
        pivot = m[j : j + 1, :]
        d = pivot[:, j : j + 1]
        f = m[:, j : j + 1] / d
        m = m - jnp.where(row_id > j, f, 0.0) * pivot
    dg = jnp.sum(jnp.where(row_id == iota((n, 2 * n), 1), m, 0.0), axis=1, keepdims=True)
    inv = m[:, n:] * lax.rsqrt(dg) * jnp.sqrt(jnp.float32(total))
    r_ref[...] = jnp.dot(inv, all_ref[...], preferred_element_type=F32, precision=lax.Precision.HIGHEST)
    me = me_ref[0]
    for k, ref in enumerate((o0_ref, o1_ref, o2_ref, o3_ref)):
        ref[...] = r_ref[pl.ds(pl.multiple_of(((me + k) & 3) * S, S), S), :]


def basis_of(gram, rows, me, total):
    n = rows.shape[1]
    return pl.pallas_call(
        functools.partial(basis_kernel, total),
        out_shape=(sds((S, n)),) * 4,
        in_specs=[VM, VM, SM],
        out_specs=(VM,) * 4,
        scratch_shapes=[pltpu.VMEM((4 * S, 8 * S), F32), pltpu.VMEM((4 * S, n), F32)],
        compiler_params=pltpu.CompilerParams(vmem_limit_bytes=VLIM),
        name="basis",
    )(gram, rows, me)


def join_kernel(q0_ref, q1_ref, q2_ref, q3_ref, me_ref, out_ref):
    me = me_ref[0]
    n = q0_ref.shape[1]
    for k, ref in enumerate((q0_ref, q1_ref, q2_ref, q3_ref)):
        out_ref[:, pl.ds(pl.multiple_of(((me - k) & 3) * n, L), n)] = ref[...]


def join(qs, me):
    return pl.pallas_call(
        join_kernel,
        out_shape=sds((S, LOC)),
        in_specs=[VM] * 4 + [SM],
        out_specs=VM,
        compiler_params=pltpu.CompilerParams(vmem_limit_bytes=VLIM),
        name="join",
    )(*qs, me)


def shift(x, axis, by, wrap):
    size = lax.axis_size(axis)
    pairs = [(i, (i + by) % size) for i in range(size) if wrap or 0 <= i + by < size]
    return lax.ppermute(x, axis, pairs)


def swap(x, axis, bits):
    size = lax.axis_size(axis)
    return lax.ppermute(x, axis, [(i, i ^ bits) for i in range(size)])


def summed(g):
    g = g + swap(g, "dom", 1)
    for axis, unit in (("dom", 2), ("dom", 8), ("band", 1)):
        others = [swap(g, axis, unit * k) for k in (1, 2, 3)]
        g = (g + others[0]) + (others[1] + others[2])
    return g


def body(
    block,
    stiffness,
    cell_scale,
    potential,
    cell_dofs,
    cell_count,
    hang_rows,
    hang_masters,
    hang_weights,
):
    me = lax.axis_index("band").astype(I32).reshape(1)
    pad = ((0, 0), (0, NPAD - NODES))
    alive = (jnp.arange(CELLS) < cell_count[0]).astype(F32)
    extra = jnp.concatenate([cell_scale[:, None], alive[:, None], jnp.zeros((CELLS, L - 2), F32)], 1)
    own = jnp.concatenate(
        [jnp.pad(cell_dofs.T.astype(F32), pad), jnp.pad(potential.T, pad), extra], axis=1
    )
    from_left = shift(own, "dom", 1, False)
    from_right = shift(own, "dom", -1, False)

    kt = jnp.pad(stiffness.T, ((0, NPAD - NODES), (0, NPAD - NODES)))
    hpad = ((0, 0), (0, HPAD - HANG))
    ent = jnp.concatenate(
        [
            jnp.pad(hang_masters, hpad, constant_values=-1).reshape(1, ME),
            jnp.pad(hang_rows[None], ((0, 0), (0, HE - HANG)), constant_values=-1),
        ],
        axis=1,
    )
    w = jnp.pad(hang_weights, hpad).reshape(1, ME)

    *hang, start, u0, first, last = prepare(ent, w, block)
    tab, pot, b0 = cell_tables(own, from_left, from_right)

    def ghosts(first, last):
        return shift(last, "dom", 1, False), shift(first, "dom", -1, False)

    args = (tab, pot, b0, kt, hang, w, start, me)
    gl, gr = ghosts(first, last)
    u1, first, last = apply_step(1, u0, gl, gr, u0, *args)
    gl, gr = ghosts(first, last)
    u2, first, last = apply_step(2, u1, gl, gr, u0, *args)
    gl, gr = ghosts(first, last)
    qs = apply_step(3, u2, gl, gr, u1, *args)
    qs = [qs[0]] + [shift(qs[k], "band", k, True) for k in (1, 2, 3)]
    gram, rows = gram_of(qs, me)
    gram = summed(gram)
    outs = basis_of(gram, rows, me, LOC * lax.axis_size("dom"))
    outs = [outs[0]] + [shift(outs[k], "band", k, True) for k in (1, 2, 3)]
    return join(outs, me)


def solution(mesh):
    return jax.shard_map(
        body,
        mesh=mesh,
        in_specs=(
            P("band", "dom"),
            P(),
            P("dom"),
            P(None, "dom"),
            P(None, "dom"),
            P("dom"),
            P("dom"),
            P(None, "dom"),
            P(None, "dom"),
        ),
        out_specs=P("band", "dom"),
        check_vma=False,
    )
```

```python
import functools
import jax
import jax.numpy as jnp
from jax import lax
from jax.experimental import pallas as pl
from jax.experimental.pallas import tpu as pltpu
from jax.sharding import PartitionSpec as P

RIM = 2048
NODES = 343
HANG = 864
MASTERS = 4
LOC = 13824
CELLS = 64
S = 16
L = 128
EXT = LOC + 2 * RIM
NB = LOC // L
RB = RIM // L
NPAD = 384
NJ = NPAD // L
WIDE = 7
NARROW = 3
PACK = 352
GROUP = 16
SLOTS = 14 * GROUP
HPAD = 896
HB = HPAD // L
ME = MASTERS * HPAD
HE = 1024
E = ME + HE
QLO = 512
QB = QLO // L
QHI = 9
BIG = 1 << 20
CENTRE = 4.5
HALF = 3.5
F32 = jnp.float32
BF16 = jnp.bfloat16
I32 = jnp.int32
VLIM = 40 * 1024 * 1024

VM = pl.BlockSpec(memory_space=pltpu.VMEM)
SM = pl.BlockSpec(memory_space=pltpu.SMEM)
NT = (((1,), (1,)), ((), ()))


def iota(shape, dim):
    return lax.broadcasted_iota(I32, shape, dim)


def lanes(x, idx):
    return jnp.take_along_axis(x, idx, axis=1, mode="promise_in_bounds")


def nn(a, b):
    return jnp.dot(a, b, preferred_element_type=F32)


def nt(a, b):
    return lax.dot_general(a, b, NT, preferred_element_type=F32)


def split(x):
    hi = x.astype(BF16)
    return hi, (x - hi.astype(F32)).astype(BF16)


def at(b):
    return pl.ds(pl.multiple_of(b * L, L), L)


def one_hot(row, n):
    return (jnp.broadcast_to(row, (n, row.shape[1])) == iota((n, row.shape[1]), 0)).astype(F32)


def hang_tables(ent_ref, a_ref, b_ref, lhs_ref, oh_ref, pe_ref, src_ref, posr_ref, hq_ref, start_ref):
    for i in range(E // L):
        col = slice(i * L, (i + 1) * L)
        row = ent_ref[0:1, col]
        a_ref[:, col] = one_hot(row >> 7, L).astype(BF16)
        b_ref[:, col] = one_hot(row & 127, L).astype(BF16)
    flag = nt(a_ref[...], b_ref[...]) > 0.5
    flagb = flag.astype(F32).astype(BF16)
    tri = (iota((L, L), 0) < iota((L, L), 1)).astype(F32).astype(BF16)
    low = (iota((L, L), 1) < iota((L, L), 0)).astype(F32).astype(BF16)
    total = nn(flagb, jnp.ones((L, L), BF16))
    pos = (nn(flagb, tri) + nn(low, total.astype(BF16))).astype(I32)
    posr_ref[...] = jnp.where(flag, pos, -1)
    totrow = nt(jnp.ones((8, L), BF16), flagb)
    start_ref[...] = nn(totrow.astype(BF16), tri).astype(I32)
    ph = (pos >> 7).astype(F32).astype(BF16)
    plo = (pos & 127).astype(F32).astype(BF16)
    for i in range(E // L):
        col = slice(i * L, (i + 1) * L)
        ent = ent_ref[0:1, col]
        mask = a_ref[:, col].astype(F32)
        b = b_ref[:, col]
        hi = jnp.sum(nn(ph, b) * mask, axis=0, keepdims=True)
        lo = jnp.sum(nn(plo, b) * mask, axis=0, keepdims=True)
        pe = jnp.where(ent >= 0, hi.astype(I32) * L + lo.astype(I32), BIG)
        pe_ref[0:1, col] = pe
        oh_ref[:, col] = one_hot(pe & (QLO - 1), QLO).astype(BF16)
        qm = one_hot(pe // QLO, 16)
        lhs_ref[0:16, col] = qm.astype(BF16)
        lhs_ref[16:32, col] = (qm * (ent >> 7).astype(F32)).astype(BF16)
        lhs_ref[32:48, col] = (qm * (ent & 127).astype(F32)).astype(BF16)
        lhs_ref[48:64, col] = (qm if i >= ME // L else jnp.zeros_like(qm)).astype(BF16)
    res = nt(lhs_ref[...], oh_ref[...])
    cnt = res[0:16]
    den = jnp.maximum(cnt, 1.0)
    blk = (res[16:32] / den + 0.5).astype(I32)
    lo = (res[32:48] / den + 0.5).astype(I32)
    src = jnp.where(cnt > 0.5, blk * L + lo, -1)
    for q in range(QHI):
        for t in range(QB):
            src_ref[QB * q + t : QB * q + t + 1, :] = src[q : q + 1, t * L : (t + 1) * L]
    hq_ref[...] = res[48:64]


def zat(c):
    return pl.ds(pl.multiple_of((c // QB) * S, S), S), pl.ds(pl.multiple_of((c % QB) * L, L), L)


UNROLL = 12


def compress(read, z_ref, src_ref, start_ref):
    z_ref[...] = jnp.zeros_like(z_ref)

    def step(i, cur):
        for k in range(UNROLL):
            b = i * UNROLL + k
            y = read(b)
            c = start_ref[0, b] >> 7
            ahead = start_ref[0, b + 1] >> 7
            parts = []
            for t in range(2):
                row = jnp.broadcast_to(src_ref[pl.ds(c + t, 1), :], (S, L))
                parts.append(((row >> 7) == b, lanes(y, row & 127)))
            cur = jnp.where(parts[0][0], parts[0][1], cur)
            r, l = zat(c)
            z_ref[r, l] = cur
            after = jnp.where(parts[1][0], parts[1][1], 0.0)
            cur = jnp.where(ahead > c, after, cur)
        return cur

    cur = lax.fori_loop(0, NB // UNROLL, step, jnp.zeros((S, L), F32))
    r, l = zat(start_ref[0, NB] >> 7)
    z_ref[r, l] = cur


def expand(b, y, z_ref, posr_ref, start_ref):
    row = jnp.broadcast_to(posr_ref[pl.ds(b, 1), :], (S, L))
    c0 = start_ref[0, b] >> 7
    for t in range(2):
        c = c0 + t
        r, l = zat(c)
        y = jnp.where((row >> 7) == c, lanes(z_ref[r, l], row & 127), y)
    return y


def gather_entries(z_ref, oh_ref, pe_ref, g_ref, first, last):
    zz = jnp.concatenate(split(z_ref[...]), axis=0)
    n = QHI * S
    w = 256
    for i in range(first // w, last // w):
        col = slice(i * w, (i + 1) * w)
        g = nn(zz, oh_ref[:, col])
        q = jnp.broadcast_to(pe_ref[0:1, col] // QLO, (S, w))
        hi = g[0:S]
        lo = g[n : n + S]
        for h in range(1, QHI):
            m = q == h
            hi = jnp.where(m, g[h * S : (h + 1) * S], hi)
            lo = jnp.where(m, g[n + h * S : n + (h + 1) * S], lo)
        g_ref[:, col] = hi + lo


def scatter_entries(g_ref, oh_ref, pe_ref, lhs_ref, first, last):
    n = QHI * S
    for i in range(first // L, last // L):
        col = slice(i * L, (i + 1) * L)
        g = g_ref[:, col]
        hi = g.astype(BF16).astype(F32)
        lo = g - hi
        q = jnp.broadcast_to(pe_ref[0:1, col] // QLO, (S, L))
        for h in range(QHI):
            m = q == h
            lhs_ref[h * S : (h + 1) * S, col] = jnp.where(m, hi, 0.0).astype(BF16)
            lhs_ref[n + h * S : n + (h + 1) * S, col] = jnp.where(m, lo, 0.0).astype(BF16)
    res = nt(lhs_ref[:, first:last], oh_ref[:, first:last])
    return res[:n] + res[n:]


def hanging_values(z_ref, oh_ref, pe_ref, w_ref, g_ref, lhs_ref, hq_ref):
    gather_entries(z_ref, oh_ref, pe_ref, g_ref, 0, ME)
    g_ref[:, ME + HPAD :] = jnp.zeros((S, HE - HPAD), F32)
    for j in range(HB):
        acc = jnp.zeros((S, L), F32)
        for k in range(MASTERS):
            col = slice(k * HPAD + j * L, k * HPAD + (j + 1) * L)
            acc = acc + g_ref[:, col] * w_ref[0:1, col]
        g_ref[:, ME + j * L : ME + (j + 1) * L] = acc
    cz = scatter_entries(g_ref, oh_ref, pe_ref, lhs_ref, ME, E)
    for h in range(QHI):
        r = slice(h * S, (h + 1) * S)
        m = jnp.broadcast_to(hq_ref[h : h + 1, :], (S, QLO)) > 0.5
        z_ref[r, :] = jnp.where(m, cz[r], z_ref[r, :])


def add_to_masters(z_ref, oh_ref, pe_ref, w_ref, g_ref, lhs_ref):
    gather_entries(z_ref, oh_ref, pe_ref, g_ref, ME, E)
    for j in range(HB):
        y = g_ref[:, ME + j * L : ME + (j + 1) * L]
        for k in range(MASTERS):
            col = slice(k * HPAD + j * L, k * HPAD + (j + 1) * L)
            g_ref[:, col] = y * w_ref[0:1, col]
    z_ref[...] += scatter_entries(g_ref, oh_ref, pe_ref, lhs_ref, 0, ME)


def prepare_kernel(
    rows_ref, masters_ref, weights_ref, block_ref,
    oh_ref, pe_ref, w_ref, src_ref, posr_ref, hq_ref, start_ref, u_ref, left_ref, right_ref,
    ent_ref, a_ref, b_ref, tab_ref, z_ref, g_ref, lhs_ref, start_s, sem,
):
    ent_ref[...] = jnp.full((1, E), -1, I32)
    w_ref[...] = jnp.zeros((1, ME), F32)
    for k in range(MASTERS):
        col = slice(k * HPAD, k * HPAD + HANG)
        ent_ref[0:1, col] = masters_ref[k : k + 1, :]
        w_ref[0:1, col] = weights_ref[k : k + 1, :]
    ent_ref[0:1, ME : ME + HANG] = rows_ref[...]
    hang_tables(ent_ref, a_ref, b_ref, tab_ref, oh_ref, pe_ref, src_ref, posr_ref, hq_ref, start_ref)
    copy = pltpu.make_async_copy(start_ref, start_s, sem)
    copy.start()
    copy.wait()
    compress(lambda b: block_ref[:, at(b)], z_ref, src_ref, start_s)
    hanging_values(z_ref, oh_ref, pe_ref, w_ref, g_ref, lhs_ref, hq_ref)

    def step(i, _):
        for k in range(UNROLL):
            b = i * UNROLL + k
            u_ref[:, at(b)] = expand(b, block_ref[:, at(b)], z_ref, posr_ref, start_s)
        return 0

    lax.fori_loop(0, NB // UNROLL, step, 0)
    left_ref[...] = u_ref[:, 0:RIM]
    right_ref[...] = u_ref[:, LOC - RIM :]


def sds(shape, dtype=F32):
    return jax.ShapeDtypeStruct(shape, dtype)


HANG_SCRATCH = [
    pltpu.VMEM((QHI * S, QLO), F32),
    pltpu.VMEM((S, E), F32),
    pltpu.VMEM((2 * QHI * S, E), BF16),
]


def prepare(rows, masters, weights, block):
    return pl.pallas_call(
        prepare_kernel,
        out_shape=(
            sds((QLO, E), BF16),
            sds((1, E), I32),
            sds((1, ME)),
            sds((QB * QHI + 4, L), I32),
            sds((L, L), I32),
            sds((16, QLO)),
            sds((8, L), I32),
            sds((S, LOC)),
            sds((S, RIM)),
            sds((S, RIM)),
        ),
        in_specs=[VM] * 4,
        out_specs=(VM,) * 10,
        scratch_shapes=[
            pltpu.VMEM((1, E), I32),
            pltpu.VMEM((L, E), BF16),
            pltpu.VMEM((L, E), BF16),
            pltpu.VMEM((64, E), BF16),
            *HANG_SCRATCH,
            pltpu.SMEM((8, L), I32),
            pltpu.SemaphoreType.DMA,
        ],
        compiler_params=pltpu.CompilerParams(vmem_limit_bytes=VLIM),
        name="prepare",
    )(rows, masters, weights, block)


def cells_kernel(
    own_ref, left_ref, right_ref, k_ref,
    tab_ref, pot_ref, kh_ref, kl_ref, base_ref,
    in_ref, all_ref, meta_ref, pad_ref, meta_s, list_s, wide_s, sem,
):
    in_ref[PACK:, :] = jnp.zeros((NPAD - PACK, L), F32)
    lane = iota((CELLS, L), 1)
    tail = NODES - 2 * L
    for i, (ref, shift) in enumerate(((own_ref, 0), (left_ref, -LOC), (right_ref, LOC))):
        r = slice(i * CELLS, (i + 1) * CELLS)
        in_ref[0:PACK, :] = ref[...]
        lows, tops = [], []
        for j in range(NJ):
            t = in_ref[j * L : (j + 1) * L, :].T
            dofs = t[0:CELLS] + float(shift)
            real = lane < (L if j < 2 else tail)
            low = jnp.where(real, dofs, float(BIG))
            all_ref[r, j * L : (j + 1) * L] = low
            all_ref[r, NPAD + j * L : NPAD + (j + 1) * L] = t[CELLS:]
            lows.append(jnp.min(low, axis=1, keepdims=True).astype(I32))
            tops.append(jnp.max(jnp.where(real, dofs, -float(BIG)), axis=1, keepdims=True).astype(I32))
        all_ref[r, 2 * NPAD :] = jnp.broadcast_to(t[0:CELLS, tail : tail + 1], (CELLS, L))
        live = t[CELLS:, tail : tail + 1] > 0.5
        low = jnp.minimum(jnp.minimum(lows[0], lows[1]), lows[2])
        top = jnp.maximum(jnp.maximum(tops[0], tops[1]), tops[2])
        used = live & (top >= RIM) & (low < RIM + LOC)
        starts = [jnp.minimum(x >> 7, EXT // L - NARROW) for x in lows]
        narrow = ((tops[0] >> 7) - starts[0] < NARROW) & ((tops[1] >> 7) - starts[1] < NARROW)
        narrow = narrow & ((tops[2] >> 7) - starts[2] < NARROW)
        base = jnp.minimum(low >> 7, EXT // L - WIDE)
        meta = jnp.where(used, jnp.where(narrow, 0, 1), -1)
        for j in range(NJ):
            meta = jnp.where(lane == 1 + j, jnp.where(narrow, starts[j], base), meta)
        meta_ref[r, :] = meta
    copy = pltpu.make_async_copy(meta_ref, meta_s, sem)
    copy.start()
    pad_ref[...] = jnp.zeros_like(pad_ref)
    pad_ref[0:NODES, 0:NODES] = k_ref[...]
    kh_ref[...], kl_ref[...] = split(pad_ref[...])
    copy.wait()

    def scan(c, counts):
        kind = meta_s[c, 0]
        n, m = counts
        list_s[n] = c
        wide_s[m] = c
        return n + jnp.where(kind == 0, 1, 0), m + jnp.where(kind == 1, 1, 0)

    n, m = lax.fori_loop(0, 3 * CELLS, scan, (0, 0), unroll=4)
    gn = (n + GROUP - 1) // GROUP
    gw = (m + GROUP - 1) // GROUP
    first = (gn + 1) * GROUP
    last = first + gw * GROUP

    def blank(i, _):
        list_s[i] = -1
        return 0

    def move(i, _):
        list_s[first + i] = wide_s[i]
        return 0

    lax.fori_loop(n, first, blank, 0)
    lax.fori_loop(0, m, move, 0)
    lax.fori_loop(first + m, last, blank, 0)
    base_ref[4 * SLOTS] = gn
    base_ref[4 * SLOTS + 1] = gw

    def one(slot):
        c = list_s[slot]
        valid = c >= 0
        c = jnp.maximum(c, 0)
        vals = all_ref[pl.ds(c, 1), :]
        for j in range(NJ):
            b = jnp.where(valid, meta_s[c, 1 + j], 0)
            base_ref[4 * slot + j] = b
            rel = vals[:, j * L : (j + 1) * L].astype(I32) - b * L
            rel = jnp.where(valid & (rel < WIDE * L), rel, BIG)
            oh = one_hot(rel & 127, L).astype(BF16)
            m = jnp.broadcast_to(rel >> 7, (8, L)) == iota((8, L), 0)
            node = jnp.where(m, iota((8, L), 1) + 1, 0).astype(F32).astype(BF16)
            tab_ref[slot, 8 + 8 * j : 16 + 8 * j, :] = nt(node, oh).astype(I32) - 1
            tab_ref[slot, j : j + 1, :] = rel
            pot_ref[slot, j : j + 1, :] = vals[:, NPAD + j * L : NPAD + (j + 1) * L]
        pot_ref[slot, 3:4, :] = vals[:, 2 * NPAD :]

    def some(i, _):
        for k in range(8):
            one(i * 8 + k)
        return 0

    lax.fori_loop(0, last // 8, some, 0)


def cell_tables(own, left, right, stiffness):
    return pl.pallas_call(
        cells_kernel,
        out_shape=(
            sds((SLOTS, 32, L), I32),
            sds((SLOTS, 8, L)),
            sds((NPAD, NPAD), BF16),
            sds((NPAD, NPAD), BF16),
            sds((4 * SLOTS + L,), I32),
        ),
        in_specs=[VM] * 4,
        out_specs=(VM, VM, VM, VM, SM),
        scratch_shapes=[
            pltpu.VMEM((NPAD, L), F32),
            pltpu.VMEM((3 * CELLS, 7 * L), F32),
            pltpu.VMEM((3 * CELLS, L), I32),
            pltpu.VMEM((NPAD, NPAD), F32),
            pltpu.SMEM((3 * CELLS, L), I32),
            pltpu.SMEM((SLOTS + GROUP,), I32),
            pltpu.SMEM((3 * CELLS + GROUP,), I32),
            pltpu.SemaphoreType.DMA,
        ],
        compiler_params=pltpu.CompilerParams(vmem_limit_bytes=VLIM),
        name="cell_tables",
    )(own, left, right, stiffness)


def step_kernel(number, *refs):
    (u_ref, gl_ref, gr_ref, prev_ref, tab_ref, pot_ref, kh_ref, kl_ref,
     oh_ref, pe_ref, w_ref, src_ref, posr_ref, hq_ref, base_ref, start_ref, me_ref) = refs[:17]
    outs = refs[17 : 17 + (4 if number == 3 else 3)]
    ext_ref, acc0_ref, acc1_ref, x_ref, p_ref, z_ref, g_ref, lhs_ref = refs[17 + len(outs) :]
    accs = (acc0_ref, acc1_ref)
    ext_ref[:, 0:RIM] = gl_ref[...]
    ext_ref[:, RIM : RIM + LOC] = u_ref[...]
    ext_ref[:, RIM + LOC :] = gr_ref[...]
    for ref in accs:
        ref[...] = jnp.zeros_like(ref)
    gn = base_ref[4 * SLOTS]
    gw = base_ref[4 * SLOTS + 1]

    def load(slot, width):
        for j in range(NJ):
            b = base_ref[4 * slot + j]
            row = jnp.broadcast_to(tab_ref[slot, j : j + 1, :], (8, L))
            lo, hi = row & 127, row >> 7
            for s in range(2):
                r = slice(8 * s, 8 * s + 8)
                acc = lanes(ext_ref[r, at(b)], lo)
                for t in range(1, width):
                    acc = jnp.where(hi == t, lanes(ext_ref[r, at(b + t)], lo), acc)
                x_ref[pl.ds(pl.multiple_of(slot * S + 8 * s, 8), 8), j * L : (j + 1) * L] = acc

    def store(slot, parity, width):
        acc_ref = accs[parity]
        scale = jnp.broadcast_to(pot_ref[slot, 3:4, :], (8, L))
        for j in range(NJ):
            b = base_ref[4 * slot + j]
            col = slice(j * L, (j + 1) * L)
            pot = jnp.broadcast_to(pot_ref[slot, j : j + 1, :], (8, L))
            vals = []
            for s in range(2):
                r = pl.ds(pl.multiple_of(slot * S + 8 * s, 8), 8)
                vals.append(scale * p_ref[r, col] + pot * x_ref[r, col])
            adds = []
            for t in range(width):
                row = jnp.broadcast_to(tab_ref[slot, 8 + 8 * j + t : 9 + 8 * j + t, :], (8, L))
                m, lo = row >= 0, row & 127
                adds.append([jnp.where(m, lanes(vals[s], lo), 0.0) for s in range(2)])
            olds = [[acc_ref[8 * s : 8 * s + 8, at(b + t)] for s in range(2)] for t in range(width)]
            for t in range(width):
                for s in range(2):
                    acc_ref[8 * s : 8 * s + 8, at(b + t)] = olds[t][s] + adds[t][s]

    def rows_of(i):
        return pl.ds(pl.multiple_of(i * (GROUP * S), GROUP * S), GROUP * S)

    def product(i):
        xh, xl = split(x_ref[rows_of(i), :])
        kh, kl = kh_ref[...], kl_ref[...]
        return nt(xh, kh) + (nt(xl, kh) + nt(xh, kl))

    def load_group(i, width):
        def four(q, _):
            for k in range(4):
                load(i * GROUP + q * 4 + k, width)
            return 0

        lax.fori_loop(0, GROUP // 4, four, 0)

    def store_group(i, width):
        def four(q, _):
            for k in range(4):
                store(i * GROUP + q * 4 + k, k % 2, width)
            return 0

        lax.fori_loop(0, GROUP // 4, four, 0)

    load_group(0, NARROW)

    def pipeline(i, _):
        prod = product(i)
        before = jnp.where(i == 0, gn, i - 1)
        for k in range(GROUP):
            store(before * GROUP + k, k % 2, NARROW)
        p_ref[rows_of(i), :] = prod
        for k in range(GROUP):
            load((i + 1) * GROUP + k, NARROW)
        return 0

    lax.fori_loop(0, gn, pipeline, 0)
    store_group(jnp.maximum(gn - 1, 0), NARROW)

    def wide(i, _):
        load_group(i, WIDE)
        p_ref[rows_of(i), :] = product(i)
        store_group(i, WIDE)
        return 0

    lax.fori_loop(gn + 1, gn + 1 + gw, wide, 0)

    def read(b):
        return acc0_ref[:, at(b + RB)] + acc1_ref[:, at(b + RB)]

    compress(read, z_ref, src_ref, start_ref)
    add_to_masters(z_ref, oh_ref, pe_ref, w_ref, g_ref, lhs_ref)
    hanging_values(z_ref, oh_ref, pe_ref, w_ref, g_ref, lhs_ref, hq_ref)
    new_ref = outs[0] if number < 3 else ext_ref

    def finish(i, _):
        for k in range(UNROLL):
            b = i * UNROLL + k
            t = expand(b, read(b), z_ref, posr_ref, start_ref)
            r = (t - CENTRE * u_ref[:, at(b)]) * ((1.0 if number == 1 else 2.0) / HALF)
            if number > 1:
                r = r - prev_ref[:, at(b)]
            new_ref[:, at(b)] = r
        return 0

    lax.fori_loop(0, NB // UNROLL, finish, 0)
    if number < 3:
        outs[1][...] = new_ref[:, 0:RIM]
        outs[2][...] = new_ref[:, LOC - RIM :]
    else:
        me = me_ref[0]
        q = LOC // 4
        for k in range(4):
            outs[k][...] = new_ref[:, pl.ds(pl.multiple_of(((me + k) & 3) * q, L), q)]


def apply_step(number, u, gl, gr, prev, cell, base, hang, start, me):
    if number == 3:
        shapes = (sds((S, LOC // 4)),) * 4
    else:
        shapes = (sds((S, LOC)), sds((S, RIM)), sds((S, RIM)))
    return pl.pallas_call(
        functools.partial(step_kernel, number),
        out_shape=shapes,
        in_specs=[VM] * 14 + [SM] * 3,
        out_specs=(VM,) * len(shapes),
        scratch_shapes=[
            pltpu.VMEM((S, EXT), F32),
            pltpu.VMEM((S, EXT), F32),
            pltpu.VMEM((S, EXT), F32),
            pltpu.VMEM((SLOTS * S, NPAD), F32),
            pltpu.VMEM((SLOTS * S, NPAD), F32),
            *HANG_SCRATCH,
        ],
        compiler_params=pltpu.CompilerParams(vmem_limit_bytes=VLIM),
        name=f"step{number}",
    )(u, gl, gr, prev, *cell, *hang, base, start, me)


def gram_kernel(q0_ref, q1_ref, q2_ref, q3_ref, me_ref, gram_ref, all_ref):
    me = me_ref[0]
    for k, ref in enumerate((q0_ref, q1_ref, q2_ref, q3_ref)):
        all_ref[pl.ds(pl.multiple_of(((me - k) & 3) * S, S), S), :] = ref[...]
    a = all_ref[...]
    gram_ref[...] = lax.dot_general(a, a, NT, preferred_element_type=F32, precision=lax.Precision.HIGHEST)


def gram_of(qs, me):
    n = qs[0].shape[1]
    return pl.pallas_call(
        gram_kernel,
        out_shape=(sds((4 * S, 4 * S)), sds((4 * S, n))),
        in_specs=[VM] * 4 + [SM],
        out_specs=(VM, VM),
        compiler_params=pltpu.CompilerParams(vmem_limit_bytes=VLIM),
        name="gram",
    )(*qs, me)


def basis_kernel(total, gram_ref, all_ref, me_ref, o0_ref, o1_ref, o2_ref, o3_ref, m_ref, r_ref):
    n = 4 * S
    eye = (iota((n, n), 0) == iota((n, n), 1)).astype(F32)
    m_ref[...] = jnp.concatenate([gram_ref[...], eye], 1)
    row_id = iota((n, 2 * n), 0)

    m = m_ref[...]
    diag = jnp.zeros((n, 1), F32)
    for j in range(n):
        pivot = m[j : j + 1, :]
        d = pivot[:, j : j + 1]
        f = m[:, j : j + 1] / d
        m = m - jnp.where(row_id > j, f, 0.0) * pivot
    dg = jnp.sum(jnp.where(row_id == iota((n, 2 * n), 1), m, 0.0), axis=1, keepdims=True)
    inv = m[:, n:] * lax.rsqrt(dg) * jnp.sqrt(jnp.float32(total))
    r_ref[...] = jnp.dot(inv, all_ref[...], preferred_element_type=F32, precision=lax.Precision.HIGHEST)
    me = me_ref[0]
    for k, ref in enumerate((o0_ref, o1_ref, o2_ref, o3_ref)):
        ref[...] = r_ref[pl.ds(pl.multiple_of(((me + k) & 3) * S, S), S), :]


def basis_of(gram, rows, me, total):
    n = rows.shape[1]
    return pl.pallas_call(
        functools.partial(basis_kernel, total),
        out_shape=(sds((S, n)),) * 4,
        in_specs=[VM, VM, SM],
        out_specs=(VM,) * 4,
        scratch_shapes=[pltpu.VMEM((4 * S, 8 * S), F32), pltpu.VMEM((4 * S, n), F32)],
        compiler_params=pltpu.CompilerParams(vmem_limit_bytes=VLIM),
        name="basis",
    )(gram, rows, me)


def join_kernel(q0_ref, q1_ref, q2_ref, q3_ref, me_ref, out_ref):
    me = me_ref[0]
    n = q0_ref.shape[1]
    for k, ref in enumerate((q0_ref, q1_ref, q2_ref, q3_ref)):
        out_ref[:, pl.ds(pl.multiple_of(((me - k) & 3) * n, L), n)] = ref[...]


def join(qs, me):
    return pl.pallas_call(
        join_kernel,
        out_shape=sds((S, LOC)),
        in_specs=[VM] * 4 + [SM],
        out_specs=VM,
        compiler_params=pltpu.CompilerParams(vmem_limit_bytes=VLIM),
        name="join",
    )(*qs, me)


def shift(x, axis, by, wrap):
    size = lax.axis_size(axis)
    pairs = [(i, (i + by) % size) for i in range(size) if wrap or 0 <= i + by < size]
    return lax.ppermute(x, axis, pairs)


def swap(x, axis, bits):
    size = lax.axis_size(axis)
    return lax.ppermute(x, axis, [(i, i ^ bits) for i in range(size)])


def summed(g):
    g = g + swap(g, "dom", 1)
    for axis, unit in (("dom", 2), ("dom", 8), ("band", 1)):
        others = [swap(g, axis, unit * k) for k in (1, 2, 3)]
        g = (g + others[0]) + (others[1] + others[2])
    return g


def body(
    block,
    stiffness,
    cell_scale,
    potential,
    cell_dofs,
    cell_count,
    hang_rows,
    hang_masters,
    hang_weights,
):
    me = lax.axis_index("band").astype(I32).reshape(1)
    alive = (jnp.arange(CELLS) < cell_count[0]).astype(F32)
    own = jnp.concatenate(
        [
            jnp.concatenate([cell_dofs.astype(F32), potential], axis=1),
            jnp.concatenate([cell_scale, alive])[None],
            jnp.zeros((PACK - NODES - 1, L), F32),
        ],
        axis=0,
    )
    from_left = shift(own, "dom", 1, False)
    from_right = shift(own, "dom", -1, False)
    *hang, start, u0, first, last = prepare(hang_rows[None], hang_masters, hang_weights, block)

    def ghosts(first, last):
        return shift(last, "dom", 1, False), shift(first, "dom", -1, False)

    gl, gr = ghosts(first, last)
    *cell, base = cell_tables(own, from_left, from_right, stiffness)
    args = (cell, base, hang, start, me)
    u1, first, last = apply_step(1, u0, gl, gr, u0, *args)
    gl, gr = ghosts(first, last)
    u2, first, last = apply_step(2, u1, gl, gr, u0, *args)
    gl, gr = ghosts(first, last)
    qs = apply_step(3, u2, gl, gr, u1, *args)
    qs = [qs[0]] + [shift(qs[k], "band", k, True) for k in (1, 2, 3)]
    gram, rows = gram_of(qs, me)
    gram = summed(gram)
    outs = basis_of(gram, rows, me, LOC * lax.axis_size("dom"))
    outs = [outs[0]] + [shift(outs[k], "band", k, True) for k in (1, 2, 3)]
    return join(outs, me)


def solution(mesh):
    return jax.shard_map(
        body,
        mesh=mesh,
        in_specs=(
            P("band", "dom"),
            P(),
            P("dom"),
            P(None, "dom"),
            P(None, "dom"),
            P("dom"),
            P("dom"),
            P(None, "dom"),
            P(None, "dom"),
        ),
        out_specs=P("band", "dom"),
        check_vma=False,
    )
```

```python
import functools
import jax
import jax.numpy as jnp
from jax import lax
from jax.experimental import pallas as pl
from jax.experimental.pallas import tpu as pltpu
from jax.sharding import PartitionSpec as P

RIM = 2048
NODES = 343
HANG = 864
MASTERS = 4
LOC = 13824
CELLS = 64
S = 16
L = 128
EXT = LOC + 2 * RIM
NB = LOC // L
RB = RIM // L
NPAD = 384
NJ = NPAD // L
WIDE = 7
NARROW = 3
PACK = 72
PW = 2 * NPAD + L
GROUP = 16
SLOTS = 14 * GROUP
HPAD = 896
HB = HPAD // L
ME = MASTERS * HPAD
HE = 1024
E = ME + HE
QLO = 512
QB = QLO // L
QHI = 9
BIG = 1 << 20
CENTRE = 4.5
HALF = 3.5
F32 = jnp.float32
BF16 = jnp.bfloat16
I32 = jnp.int32
VLIM = 40 * 1024 * 1024
SMALL = 20 * 1024 * 1024
WHOLE = 64 * 1024 * 1024

VM = pl.BlockSpec(memory_space=pltpu.VMEM)
SM = pl.BlockSpec(memory_space=pltpu.SMEM)
HBM = pl.BlockSpec(memory_space=pltpu.HBM)
NT = (((1,), (1,)), ((), ()))


def iota(shape, dim):
    return lax.broadcasted_iota(I32, shape, dim)


def lanes(x, idx):
    return jnp.take_along_axis(x, idx, axis=1, mode="promise_in_bounds")


def nn(a, b):
    return jnp.dot(a, b, preferred_element_type=F32)


def nt(a, b):
    return lax.dot_general(a, b, NT, preferred_element_type=F32)


def split(x):
    hi = x.astype(BF16)
    return hi, (x - hi.astype(F32)).astype(BF16)


def at(b):
    return pl.ds(pl.multiple_of(b * L, L), L)


def one_hot(row, n):
    return (jnp.broadcast_to(row, (n, row.shape[1])) == iota((n, row.shape[1]), 0)).astype(F32)


def hang_tables(ent_ref, a_ref, b_ref, lhs_ref, oh_ref, pe_ref, src_ref, posr_ref, hq_ref, start_ref):
    for i in range(E // L):
        col = slice(i * L, (i + 1) * L)
        row = ent_ref[0:1, col]
        a_ref[:, col] = one_hot(row >> 7, L).astype(BF16)
        b_ref[:, col] = one_hot(row & 127, L).astype(BF16)
    flag = nt(a_ref[...], b_ref[...]) > 0.5
    flagb = flag.astype(F32).astype(BF16)
    tri = (iota((L, L), 0) < iota((L, L), 1)).astype(F32).astype(BF16)
    low = (iota((L, L), 1) < iota((L, L), 0)).astype(F32).astype(BF16)
    total = nn(flagb, jnp.ones((L, L), BF16))
    pos = (nn(flagb, tri) + nn(low, total.astype(BF16))).astype(I32)
    posr_ref[...] = jnp.where(flag, pos, -1)
    totrow = nt(jnp.ones((8, L), BF16), flagb)
    start_ref[...] = nn(totrow.astype(BF16), tri).astype(I32)
    ph = (pos >> 7).astype(F32).astype(BF16)
    plo = (pos & 127).astype(F32).astype(BF16)
    for i in range(E // L):
        col = slice(i * L, (i + 1) * L)
        ent = ent_ref[0:1, col]
        mask = a_ref[:, col].astype(F32)
        b = b_ref[:, col]
        hi = jnp.sum(nn(ph, b) * mask, axis=0, keepdims=True)
        lo = jnp.sum(nn(plo, b) * mask, axis=0, keepdims=True)
        pe = jnp.where(ent >= 0, hi.astype(I32) * L + lo.astype(I32), BIG)
        pe_ref[0:1, col] = pe
        oh_ref[:, col] = one_hot(pe & (QLO - 1), QLO).astype(BF16)
        qm = one_hot(pe // QLO, 16)
        lhs_ref[0:16, col] = qm.astype(BF16)
        lhs_ref[16:32, col] = (qm * (ent >> 7).astype(F32)).astype(BF16)
        lhs_ref[32:48, col] = (qm * (ent & 127).astype(F32)).astype(BF16)
        lhs_ref[48:64, col] = (qm if i >= ME // L else jnp.zeros_like(qm)).astype(BF16)
    res = nt(lhs_ref[...], oh_ref[...])
    cnt = res[0:16]
    den = jnp.maximum(cnt, 1.0)
    blk = (res[16:32] / den + 0.5).astype(I32)
    lo = (res[32:48] / den + 0.5).astype(I32)
    src = jnp.where(cnt > 0.5, blk * L + lo, -1)
    for q in range(QHI):
        for t in range(QB):
            src_ref[QB * q + t : QB * q + t + 1, :] = src[q : q + 1, t * L : (t + 1) * L]
    hq_ref[...] = res[48:64]


def zat(c):
    return pl.ds(pl.multiple_of((c // QB) * S, S), S), pl.ds(pl.multiple_of((c % QB) * L, L), L)


UNROLL = 12


def compress(read, z_ref, src_ref, start_ref):
    z_ref[...] = jnp.zeros_like(z_ref)

    def step(i, cur):
        for k in range(UNROLL):
            b = i * UNROLL + k
            y = read(b)
            c = start_ref[0, b] >> 7
            ahead = start_ref[0, b + 1] >> 7
            parts = []
            for t in range(2):
                row = jnp.broadcast_to(src_ref[pl.ds(c + t, 1), :], (S, L))
                parts.append(((row >> 7) == b, lanes(y, row & 127)))
            cur = jnp.where(parts[0][0], parts[0][1], cur)
            r, l = zat(c)
            z_ref[r, l] = cur
            after = jnp.where(parts[1][0], parts[1][1], 0.0)
            cur = jnp.where(ahead > c, after, cur)
        return cur

    cur = lax.fori_loop(0, NB // UNROLL, step, jnp.zeros((S, L), F32))
    r, l = zat(start_ref[0, NB] >> 7)
    z_ref[r, l] = cur


def expand(b, y, z_ref, posr_ref, start_ref):
    row = jnp.broadcast_to(posr_ref[pl.ds(b, 1), :], (S, L))
    c0 = start_ref[0, b] >> 7
    for t in range(2):
        c = c0 + t
        r, l = zat(c)
        y = jnp.where((row >> 7) == c, lanes(z_ref[r, l], row & 127), y)
    return y


def gather_entries(z_ref, oh_ref, pe_ref, g_ref, first, last):
    zz = jnp.concatenate(split(z_ref[...]), axis=0)
    n = QHI * S
    w = 256
    for i in range(first // w, last // w):
        col = slice(i * w, (i + 1) * w)
        g = nn(zz, oh_ref[:, col])
        q = jnp.broadcast_to(pe_ref[0:1, col] // QLO, (S, w))
        hi = g[0:S]
        lo = g[n : n + S]
        for h in range(1, QHI):
            m = q == h
            hi = jnp.where(m, g[h * S : (h + 1) * S], hi)
            lo = jnp.where(m, g[n + h * S : n + (h + 1) * S], lo)
        g_ref[:, col] = hi + lo


def scatter_entries(g_ref, oh_ref, pe_ref, lhs_ref, first, last):
    n = QHI * S
    for i in range(first // L, last // L):
        col = slice(i * L, (i + 1) * L)
        g = g_ref[:, col]
        hi = g.astype(BF16).astype(F32)
        lo = g - hi
        q = jnp.broadcast_to(pe_ref[0:1, col] // QLO, (S, L))
        for h in range(QHI):
            m = q == h
            lhs_ref[h * S : (h + 1) * S, col] = jnp.where(m, hi, 0.0).astype(BF16)
            lhs_ref[n + h * S : n + (h + 1) * S, col] = jnp.where(m, lo, 0.0).astype(BF16)
    res = nt(lhs_ref[:, first:last], oh_ref[:, first:last])
    return res[:n] + res[n:]


def hanging_values(z_ref, oh_ref, pe_ref, w_ref, g_ref, lhs_ref, hq_ref):
    gather_entries(z_ref, oh_ref, pe_ref, g_ref, 0, ME)
    g_ref[:, ME + HPAD :] = jnp.zeros((S, HE - HPAD), F32)
    for j in range(HB):
        acc = jnp.zeros((S, L), F32)
        for k in range(MASTERS):
            col = slice(k * HPAD + j * L, k * HPAD + (j + 1) * L)
            acc = acc + g_ref[:, col] * w_ref[0:1, col]
        g_ref[:, ME + j * L : ME + (j + 1) * L] = acc
    cz = scatter_entries(g_ref, oh_ref, pe_ref, lhs_ref, ME, E)
    for h in range(QHI):
        r = slice(h * S, (h + 1) * S)
        m = jnp.broadcast_to(hq_ref[h : h + 1, :], (S, QLO)) > 0.5
        z_ref[r, :] = jnp.where(m, cz[r], z_ref[r, :])


def add_to_masters(z_ref, oh_ref, pe_ref, w_ref, g_ref, lhs_ref):
    gather_entries(z_ref, oh_ref, pe_ref, g_ref, ME, E)
    for j in range(HB):
        y = g_ref[:, ME + j * L : ME + (j + 1) * L]
        for k in range(MASTERS):
            col = slice(k * HPAD + j * L, k * HPAD + (j + 1) * L)
            g_ref[:, col] = y * w_ref[0:1, col]
    z_ref[...] += scatter_entries(g_ref, oh_ref, pe_ref, lhs_ref, 0, ME)


def prepare_kernel(
    rows_hbm, masters_hbm, weights_hbm, block_hbm,
    oh_ref, pe_ref, w_ref, src_ref, posr_ref, hq_ref, start_ref, u_ref, left_ref, right_ref,
    rows_ref, masters_ref, weights_ref, block_ref,
    ent_ref, a_ref, b_ref, tab_ref, z_ref, g_ref, lhs_ref, start_s, sem, sems,
):
    loads = [
        pltpu.make_async_copy(src, dst, sems.at[i])
        for i, (src, dst) in enumerate(
            (
                (rows_hbm, rows_ref),
                (masters_hbm, masters_ref),
                (weights_hbm, weights_ref),
                (block_hbm, block_ref),
            )
        )
    ]
    for load in loads:
        load.start()
    ent_ref[...] = jnp.full((1, E), -1, I32)
    w_ref[...] = jnp.zeros((1, ME), F32)
    for load in loads[:3]:
        load.wait()
    for k in range(MASTERS):
        col = slice(k * HPAD, k * HPAD + HANG)
        ent_ref[0:1, col] = masters_ref[k : k + 1, :]
        w_ref[0:1, col] = weights_ref[k : k + 1, :]
    ent_ref[0:1, ME : ME + HANG] = rows_ref[...]
    hang_tables(ent_ref, a_ref, b_ref, tab_ref, oh_ref, pe_ref, src_ref, posr_ref, hq_ref, start_ref)
    copy = pltpu.make_async_copy(start_ref, start_s, sem)
    copy.start()
    copy.wait()
    loads[3].wait()
    compress(lambda b: block_ref[:, at(b)], z_ref, src_ref, start_s)
    hanging_values(z_ref, oh_ref, pe_ref, w_ref, g_ref, lhs_ref, hq_ref)

    def step(i, _):
        for k in range(UNROLL):
            b = i * UNROLL + k
            u_ref[:, at(b)] = expand(b, block_ref[:, at(b)], z_ref, posr_ref, start_s)
        return 0

    lax.fori_loop(0, NB // UNROLL, step, 0)
    left_ref[...] = u_ref[:, 0:RIM]
    right_ref[...] = u_ref[:, LOC - RIM :]


def sds(shape, dtype=F32):
    return jax.ShapeDtypeStruct(shape, dtype)


HANG_SCRATCH = [
    pltpu.VMEM((QHI * S, QLO), F32),
    pltpu.VMEM((S, E), F32),
    pltpu.VMEM((2 * QHI * S, E), BF16),
]


def prepare(rows, masters, weights, block):
    return pl.pallas_call(
        prepare_kernel,
        out_shape=(
            sds((QLO, E), BF16),
            sds((1, E), I32),
            sds((1, ME)),
            sds((QB * QHI + 4, L), I32),
            sds((L, L), I32),
            sds((16, QLO)),
            sds((8, L), I32),
            sds((S, LOC)),
            sds((S, RIM)),
            sds((S, RIM)),
        ),
        in_specs=[HBM] * 4,
        out_specs=(VM,) * 10,
        scratch_shapes=[
            pltpu.VMEM((1, HANG), I32),
            pltpu.VMEM((MASTERS, HANG), I32),
            pltpu.VMEM((MASTERS, HANG), F32),
            pltpu.VMEM((S, LOC), F32),
            pltpu.VMEM((1, E), I32),
            pltpu.VMEM((L, E), BF16),
            pltpu.VMEM((L, E), BF16),
            pltpu.VMEM((64, E), BF16),
            *HANG_SCRATCH,
            pltpu.SMEM((8, L), I32),
            pltpu.SemaphoreType.DMA,
            pltpu.SemaphoreType.DMA((4,)),
        ],
        compiler_params=pltpu.CompilerParams(vmem_limit_bytes=VLIM),
        name="prepare",
    )(rows, masters, weights, block)


def pack_kernel(dofs_hbm, pot_hbm, scale_hbm, count_ref, own_ref, dofs_ref, pot_ref, scale_ref, sems):
    moves = ((dofs_hbm, dofs_ref), (pot_hbm, pot_ref), (scale_hbm, scale_ref))
    loads = [pltpu.make_async_copy(src, dst, sems.at[i]) for i, (src, dst) in enumerate(moves)]
    for load in loads:
        load.start()
    for load in loads:
        load.wait()
    own_ref[0:CELLS, 0:NODES] = dofs_ref[...].astype(F32)
    own_ref[0:CELLS, NPAD : NPAD + NODES] = pot_ref[...]
    own_ref[CELLS:PACK, 0:CELLS] = jnp.broadcast_to(scale_ref[...], (PACK - CELLS, CELLS))
    own_ref[CELLS:PACK, L : 2 * L] = jnp.full((PACK - CELLS, L), count_ref[0]).astype(F32)


def pack(dofs, pot, scale, count):
    return pl.pallas_call(
        pack_kernel,
        out_shape=sds((PACK, PW)),
        in_specs=[HBM] * 3 + [SM],
        out_specs=VM,
        scratch_shapes=[
            pltpu.VMEM((CELLS, NODES), I32),
            pltpu.VMEM((CELLS, NODES), F32),
            pltpu.VMEM((1, CELLS), F32),
            pltpu.SemaphoreType.DMA((3,)),
        ],
        compiler_params=pltpu.CompilerParams(vmem_limit_bytes=WHOLE),
        name="pack",
    )(dofs, pot, scale, count)


def inverse(rels):
    oh = jnp.concatenate([one_hot(rel & 127, L) for rel in rels], axis=1).astype(BF16)
    rows = []
    for j, rel in enumerate(rels):
        m = jnp.broadcast_to(rel >> 7, (8, L)) == iota((8, L), 0)
        node = jnp.where(m, iota((8, L), 1) + 1, 0).astype(F32)
        zero = jnp.zeros((8, L), F32)
        rows.append(jnp.concatenate([node if i == j else zero for i in range(len(rels))], axis=1))
    return nt(jnp.concatenate(rows, axis=0).astype(BF16), oh).astype(I32) - 1


def cells_kernel(
    own_ref, left_ref, right_ref, dom_ref, k_hbm,
    tab_ref, pot_ref, kh_ref, kl_ref, base_ref,
    all_ref, meta_ref, k_ref, pad_ref, meta_s, list_s, wide_s, sem, sem_k,
):
    load = pltpu.make_async_copy(k_hbm, k_ref, sem_k)
    load.start()
    lane = iota((CELLS, L), 1)
    cell = iota((CELLS, L), 0)
    tail = NODES - 2 * L
    sources = ((own_ref, 0, None), (left_ref, -LOC, 0), (right_ref, LOC, 1))
    for i, (ref, shift, side) in enumerate(sources):
        r = slice(i * CELLS, (i + 1) * CELLS)
        lows, tops = [], []
        for j in range(NJ):
            dofs = ref[0:CELLS, j * L : (j + 1) * L] + float(shift)
            real = lane < (L if j < 2 else tail)
            low = jnp.where(real, dofs, float(BIG))
            all_ref[r, j * L : (j + 1) * L] = low
            pot = ref[0:CELLS, NPAD + j * L : NPAD + (j + 1) * L]
            all_ref[r, NPAD + j * L : NPAD + (j + 1) * L] = jnp.where(real, pot, 0.0)
            lows.append(jnp.min(low, axis=1, keepdims=True).astype(I32))
            tops.append(jnp.max(jnp.where(real, dofs, -float(BIG)), axis=1, keepdims=True).astype(I32))
        scales = jnp.broadcast_to(ref[CELLS : CELLS + 1, 0:L], (CELLS, L))
        scale = jnp.sum(jnp.where(lane == cell, scales, 0.0), axis=1, keepdims=True)
        all_ref[r, 2 * NPAD :] = jnp.broadcast_to(scale, (CELLS, L))
        count = jnp.broadcast_to(ref[CELLS : CELLS + 1, L : 2 * L], (CELLS, L))
        live = cell.astype(F32) < count
        if side is not None:
            live = live & jnp.full((CELLS, L), dom_ref[1 + side] > 0)
        low = jnp.minimum(jnp.minimum(lows[0], lows[1]), lows[2])
        top = jnp.maximum(jnp.maximum(tops[0], tops[1]), tops[2])
        used = live & (top >= RIM) & (low < RIM + LOC)
        starts = [jnp.minimum(x >> 7, EXT // L - NARROW) for x in lows]
        narrow = ((tops[0] >> 7) - starts[0] < NARROW) & ((tops[1] >> 7) - starts[1] < NARROW)
        narrow = narrow & ((tops[2] >> 7) - starts[2] < NARROW)
        base = jnp.minimum(low >> 7, EXT // L - WIDE)
        meta = jnp.where(used, jnp.where(narrow, 0, 1), -1)
        for j in range(NJ):
            meta = jnp.where(lane == 1 + j, jnp.where(narrow, starts[j], base), meta)
        meta_ref[r, :] = meta
    copy = pltpu.make_async_copy(meta_ref, meta_s, sem)
    copy.start()
    pad_ref[...] = jnp.zeros_like(pad_ref)
    load.wait()
    pad_ref[0:NODES, 0:NODES] = k_ref[...]
    kh_ref[...], kl_ref[...] = split(pad_ref[...])
    copy.wait()

    def scan(c, counts):
        kind = meta_s[c, 0]
        n, m = counts
        list_s[n] = c
        wide_s[m] = c
        return n + jnp.where(kind == 0, 1, 0), m + jnp.where(kind == 1, 1, 0)

    n, m = lax.fori_loop(0, 3 * CELLS, scan, (0, 0), unroll=4)
    gn = (n + GROUP - 1) // GROUP
    gw = (m + GROUP - 1) // GROUP
    first = (gn + 1) * GROUP
    last = first + gw * GROUP

    def blank(i, _):
        list_s[i] = -1
        return 0

    def move(i, _):
        list_s[first + i] = wide_s[i]
        return 0

    lax.fori_loop(n, first, blank, 0)
    lax.fori_loop(0, m, move, 0)
    lax.fori_loop(first + m, last, blank, 0)
    base_ref[4 * SLOTS] = gn
    base_ref[4 * SLOTS + 1] = gw

    def one(slot):
        c = list_s[slot]
        valid = c >= 0
        c = jnp.maximum(c, 0)
        vals = all_ref[pl.ds(c, 1), :]
        rels = []
        for j in range(NJ):
            b = jnp.where(valid, meta_s[c, 1 + j], 0)
            base_ref[4 * slot + j] = b
            rel = vals[:, j * L : (j + 1) * L].astype(I32) - b * L
            rel = jnp.where(valid & (rel < WIDE * L), rel, BIG)
            rels.append(rel)
            tab_ref[slot, j : j + 1, :] = rel
            pot_ref[slot, j : j + 1, :] = vals[:, NPAD + j * L : NPAD + (j + 1) * L]
        pot_ref[slot, 3:4, :] = vals[:, 2 * NPAD :]
        inv = inverse(rels)
        for j in range(NJ):
            tab_ref[slot, 3 + 3 * j : 6 + 3 * j, :] = inv[8 * j : 8 * j + NARROW]

    def some(i, _):
        for k in range(8):
            one(i * 8 + k)
        return 0

    lax.fori_loop(0, last // 8, some, 0)


def cell_tables(own, left, right, dom, stiffness):
    return pl.pallas_call(
        cells_kernel,
        out_shape=(
            sds((SLOTS, 16, L), I32),
            sds((SLOTS, 8, L)),
            sds((NPAD, NPAD), BF16),
            sds((NPAD, NPAD), BF16),
            sds((4 * SLOTS + L,), I32),
        ),
        in_specs=[VM] * 3 + [SM, HBM],
        out_specs=(VM, VM, VM, VM, SM),
        scratch_shapes=[
            pltpu.VMEM((3 * CELLS, PW), F32),
            pltpu.VMEM((3 * CELLS, L), I32),
            pltpu.VMEM((NODES, NODES), F32),
            pltpu.VMEM((NPAD, NPAD), F32),
            pltpu.SMEM((3 * CELLS, L), I32),
            pltpu.SMEM((SLOTS + GROUP,), I32),
            pltpu.SMEM((3 * CELLS + GROUP,), I32),
            pltpu.SemaphoreType.DMA,
            pltpu.SemaphoreType.DMA,
        ],
        compiler_params=pltpu.CompilerParams(vmem_limit_bytes=SMALL),
        name="cell_tables",
    )(own, left, right, dom, stiffness)


def step_kernel(number, *refs):
    (u_ref, gl_ref, gr_ref, prev_ref, tab_ref, pot_ref, kh_ref, kl_ref,
     oh_ref, pe_ref, w_ref, src_ref, posr_ref, hq_ref, base_ref, start_ref, me_ref) = refs[:17]
    outs = refs[17 : 17 + (4 if number == 3 else 3)]
    ext_ref, acc0_ref, acc1_ref, x_ref, p_ref, z_ref, g_ref, lhs_ref = refs[17 + len(outs) :]
    accs = (acc0_ref, acc1_ref)
    ext_ref[:, 0:RIM] = jnp.where(me_ref[1] > 0, gl_ref[...], 0.0)
    ext_ref[:, RIM : RIM + LOC] = u_ref[...]
    ext_ref[:, RIM + LOC :] = jnp.where(me_ref[2] > 0, gr_ref[...], 0.0)
    for ref in accs:
        ref[...] = jnp.zeros_like(ref)
    gn = base_ref[4 * SLOTS]
    gw = base_ref[4 * SLOTS + 1]

    def load(slot, width):
        for j in range(NJ):
            b = base_ref[4 * slot + j]
            row = jnp.broadcast_to(tab_ref[slot, j : j + 1, :], (8, L))
            lo, hi = row & 127, row >> 7
            for s in range(2):
                r = slice(8 * s, 8 * s + 8)
                acc = lanes(ext_ref[r, at(b)], lo)
                for t in range(1, width):
                    acc = jnp.where(hi == t, lanes(ext_ref[r, at(b + t)], lo), acc)
                x_ref[pl.ds(pl.multiple_of(slot * S + 8 * s, 8), 8), j * L : (j + 1) * L] = acc

    def store(slot, parity, width):
        acc_ref = accs[parity]
        scale = jnp.broadcast_to(pot_ref[slot, 3:4, :], (8, L))
        if width == NARROW:
            inv = [[tab_ref[slot, 3 + 3 * j + t : 4 + 3 * j + t, :] for t in range(width)] for j in range(NJ)]
        else:
            full = inverse([tab_ref[slot, j : j + 1, :] for j in range(NJ)])
            inv = [[full[8 * j + t : 8 * j + t + 1] for t in range(width)] for j in range(NJ)]
        for j in range(NJ):
            b = base_ref[4 * slot + j]
            col = slice(j * L, (j + 1) * L)
            pot = jnp.broadcast_to(pot_ref[slot, j : j + 1, :], (8, L))
            vals = []
            for s in range(2):
                r = pl.ds(pl.multiple_of(slot * S + 8 * s, 8), 8)
                vals.append(scale * p_ref[r, col] + pot * x_ref[r, col])
            adds = []
            for t in range(width):
                row = jnp.broadcast_to(inv[j][t], (8, L))
                m, lo = row >= 0, row & 127
                adds.append([jnp.where(m, lanes(vals[s], lo), 0.0) for s in range(2)])
            olds = [[acc_ref[8 * s : 8 * s + 8, at(b + t)] for s in range(2)] for t in range(width)]
            for t in range(width):
                for s in range(2):
                    acc_ref[8 * s : 8 * s + 8, at(b + t)] = olds[t][s] + adds[t][s]

    def rows_of(i):
        return pl.ds(pl.multiple_of(i * (GROUP * S), GROUP * S), GROUP * S)

    def product(i):
        xh, xl = split(x_ref[rows_of(i), :])
        kh, kl = kh_ref[...], kl_ref[...]
        return nt(xh, kh) + (nt(xl, kh) + nt(xh, kl))

    def load_group(i, width):
        def four(q, _):
            for k in range(4):
                load(i * GROUP + q * 4 + k, width)
            return 0

        lax.fori_loop(0, GROUP // 4, four, 0)

    def store_group(i, width):
        def four(q, _):
            for k in range(4):
                store(i * GROUP + q * 4 + k, k % 2, width)
            return 0

        lax.fori_loop(0, GROUP // 4, four, 0)

    load_group(0, NARROW)

    def pipeline(i, _):
        prod = product(i)
        before = jnp.where(i == 0, gn, i - 1)
        for k in range(GROUP):
            store(before * GROUP + k, k % 2, NARROW)
        p_ref[rows_of(i), :] = prod
        for k in range(GROUP):
            load((i + 1) * GROUP + k, NARROW)
        return 0

    lax.fori_loop(0, gn, pipeline, 0)
    store_group(jnp.maximum(gn - 1, 0), NARROW)

    def wide(i, _):
        load_group(i, WIDE)
        p_ref[rows_of(i), :] = product(i)
        store_group(i, WIDE)
        return 0

    lax.fori_loop(gn + 1, gn + 1 + gw, wide, 0)

    def read(b):
        return acc0_ref[:, at(b + RB)] + acc1_ref[:, at(b + RB)]

    compress(read, z_ref, src_ref, start_ref)
    add_to_masters(z_ref, oh_ref, pe_ref, w_ref, g_ref, lhs_ref)
    hanging_values(z_ref, oh_ref, pe_ref, w_ref, g_ref, lhs_ref, hq_ref)
    new_ref = outs[0] if number < 3 else ext_ref

    def finish(i, _):
        for k in range(UNROLL):
            b = i * UNROLL + k
            t = expand(b, read(b), z_ref, posr_ref, start_ref)
            r = (t - CENTRE * u_ref[:, at(b)]) * ((1.0 if number == 1 else 2.0) / HALF)
            if number > 1:
                r = r - prev_ref[:, at(b)]
            new_ref[:, at(b)] = r
        return 0

    lax.fori_loop(0, NB // UNROLL, finish, 0)
    if number < 3:
        outs[1][...] = new_ref[:, 0:RIM]
        outs[2][...] = new_ref[:, LOC - RIM :]
    else:
        me = me_ref[0]
        q = LOC // 4
        for k in range(4):
            outs[k][...] = new_ref[:, pl.ds(pl.multiple_of(((me + k) & 3) * q, L), q)]


def apply_step(number, u, gl, gr, prev, cell, base, hang, start, me):
    if number == 3:
        shapes = (sds((S, LOC // 4)),) * 4
    else:
        shapes = (sds((S, LOC)), sds((S, RIM)), sds((S, RIM)))
    return pl.pallas_call(
        functools.partial(step_kernel, number),
        out_shape=shapes,
        in_specs=[VM] * 14 + [SM] * 3,
        out_specs=(VM,) * len(shapes),
        scratch_shapes=[
            pltpu.VMEM((S, EXT), F32),
            pltpu.VMEM((S, EXT), F32),
            pltpu.VMEM((S, EXT), F32),
            pltpu.VMEM((SLOTS * S, NPAD), F32),
            pltpu.VMEM((SLOTS * S, NPAD), F32),
            *HANG_SCRATCH,
        ],
        compiler_params=pltpu.CompilerParams(vmem_limit_bytes=VLIM),
        name=f"step{number}",
    )(u, gl, gr, prev, *cell, *hang, base, start, me)


def gram_kernel(q0_ref, q1_ref, q2_ref, q3_ref, me_ref, gram_ref, all_ref):
    me = me_ref[0]
    for k, ref in enumerate((q0_ref, q1_ref, q2_ref, q3_ref)):
        all_ref[pl.ds(pl.multiple_of(((me - k) & 3) * S, S), S), :] = ref[...]
    a = all_ref[...]
    gram_ref[...] = lax.dot_general(a, a, NT, preferred_element_type=F32, precision=lax.Precision.HIGHEST)


def gram_of(qs, me):
    n = qs[0].shape[1]
    return pl.pallas_call(
        gram_kernel,
        out_shape=(sds((4 * S, 4 * S)), sds((4 * S, n))),
        in_specs=[VM] * 4 + [SM],
        out_specs=(VM, VM),
        compiler_params=pltpu.CompilerParams(vmem_limit_bytes=VLIM),
        name="gram",
    )(*qs, me)


def basis_kernel(total, gram_ref, all_ref, me_ref, o0_ref, o1_ref, o2_ref, o3_ref, m_ref, r_ref):
    n = 4 * S
    eye = (iota((n, n), 0) == iota((n, n), 1)).astype(F32)
    m_ref[...] = jnp.concatenate([gram_ref[...], eye], 1)
    row_id = iota((n, 2 * n), 0)

    m = m_ref[...]
    diag = jnp.zeros((n, 1), F32)
    for j in range(n):
        pivot = m[j : j + 1, :]
        d = pivot[:, j : j + 1]
        f = m[:, j : j + 1] / d
        m = m - jnp.where(row_id > j, f, 0.0) * pivot
    dg = jnp.sum(jnp.where(row_id == iota((n, 2 * n), 1), m, 0.0), axis=1, keepdims=True)
    inv = m[:, n:] * lax.rsqrt(dg) * jnp.sqrt(jnp.float32(total))
    r_ref[...] = jnp.dot(inv, all_ref[...], preferred_element_type=F32, precision=lax.Precision.HIGHEST)
    me = me_ref[0]
    for k, ref in enumerate((o0_ref, o1_ref, o2_ref, o3_ref)):
        ref[...] = r_ref[pl.ds(pl.multiple_of(((me + k) & 3) * S, S), S), :]


def basis_of(gram, rows, me, total):
    n = rows.shape[1]
    return pl.pallas_call(
        functools.partial(basis_kernel, total),
        out_shape=(sds((S, n)),) * 4,
        in_specs=[VM, VM, SM],
        out_specs=(VM,) * 4,
        scratch_shapes=[pltpu.VMEM((4 * S, 8 * S), F32), pltpu.VMEM((4 * S, n), F32)],
        compiler_params=pltpu.CompilerParams(vmem_limit_bytes=VLIM),
        name="basis",
    )(gram, rows, me)


def join_kernel(q0_ref, q1_ref, q2_ref, q3_ref, me_ref, out_ref):
    me = me_ref[0]
    n = q0_ref.shape[1]
    for k, ref in enumerate((q0_ref, q1_ref, q2_ref, q3_ref)):
        out_ref[:, pl.ds(pl.multiple_of(((me - k) & 3) * n, L), n)] = ref[...]


def join(qs, me):
    return pl.pallas_call(
        join_kernel,
        out_shape=sds((S, LOC)),
        in_specs=[VM] * 4 + [SM],
        out_specs=VM,
        compiler_params=pltpu.CompilerParams(vmem_limit_bytes=VLIM),
        name="join",
    )(*qs, me)


def shift(x, axis, by):
    size = lax.axis_size(axis)
    return lax.ppermute(x, axis, [(i, (i + by) % size) for i in range(size)])


def swap(x, axis, bits):
    size = lax.axis_size(axis)
    return lax.ppermute(x, axis, [(i, i ^ bits) for i in range(size)])


def summed(g):
    g = g + swap(g, "dom", 1)
    for axis, unit in (("dom", 2), ("dom", 8), ("band", 1)):
        others = [swap(g, axis, unit * k) for k in (1, 2, 3)]
        g = (g + others[0]) + (others[1] + others[2])
    return g


def body(
    block,
    stiffness,
    cell_scale,
    potential,
    cell_dofs,
    cell_count,
    hang_rows,
    hang_masters,
    hang_weights,
):
    dom = lax.axis_index("dom")
    inside = [lax.axis_index("band"), dom > 0, dom < lax.axis_size("dom") - 1]
    me = jnp.stack([jnp.asarray(x).astype(I32) for x in inside])
    own = pack(cell_dofs.T, potential.T, cell_scale[None], cell_count)
    from_left = shift(own, "dom", 1)
    from_right = shift(own, "dom", -1)
    *hang, start, u0, first, last = prepare(hang_rows[None], hang_masters, hang_weights, block)

    def ghosts(first, last):
        return shift(last, "dom", 1), shift(first, "dom", -1)

    gl, gr = ghosts(first, last)
    *cell, base = cell_tables(own, from_left, from_right, me, stiffness)
    args = (cell, base, hang, start, me)
    u1, first, last = apply_step(1, u0, gl, gr, u0, *args)
    gl, gr = ghosts(first, last)
    u2, first, last = apply_step(2, u1, gl, gr, u0, *args)
    gl, gr = ghosts(first, last)
    qs = apply_step(3, u2, gl, gr, u1, *args)
    qs = [qs[0]] + [shift(qs[k], "band", k) for k in (1, 2, 3)]
    gram, rows = gram_of(qs, me)
    gram = summed(gram)
    outs = basis_of(gram, rows, me, LOC * lax.axis_size("dom"))
    outs = [outs[0]] + [shift(outs[k], "band", k) for k in (1, 2, 3)]
    return join(outs, me)


def solution(mesh):
    return jax.shard_map(
        body,
        mesh=mesh,
        in_specs=(
            P("band", "dom"),
            P(),
            P("dom"),
            P(None, "dom"),
            P(None, "dom"),
            P("dom"),
            P("dom"),
            P(None, "dom"),
            P(None, "dom"),
        ),
        out_specs=P("band", "dom"),
        check_vma=False,
    )
```

```python
import functools
import jax
import jax.numpy as jnp
from jax import lax
from jax.experimental import pallas as pl
from jax.experimental.pallas import tpu as pltpu
from jax.sharding import PartitionSpec as P

RIM = 2048
NODES = 343
HANG = 864
MASTERS = 4
LOC = 13824
CELLS = 64
S = 16
L = 128
EXT = LOC + 2 * RIM
NB = LOC // L
RB = RIM // L
NPAD = 384
NJ = NPAD // L
WIDE = 7
NARROW = 3
PACK = 72
PW = 2 * NPAD + L
GROUP = 16
RING = 4 * GROUP
SLOTS = 14 * GROUP
HPAD = 896
HB = HPAD // L
ME = MASTERS * HPAD
HE = 1024
E = ME + HE
QLO = 512
QB = QLO // L
QHI = 9
BIG = 1 << 20
CENTRE = 4.5
HALF = 3.5
F32 = jnp.float32
BF16 = jnp.bfloat16
I32 = jnp.int32
VLIM = 28 * 1024 * 1024
SMALL = 20 * 1024 * 1024
WHOLE = 64 * 1024 * 1024

VM = pl.BlockSpec(memory_space=pltpu.VMEM)
SM = pl.BlockSpec(memory_space=pltpu.SMEM)
HBM = pl.BlockSpec(memory_space=pltpu.HBM)
NT = (((1,), (1,)), ((), ()))


def iota(shape, dim):
    return lax.broadcasted_iota(I32, shape, dim)


def lanes(x, idx):
    return jnp.take_along_axis(x, idx, axis=1, mode="promise_in_bounds")


def nn(a, b):
    return jnp.dot(a, b, preferred_element_type=F32)


def nt(a, b):
    return lax.dot_general(a, b, NT, preferred_element_type=F32)


def split(x):
    hi = x.astype(BF16)
    return hi, (x - hi.astype(F32)).astype(BF16)


def at(b):
    return pl.ds(pl.multiple_of(b * L, L), L)


def one_hot(row, n):
    return (jnp.broadcast_to(row, (n, row.shape[1])) == iota((n, row.shape[1]), 0)).astype(F32)


def hang_tables(ent_ref, a_ref, b_ref, lhs_ref, oh_ref, pe_ref, src_ref, posr_ref, hq_ref, start_ref):
    for i in range(E // L):
        col = slice(i * L, (i + 1) * L)
        row = ent_ref[0:1, col]
        a_ref[:, col] = one_hot(row >> 7, L).astype(BF16)
        b_ref[:, col] = one_hot(row & 127, L).astype(BF16)
    flag = nt(a_ref[...], b_ref[...]) > 0.5
    flagb = flag.astype(F32).astype(BF16)
    tri = (iota((L, L), 0) < iota((L, L), 1)).astype(F32).astype(BF16)
    low = (iota((L, L), 1) < iota((L, L), 0)).astype(F32).astype(BF16)
    total = nn(flagb, jnp.ones((L, L), BF16))
    pos = (nn(flagb, tri) + nn(low, total.astype(BF16))).astype(I32)
    posr_ref[...] = jnp.where(flag, pos, -1)
    totrow = nt(jnp.ones((8, L), BF16), flagb)
    start_ref[...] = nn(totrow.astype(BF16), tri).astype(I32)
    ph = (pos >> 7).astype(F32).astype(BF16)
    plo = (pos & 127).astype(F32).astype(BF16)
    for i in range(E // L):
        col = slice(i * L, (i + 1) * L)
        ent = ent_ref[0:1, col]
        mask = a_ref[:, col].astype(F32)
        b = b_ref[:, col]
        hi = jnp.sum(nn(ph, b) * mask, axis=0, keepdims=True)
        lo = jnp.sum(nn(plo, b) * mask, axis=0, keepdims=True)
        pe = jnp.where(ent >= 0, hi.astype(I32) * L + lo.astype(I32), BIG)
        pe_ref[0:1, col] = pe
        oh_ref[:, col] = one_hot(pe & (QLO - 1), QLO).astype(BF16)
        qm = one_hot(pe // QLO, 16)
        lhs_ref[0:16, col] = qm.astype(BF16)
        lhs_ref[16:32, col] = (qm * (ent >> 7).astype(F32)).astype(BF16)
        lhs_ref[32:48, col] = (qm * (ent & 127).astype(F32)).astype(BF16)
        lhs_ref[48:64, col] = (qm if i >= ME // L else jnp.zeros_like(qm)).astype(BF16)
    res = nt(lhs_ref[...], oh_ref[...])
    cnt = res[0:16]
    den = jnp.maximum(cnt, 1.0)
    blk = (res[16:32] / den + 0.5).astype(I32)
    lo = (res[32:48] / den + 0.5).astype(I32)
    src = jnp.where(cnt > 0.5, blk * L + lo, -1)
    for q in range(QHI):
        for t in range(QB):
            src_ref[QB * q + t : QB * q + t + 1, :] = src[q : q + 1, t * L : (t + 1) * L]
    hq_ref[...] = res[48:64]


def zat(c):
    return pl.ds(pl.multiple_of((c // QB) * S, S), S), pl.ds(pl.multiple_of((c % QB) * L, L), L)


UNROLL = 12


def compress(read, z_ref, src_ref, start_ref):
    z_ref[...] = jnp.zeros_like(z_ref)

    def step(i, cur):
        for k in range(UNROLL):
            b = i * UNROLL + k
            y = read(b)
            c = start_ref[0, b] >> 7
            ahead = start_ref[0, b + 1] >> 7
            parts = []
            for t in range(2):
                row = jnp.broadcast_to(src_ref[pl.ds(c + t, 1), :], (S, L))
                parts.append(((row >> 7) == b, lanes(y, row & 127)))
            cur = jnp.where(parts[0][0], parts[0][1], cur)
            r, l = zat(c)
            z_ref[r, l] = cur
            after = jnp.where(parts[1][0], parts[1][1], 0.0)
            cur = jnp.where(ahead > c, after, cur)
        return cur

    cur = lax.fori_loop(0, NB // UNROLL, step, jnp.zeros((S, L), F32))
    r, l = zat(start_ref[0, NB] >> 7)
    z_ref[r, l] = cur


def expand(b, y, z_ref, posr_ref, start_ref):
    row = jnp.broadcast_to(posr_ref[pl.ds(b, 1), :], (S, L))
    c0 = start_ref[0, b] >> 7
    for t in range(2):
        c = c0 + t
        r, l = zat(c)
        y = jnp.where((row >> 7) == c, lanes(z_ref[r, l], row & 127), y)
    return y


def gather_entries(z_ref, oh_ref, pe_ref, g_ref, first, last):
    zz = jnp.concatenate(split(z_ref[...]), axis=0)
    n = QHI * S
    w = 256
    for i in range(first // w, last // w):
        col = slice(i * w, (i + 1) * w)
        g = nn(zz, oh_ref[:, col])
        q = jnp.broadcast_to(pe_ref[0:1, col] // QLO, (S, w))
        hi = g[0:S]
        lo = g[n : n + S]
        for h in range(1, QHI):
            m = q == h
            hi = jnp.where(m, g[h * S : (h + 1) * S], hi)
            lo = jnp.where(m, g[n + h * S : n + (h + 1) * S], lo)
        g_ref[:, col] = hi + lo


def scatter_entries(g_ref, oh_ref, pe_ref, lhs_ref, first, last):
    n = QHI * S
    for i in range(first // L, last // L):
        col = slice(i * L, (i + 1) * L)
        g = g_ref[:, col]
        hi = g.astype(BF16).astype(F32)
        lo = g - hi
        q = jnp.broadcast_to(pe_ref[0:1, col] // QLO, (S, L))
        for h in range(QHI):
            m = q == h
            lhs_ref[h * S : (h + 1) * S, col] = jnp.where(m, hi, 0.0).astype(BF16)
            lhs_ref[n + h * S : n + (h + 1) * S, col] = jnp.where(m, lo, 0.0).astype(BF16)
    res = nt(lhs_ref[:, first:last], oh_ref[:, first:last])
    return res[:n] + res[n:]


def hanging_values(z_ref, oh_ref, pe_ref, w_ref, g_ref, lhs_ref, hq_ref):
    gather_entries(z_ref, oh_ref, pe_ref, g_ref, 0, ME)
    g_ref[:, ME + HPAD :] = jnp.zeros((S, HE - HPAD), F32)
    for j in range(HB):
        acc = jnp.zeros((S, L), F32)
        for k in range(MASTERS):
            col = slice(k * HPAD + j * L, k * HPAD + (j + 1) * L)
            acc = acc + g_ref[:, col] * w_ref[0:1, col]
        g_ref[:, ME + j * L : ME + (j + 1) * L] = acc
    cz = scatter_entries(g_ref, oh_ref, pe_ref, lhs_ref, ME, E)
    for h in range(QHI):
        r = slice(h * S, (h + 1) * S)
        m = jnp.broadcast_to(hq_ref[h : h + 1, :], (S, QLO)) > 0.5
        z_ref[r, :] = jnp.where(m, cz[r], z_ref[r, :])


def add_to_masters(z_ref, oh_ref, pe_ref, w_ref, g_ref, lhs_ref):
    gather_entries(z_ref, oh_ref, pe_ref, g_ref, ME, E)
    for j in range(HB):
        y = g_ref[:, ME + j * L : ME + (j + 1) * L]
        for k in range(MASTERS):
            col = slice(k * HPAD + j * L, k * HPAD + (j + 1) * L)
            g_ref[:, col] = y * w_ref[0:1, col]
    z_ref[...] += scatter_entries(g_ref, oh_ref, pe_ref, lhs_ref, 0, ME)


def prepare_kernel(
    rows_hbm, masters_hbm, weights_hbm, block_hbm,
    oh_ref, pe_ref, w_ref, src_ref, posr_ref, hq_ref, start_ref, u_ref, left_ref, right_ref,
    rows_ref, masters_ref, weights_ref, block_ref,
    ent_ref, a_ref, b_ref, tab_ref, z_ref, g_ref, lhs_ref, start_s, sem, sems,
):
    loads = [
        pltpu.make_async_copy(src, dst, sems.at[i])
        for i, (src, dst) in enumerate(
            (
                (rows_hbm, rows_ref),
                (masters_hbm, masters_ref),
                (weights_hbm, weights_ref),
                (block_hbm, block_ref),
            )
        )
    ]
    for load in loads:
        load.start()
    ent_ref[...] = jnp.full((1, E), -1, I32)
    w_ref[...] = jnp.zeros((1, ME), F32)
    for load in loads[:3]:
        load.wait()
    for k in range(MASTERS):
        col = slice(k * HPAD, k * HPAD + HANG)
        ent_ref[0:1, col] = masters_ref[k : k + 1, :]
        w_ref[0:1, col] = weights_ref[k : k + 1, :]
    ent_ref[0:1, ME : ME + HANG] = rows_ref[...]
    hang_tables(ent_ref, a_ref, b_ref, tab_ref, oh_ref, pe_ref, src_ref, posr_ref, hq_ref, start_ref)
    copy = pltpu.make_async_copy(start_ref, start_s, sem)
    copy.start()
    copy.wait()
    loads[3].wait()
    compress(lambda b: block_ref[:, at(b)], z_ref, src_ref, start_s)
    hanging_values(z_ref, oh_ref, pe_ref, w_ref, g_ref, lhs_ref, hq_ref)

    def step(i, _):
        for k in range(UNROLL):
            b = i * UNROLL + k
            u_ref[:, at(b)] = expand(b, block_ref[:, at(b)], z_ref, posr_ref, start_s)
        return 0

    lax.fori_loop(0, NB // UNROLL, step, 0)
    left_ref[...] = u_ref[:, 0:RIM]
    right_ref[...] = u_ref[:, LOC - RIM :]


def sds(shape, dtype=F32):
    return jax.ShapeDtypeStruct(shape, dtype)


HANG_SCRATCH = [
    pltpu.VMEM((QHI * S, QLO), F32),
    pltpu.VMEM((S, E), F32),
    pltpu.VMEM((2 * QHI * S, E), BF16),
]


def prepare(rows, masters, weights, block):
    return pl.pallas_call(
        prepare_kernel,
        out_shape=(
            sds((QLO, E), BF16),
            sds((1, E), I32),
            sds((1, ME)),
            sds((QB * QHI + 4, L), I32),
            sds((L, L), I32),
            sds((16, QLO)),
            sds((8, L), I32),
            sds((S, LOC)),
            sds((S, RIM)),
            sds((S, RIM)),
        ),
        in_specs=[HBM] * 4,
        out_specs=(VM,) * 10,
        scratch_shapes=[
            pltpu.VMEM((1, HANG), I32),
            pltpu.VMEM((MASTERS, HANG), I32),
            pltpu.VMEM((MASTERS, HANG), F32),
            pltpu.VMEM((S, LOC), F32),
            pltpu.VMEM((1, E), I32),
            pltpu.VMEM((L, E), BF16),
            pltpu.VMEM((L, E), BF16),
            pltpu.VMEM((64, E), BF16),
            *HANG_SCRATCH,
            pltpu.SMEM((8, L), I32),
            pltpu.SemaphoreType.DMA,
            pltpu.SemaphoreType.DMA((4,)),
        ],
        compiler_params=pltpu.CompilerParams(vmem_limit_bytes=VLIM),
        name="prepare",
    )(rows, masters, weights, block)


def pack_kernel(dofs_hbm, pot_hbm, scale_hbm, count_ref, own_ref, dofs_ref, pot_ref, scale_ref, sems):
    moves = ((dofs_hbm, dofs_ref), (pot_hbm, pot_ref), (scale_hbm, scale_ref))
    loads = [pltpu.make_async_copy(src, dst, sems.at[i]) for i, (src, dst) in enumerate(moves)]
    for load in loads:
        load.start()
    for load in loads:
        load.wait()
    own_ref[0:CELLS, 0:NODES] = dofs_ref[...].astype(F32)
    own_ref[0:CELLS, NPAD : NPAD + NODES] = pot_ref[...]
    own_ref[CELLS:PACK, 0:CELLS] = jnp.broadcast_to(scale_ref[...], (PACK - CELLS, CELLS))
    own_ref[CELLS:PACK, L : 2 * L] = jnp.full((PACK - CELLS, L), count_ref[0]).astype(F32)


def pack(dofs, pot, scale, count):
    return pl.pallas_call(
        pack_kernel,
        out_shape=sds((PACK, PW)),
        in_specs=[HBM] * 3 + [SM],
        out_specs=VM,
        scratch_shapes=[
            pltpu.VMEM((CELLS, NODES), I32),
            pltpu.VMEM((CELLS, NODES), F32),
            pltpu.VMEM((1, CELLS), F32),
            pltpu.SemaphoreType.DMA((3,)),
        ],
        compiler_params=pltpu.CompilerParams(vmem_limit_bytes=WHOLE),
        name="pack",
    )(dofs, pot, scale, count)


def inverse(rels):
    oh = jnp.concatenate([one_hot(rel & 127, L) for rel in rels], axis=1).astype(BF16)
    rows = []
    for j, rel in enumerate(rels):
        m = jnp.broadcast_to(rel >> 7, (8, L)) == iota((8, L), 0)
        node = jnp.where(m, iota((8, L), 1) + 1, 0).astype(F32)
        zero = jnp.zeros((8, L), F32)
        rows.append(jnp.concatenate([node if i == j else zero for i in range(len(rels))], axis=1))
    return nt(jnp.concatenate(rows, axis=0).astype(BF16), oh).astype(I32) - 1


def cells_kernel(
    own_ref, left_ref, right_ref, dom_ref, k_hbm,
    tab_ref, pot_ref, kh_ref, kl_ref, base_ref,
    all_ref, meta_ref, k_ref, pad_ref, meta_s, list_s, wide_s, sem, sem_k,
):
    load = pltpu.make_async_copy(k_hbm, k_ref, sem_k)
    load.start()
    lane = iota((CELLS, L), 1)
    cell = iota((CELLS, L), 0)
    tail = NODES - 2 * L
    sources = ((own_ref, 0, None), (left_ref, -LOC, 0), (right_ref, LOC, 1))
    for i, (ref, shift, side) in enumerate(sources):
        r = slice(i * CELLS, (i + 1) * CELLS)
        lows, tops = [], []
        for j in range(NJ):
            dofs = ref[0:CELLS, j * L : (j + 1) * L] + float(shift)
            real = lane < (L if j < 2 else tail)
            low = jnp.where(real, dofs, float(BIG))
            all_ref[r, j * L : (j + 1) * L] = low
            pot = ref[0:CELLS, NPAD + j * L : NPAD + (j + 1) * L]
            all_ref[r, NPAD + j * L : NPAD + (j + 1) * L] = jnp.where(real, pot, 0.0)
            lows.append(jnp.min(low, axis=1, keepdims=True).astype(I32))
            tops.append(jnp.max(jnp.where(real, dofs, -float(BIG)), axis=1, keepdims=True).astype(I32))
        scales = jnp.broadcast_to(ref[CELLS : CELLS + 1, 0:L], (CELLS, L))
        scale = jnp.sum(jnp.where(lane == cell, scales, 0.0), axis=1, keepdims=True)
        all_ref[r, 2 * NPAD :] = jnp.broadcast_to(scale, (CELLS, L))
        count = jnp.broadcast_to(ref[CELLS : CELLS + 1, L : 2 * L], (CELLS, L))
        live = cell.astype(F32) < count
        if side is not None:
            live = live & jnp.full((CELLS, L), dom_ref[1 + side] > 0)
        low = jnp.minimum(jnp.minimum(lows[0], lows[1]), lows[2])
        top = jnp.maximum(jnp.maximum(tops[0], tops[1]), tops[2])
        used = live & (top >= RIM) & (low < RIM + LOC)
        starts = [jnp.minimum(x >> 7, EXT // L - NARROW) for x in lows]
        narrow = ((tops[0] >> 7) - starts[0] < NARROW) & ((tops[1] >> 7) - starts[1] < NARROW)
        narrow = narrow & ((tops[2] >> 7) - starts[2] < NARROW)
        base = jnp.minimum(low >> 7, EXT // L - WIDE)
        meta = jnp.where(used, jnp.where(narrow, 0, 1), -1)
        for j in range(NJ):
            meta = jnp.where(lane == 1 + j, jnp.where(narrow, starts[j], base), meta)
        meta_ref[r, :] = meta
    copy = pltpu.make_async_copy(meta_ref, meta_s, sem)
    copy.start()
    pad_ref[...] = jnp.zeros_like(pad_ref)
    load.wait()
    pad_ref[0:NODES, 0:NODES] = k_ref[...]
    kh_ref[...], kl_ref[...] = split(pad_ref[...])
    copy.wait()

    def scan(c, counts):
        kind = meta_s[c, 0]
        n, m = counts
        list_s[n] = c
        wide_s[m] = c
        return n + jnp.where(kind == 0, 1, 0), m + jnp.where(kind == 1, 1, 0)

    n, m = lax.fori_loop(0, 3 * CELLS, scan, (0, 0), unroll=4)
    gn = (n + GROUP - 1) // GROUP
    gw = (m + GROUP - 1) // GROUP
    first = (gn + 1) * GROUP
    last = first + gw * GROUP

    def blank(i, _):
        list_s[i] = -1
        return 0

    def move(i, _):
        list_s[first + i] = wide_s[i]
        return 0

    lax.fori_loop(n, first, blank, 0)
    lax.fori_loop(0, m, move, 0)
    lax.fori_loop(first + m, last, blank, 0)
    base_ref[4 * SLOTS] = gn
    base_ref[4 * SLOTS + 1] = gw

    def one(slot):
        c = list_s[slot]
        valid = c >= 0
        c = jnp.maximum(c, 0)
        vals = all_ref[pl.ds(c, 1), :]
        rels = []
        for j in range(NJ):
            b = jnp.where(valid, meta_s[c, 1 + j], 0)
            base_ref[4 * slot + j] = b
            rel = vals[:, j * L : (j + 1) * L].astype(I32) - b * L
            rel = jnp.where(valid & (rel < WIDE * L), rel, BIG)
            rels.append(rel)
            tab_ref[slot, j : j + 1, :] = rel
            pot_ref[slot, j : j + 1, :] = vals[:, NPAD + j * L : NPAD + (j + 1) * L]
        pot_ref[slot, 3:4, :] = vals[:, 2 * NPAD :]
        inv = inverse(rels)
        for j in range(NJ):
            tab_ref[slot, 3 + 3 * j : 6 + 3 * j, :] = inv[8 * j : 8 * j + NARROW]

    def some(i, _):
        for k in range(8):
            one(i * 8 + k)
        return 0

    lax.fori_loop(0, last // 8, some, 0)


def cell_tables(own, left, right, dom, stiffness):
    return pl.pallas_call(
        cells_kernel,
        out_shape=(
            sds((SLOTS, 16, L), I32),
            sds((SLOTS, 8, L)),
            sds((NPAD, NPAD), BF16),
            sds((NPAD, NPAD), BF16),
            sds((4 * SLOTS + L,), I32),
        ),
        in_specs=[VM] * 3 + [SM, HBM],
        out_specs=(VM, VM, VM, VM, SM),
        scratch_shapes=[
            pltpu.VMEM((3 * CELLS, PW), F32),
            pltpu.VMEM((3 * CELLS, L), I32),
            pltpu.VMEM((NODES, NODES), F32),
            pltpu.VMEM((NPAD, NPAD), F32),
            pltpu.SMEM((3 * CELLS, L), I32),
            pltpu.SMEM((SLOTS + GROUP,), I32),
            pltpu.SMEM((3 * CELLS + GROUP,), I32),
            pltpu.SemaphoreType.DMA,
            pltpu.SemaphoreType.DMA,
        ],
        compiler_params=pltpu.CompilerParams(vmem_limit_bytes=SMALL),
        name="cell_tables",
    )(own, left, right, dom, stiffness)


def step_kernel(number, *refs):
    (u_ref, gl_ref, gr_ref, prev_ref, tab_ref, pot_ref, kh_ref, kl_ref,
     oh_ref, pe_ref, w_ref, src_ref, posr_ref, hq_ref, base_ref, start_ref, me_ref) = refs[:17]
    outs = refs[17 : 17 + (8 if number == 3 else 3)]
    ext_ref, acc0_ref, acc1_ref, x_ref, p_ref, z_ref, g_ref, lhs_ref = refs[17 + len(outs) :]
    accs = (acc0_ref, acc1_ref)
    ext_ref[:, 0:RIM] = jnp.where(me_ref[1] > 0, gl_ref[...], 0.0)
    ext_ref[:, RIM : RIM + LOC] = u_ref[...]
    ext_ref[:, RIM + LOC :] = jnp.where(me_ref[2] > 0, gr_ref[...], 0.0)
    for ref in accs:
        ref[...] = jnp.zeros_like(ref)
    gn = base_ref[4 * SLOTS]
    gw = base_ref[4 * SLOTS + 1]

    def load(slot, width):
        for j in range(NJ):
            b = base_ref[4 * slot + j]
            row = jnp.broadcast_to(tab_ref[slot, j : j + 1, :], (8, L))
            lo, hi = row & 127, row >> 7
            for s in range(2):
                r = slice(8 * s, 8 * s + 8)
                acc = lanes(ext_ref[r, at(b)], lo)
                for t in range(1, width):
                    acc = jnp.where(hi == t, lanes(ext_ref[r, at(b + t)], lo), acc)
                x_ref[pl.ds(pl.multiple_of((slot & (RING - 1)) * S + 8 * s, 8), 8), j * L : (j + 1) * L] = acc

    def store(slot, parity, width):
        acc_ref = accs[parity]
        scale = jnp.broadcast_to(pot_ref[slot, 3:4, :], (8, L))
        if width == NARROW:
            inv = [[tab_ref[slot, 3 + 3 * j + t : 4 + 3 * j + t, :] for t in range(width)] for j in range(NJ)]
        else:
            full = inverse([tab_ref[slot, j : j + 1, :] for j in range(NJ)])
            inv = [[full[8 * j + t : 8 * j + t + 1] for t in range(width)] for j in range(NJ)]
        for j in range(NJ):
            b = base_ref[4 * slot + j]
            col = slice(j * L, (j + 1) * L)
            pot = jnp.broadcast_to(pot_ref[slot, j : j + 1, :], (8, L))
            vals = []
            for s in range(2):
                r = pl.ds(pl.multiple_of((slot & (RING - 1)) * S + 8 * s, 8), 8)
                vals.append(scale * p_ref[r, col] + pot * x_ref[r, col])
            adds = []
            for t in range(width):
                row = jnp.broadcast_to(inv[j][t], (8, L))
                m, lo = row >= 0, row & 127
                adds.append([jnp.where(m, lanes(vals[s], lo), 0.0) for s in range(2)])
            olds = [[acc_ref[8 * s : 8 * s + 8, at(b + t)] for s in range(2)] for t in range(width)]
            for t in range(width):
                for s in range(2):
                    acc_ref[8 * s : 8 * s + 8, at(b + t)] = olds[t][s] + adds[t][s]

    def rows_of(i):
        return pl.ds(pl.multiple_of((i & 3) * (GROUP * S), GROUP * S), GROUP * S)

    def product(i):
        xh, xl = split(x_ref[rows_of(i), :])
        kh, kl = kh_ref[...], kl_ref[...]
        return nt(xh, kh) + (nt(xl, kh) + nt(xh, kl))

    def load_group(i, width):
        def four(q, _):
            for k in range(4):
                load(i * GROUP + q * 4 + k, width)
            return 0

        lax.fori_loop(0, GROUP // 4, four, 0)

    def store_group(i, width):
        def four(q, _):
            for k in range(4):
                store(i * GROUP + q * 4 + k, k % 2, width)
            return 0

        lax.fori_loop(0, GROUP // 4, four, 0)

    load_group(0, NARROW)

    def pipeline(i, _):
        prod = product(i)
        before = jnp.where(i == 0, gn, i - 1)
        for k in range(GROUP):
            store(before * GROUP + k, k % 2, NARROW)
        p_ref[rows_of(i), :] = prod
        for k in range(GROUP):
            load((i + 1) * GROUP + k, NARROW)
        return 0

    lax.fori_loop(0, gn, pipeline, 0)
    store_group(jnp.maximum(gn - 1, 0), NARROW)

    def wide(i, _):
        load_group(i, WIDE)
        p_ref[rows_of(i), :] = product(i)
        store_group(i, WIDE)
        return 0

    lax.fori_loop(gn + 1, gn + 1 + gw, wide, 0)

    def read(b):
        return acc0_ref[:, at(b + RB)] + acc1_ref[:, at(b + RB)]

    compress(read, z_ref, src_ref, start_ref)
    add_to_masters(z_ref, oh_ref, pe_ref, w_ref, g_ref, lhs_ref)
    hanging_values(z_ref, oh_ref, pe_ref, w_ref, g_ref, lhs_ref, hq_ref)
    new_ref = outs[0] if number < 3 else ext_ref

    def finish(i, _):
        for k in range(UNROLL):
            b = i * UNROLL + k
            t = expand(b, read(b), z_ref, posr_ref, start_ref)
            r = (t - CENTRE * u_ref[:, at(b)]) * ((1.0 if number == 1 else 2.0) / HALF)
            if number > 1:
                r = r - prev_ref[:, at(b)]
            new_ref[:, at(b)] = r
        return 0

    lax.fori_loop(0, NB // UNROLL, finish, 0)
    if number < 3:
        outs[1][...] = new_ref[:, 0:RIM]
        outs[2][...] = new_ref[:, LOC - RIM :]
    else:
        me = me_ref[0]
        q = LOC // 4
        for k in range(4):
            outs[k][...] = new_ref[:, pl.ds(pl.multiple_of(((me + k) & 3) * q, L), q)]
            for r in range(1, 4):
                part = new_ref[:, pl.ds(pl.multiple_of(((me + k + r) & 3) * q, L), q)]
                outs[4 + k][:, (r - 1) * q : r * q] = part


def apply_step(number, u, gl, gr, prev, cell, base, hang, start, me):
    if number == 3:
        shapes = (sds((S, LOC // 4)),) * 4 + (sds((S, 3 * LOC // 4)),) * 4
    else:
        shapes = (sds((S, LOC)), sds((S, RIM)), sds((S, RIM)))
    return pl.pallas_call(
        functools.partial(step_kernel, number),
        out_shape=shapes,
        in_specs=[VM] * 14 + [SM] * 3,
        out_specs=(VM,) * len(shapes),
        scratch_shapes=[
            pltpu.VMEM((S, EXT), F32),
            pltpu.VMEM((S, EXT), F32),
            pltpu.VMEM((S, EXT), F32),
            pltpu.VMEM((RING * S, NPAD), F32),
            pltpu.VMEM((RING * S, NPAD), F32),
            *HANG_SCRATCH,
        ],
        compiler_params=pltpu.CompilerParams(vmem_limit_bytes=VLIM),
        name=f"step{number}",
    )(u, gl, gr, prev, *cell, *hang, base, start, me)


def gram_kernel(q0_ref, q1_ref, q2_ref, q3_ref, me_ref, gram_ref, all_ref):
    me = me_ref[0]
    for k, ref in enumerate((q0_ref, q1_ref, q2_ref, q3_ref)):
        all_ref[pl.ds(pl.multiple_of(((me - k) & 3) * S, S), S), :] = ref[...]
    a = all_ref[...]
    gram_ref[...] = lax.dot_general(a, a, NT, preferred_element_type=F32, precision=lax.Precision.HIGHEST)


def gram_of(qs, me):
    n = qs[0].shape[1]
    return pl.pallas_call(
        gram_kernel,
        out_shape=(sds((4 * S, 4 * S)), sds((4 * S, n))),
        in_specs=[VM] * 4 + [SM],
        out_specs=(VM, VM),
        compiler_params=pltpu.CompilerParams(vmem_limit_bytes=VLIM),
        name="gram",
    )(*qs, me)


def factor_kernel(total, gram_ref, inv_ref):
    n = 4 * S
    eye = (iota((n, n), 0) == iota((n, n), 1)).astype(F32)
    m = jnp.concatenate([gram_ref[...], eye], 1)
    row = iota((n, 2 * n), 0)
    for j in range(0, n, 2):
        p1, p2 = m[j : j + 1, :], m[j + 1 : j + 2, :]
        c1, c2 = m[:, j : j + 1], m[:, j + 1 : j + 2]
        ra = 1.0 / p1[:, j : j + 1]
        l = p2[:, j : j + 1] * ra
        p2 = p2 - l * p1
        rc = 1.0 / (m[j + 1 : j + 2, j + 1 : j + 2] - l * p1[:, j + 1 : j + 2])
        update = c1 * (p1 * ra) + (c2 - c1 * (p1[:, j + 1 : j + 2] * ra)) * (p2 * rc)
        m = jnp.where(row > j + 1, m - update, jnp.where(row == j + 1, p2, m))
    dg = jnp.sum(jnp.where(row == iota((n, 2 * n), 1), m, 0.0), axis=1, keepdims=True)
    inv_ref[...] = m[:, n:] * lax.rsqrt(dg) * jnp.sqrt(jnp.float32(total))


def factor_of(gram, total):
    return pl.pallas_call(
        functools.partial(factor_kernel, total),
        out_shape=sds((4 * S, 4 * S)),
        in_specs=[VM],
        out_specs=VM,
        compiler_params=pltpu.CompilerParams(vmem_limit_bytes=SMALL),
        name="factor",
    )(gram)


def basis_kernel(inv_ref, rows_ref, r0_ref, r1_ref, r2_ref, r3_ref, me_ref, out_ref, all_ref):
    me = me_ref[0]
    n = rows_ref.shape[1]
    ih, il = split(inv_ref[pl.ds(pl.multiple_of(me * S, S), S), :])
    lhs = jnp.concatenate([jnp.concatenate([ih, ih], 1), jnp.concatenate([il, jnp.zeros_like(il)], 1)], 0)
    for k, ref in enumerate((r0_ref, r1_ref, r2_ref, r3_ref)):
        all_ref[pl.ds(pl.multiple_of(((me - k) & 3) * S, S), S), :] = ref[...]

    def times(x):
        r = nn(lhs, jnp.concatenate(split(x), 0))
        return r[:S] + r[S:]

    for r in range(4):
        for i in range(3):
            w = n // 3
            col = slice(i * w, (i + 1) * w)
            x = rows_ref[:, col] if r == 0 else all_ref[:, (r - 1) * n + i * w : (r - 1) * n + (i + 1) * w]
            out_ref[:, pl.ds(pl.multiple_of(((me + r) & 3) * n + i * w, L), w)] = times(x)


def basis_of(inv, rows, rest, me):
    return pl.pallas_call(
        basis_kernel,
        out_shape=sds((S, LOC)),
        in_specs=[VM] * 6 + [SM],
        out_specs=VM,
        scratch_shapes=[pltpu.VMEM((4 * S, 3 * LOC // 4), F32)],
        compiler_params=pltpu.CompilerParams(vmem_limit_bytes=SMALL),
        name="basis",
    )(inv, rows, *rest, me)


def shift(x, axis, by):
    size = lax.axis_size(axis)
    return lax.ppermute(x, axis, [(i, (i + by) % size) for i in range(size)])


def swap(x, axis, bits):
    size = lax.axis_size(axis)
    return lax.ppermute(x, axis, [(i, i ^ bits) for i in range(size)])


def four(g, axis, unit):
    others = [swap(g, axis, unit * k) for k in (1, 2, 3)]
    return (g + others[0]) + (others[1] + others[2])


def body(
    block,
    stiffness,
    cell_scale,
    potential,
    cell_dofs,
    cell_count,
    hang_rows,
    hang_masters,
    hang_weights,
):
    dom = lax.axis_index("dom")
    inside = [lax.axis_index("band"), dom > 0, dom < lax.axis_size("dom") - 1]
    me = jnp.stack([jnp.asarray(x).astype(I32) for x in inside])
    own = pack(cell_dofs.T, potential.T, cell_scale[None], cell_count)
    from_left = shift(own, "dom", 1)
    from_right = shift(own, "dom", -1)
    *hang, start, u0, first, last = prepare(hang_rows[None], hang_masters, hang_weights, block)

    def ghosts(first, last):
        return shift(last, "dom", 1), shift(first, "dom", -1)

    gl, gr = ghosts(first, last)
    *cell, base = cell_tables(own, from_left, from_right, me, stiffness)
    args = (cell, base, hang, start, me)
    u1, first, last = apply_step(1, u0, gl, gr, u0, *args)
    gl, gr = ghosts(first, last)
    u2, first, last = apply_step(2, u1, gl, gr, u0, *args)
    gl, gr = ghosts(first, last)
    *qs, r0, r1, r2, r3 = apply_step(3, u2, gl, gr, u1, *args)
    qs = [qs[0]] + [shift(qs[k], "band", k) for k in (1, 2, 3)]
    gram, rows = gram_of(qs, me)
    gram = four(gram, "band", 1)
    gram, r1, r2, r3 = lax.optimization_barrier((gram, r1, r2, r3))
    rest = [r0] + [shift(r, "band", k) for k, r in ((1, r1), (2, r2), (3, r3))]
    gram = gram + swap(gram, "dom", 1)
    gram = four(four(gram, "dom", 2), "dom", 8)
    inv = factor_of(gram, LOC * lax.axis_size("dom"))
    return basis_of(inv, rows, rest, me)


def solution(mesh):
    return jax.shard_map(
        body,
        mesh=mesh,
        in_specs=(
            P("band", "dom"),
            P(),
            P("dom"),
            P(None, "dom"),
            P(None, "dom"),
            P("dom"),
            P("dom"),
            P(None, "dom"),
            P(None, "dom"),
        ),
        out_specs=P("band", "dom"),
        check_vma=False,
    )
```

```python
import functools
import jax
import jax.numpy as jnp
from jax import lax
from jax.experimental import pallas as pl
from jax.experimental.pallas import tpu as pltpu
from jax.sharding import PartitionSpec as P

RIM = 2048
NODES = 343
HANG = 864
MASTERS = 4
LOC = 13824
CELLS = 64
S = 16
L = 128
EXT = LOC + 2 * RIM
NB = LOC // L
RB = RIM // L
NPAD = 384
NJ = NPAD // L
WIDE = 7
NARROW = 3
PACK = 72
PW = 2 * NPAD + L
GROUP = 16
RING = 4 * GROUP
SLOTS = 14 * GROUP
HPAD = 896
HB = HPAD // L
ME = MASTERS * HPAD
HE = 1024
E = ME + HE
QLO = 512
QB = QLO // L
QHI = 9
BIG = 1 << 20
CENTRE = 4.5
HALF = 3.5
F32 = jnp.float32
BF16 = jnp.bfloat16
I32 = jnp.int32
VLIM = 28 * 1024 * 1024
SMALL = 20 * 1024 * 1024
WHOLE = 64 * 1024 * 1024

VM = pl.BlockSpec(memory_space=pltpu.VMEM)
SM = pl.BlockSpec(memory_space=pltpu.SMEM)
HBM = pl.BlockSpec(memory_space=pltpu.HBM)
NT = (((1,), (1,)), ((), ()))


def iota(shape, dim):
    return lax.broadcasted_iota(I32, shape, dim)


def lanes(x, idx):
    return jnp.take_along_axis(x, idx, axis=1, mode="promise_in_bounds")


def nn(a, b):
    return jnp.dot(a, b, preferred_element_type=F32)


def nt(a, b):
    return lax.dot_general(a, b, NT, preferred_element_type=F32)


def split(x):
    hi = x.astype(BF16)
    return hi, (x - hi.astype(F32)).astype(BF16)


def at(b):
    return pl.ds(pl.multiple_of(b * L, L), L)


def one_hot(row, n):
    return (jnp.broadcast_to(row, (n, row.shape[1])) == iota((n, row.shape[1]), 0)).astype(F32)


def hang_tables(ent_ref, a_ref, b_ref, lhs_ref, oh_ref, pe_ref, src_ref, posr_ref, hq_ref, start_ref):
    for i in range(E // L):
        col = slice(i * L, (i + 1) * L)
        row = ent_ref[0:1, col]
        a_ref[:, col] = one_hot(row >> 7, L).astype(BF16)
        b_ref[:, col] = one_hot(row & 127, L).astype(BF16)
    flag = nt(a_ref[...], b_ref[...]) > 0.5
    flagb = flag.astype(F32).astype(BF16)
    tri = (iota((L, L), 0) < iota((L, L), 1)).astype(F32).astype(BF16)
    low = (iota((L, L), 1) < iota((L, L), 0)).astype(F32).astype(BF16)
    total = nn(flagb, jnp.ones((L, L), BF16))
    pos = (nn(flagb, tri) + nn(low, total.astype(BF16))).astype(I32)
    posr_ref[...] = jnp.where(flag, pos, -1)
    totrow = nt(jnp.ones((8, L), BF16), flagb)
    start_ref[...] = nn(totrow.astype(BF16), tri).astype(I32)
    ph = (pos >> 7).astype(F32).astype(BF16)
    plo = (pos & 127).astype(F32).astype(BF16)
    for i in range(E // L):
        col = slice(i * L, (i + 1) * L)
        ent = ent_ref[0:1, col]
        mask = a_ref[:, col].astype(F32)
        b = b_ref[:, col]
        hi = jnp.sum(nn(ph, b) * mask, axis=0, keepdims=True)
        lo = jnp.sum(nn(plo, b) * mask, axis=0, keepdims=True)
        pe = jnp.where(ent >= 0, hi.astype(I32) * L + lo.astype(I32), BIG)
        pe_ref[0:1, col] = pe
        oh_ref[:, col] = one_hot(pe & (QLO - 1), QLO).astype(BF16)
        qm = one_hot(pe // QLO, 16)
        lhs_ref[0:16, col] = qm.astype(BF16)
        lhs_ref[16:32, col] = (qm * (ent >> 7).astype(F32)).astype(BF16)
        lhs_ref[32:48, col] = (qm * (ent & 127).astype(F32)).astype(BF16)
        lhs_ref[48:64, col] = (qm if i >= ME // L else jnp.zeros_like(qm)).astype(BF16)
    res = nt(lhs_ref[...], oh_ref[...])
    cnt = res[0:16]
    den = jnp.maximum(cnt, 1.0)
    blk = (res[16:32] / den + 0.5).astype(I32)
    lo = (res[32:48] / den + 0.5).astype(I32)
    src = jnp.where(cnt > 0.5, blk * L + lo, -1)
    for q in range(QHI):
        for t in range(QB):
            src_ref[QB * q + t : QB * q + t + 1, :] = src[q : q + 1, t * L : (t + 1) * L]
    hq_ref[...] = res[48:64]


def zat(c):
    return pl.ds(pl.multiple_of((c // QB) * S, S), S), pl.ds(pl.multiple_of((c % QB) * L, L), L)


UNROLL = 12


def compress(read, z_ref, src_ref, start_ref):
    z_ref[...] = jnp.zeros_like(z_ref)

    def step(i, cur):
        for k in range(UNROLL):
            b = i * UNROLL + k
            y = read(b)
            c = start_ref[0, b] >> 7
            ahead = start_ref[0, b + 1] >> 7
            parts = []
            for t in range(2):
                row = jnp.broadcast_to(src_ref[pl.ds(c + t, 1), :], (S, L))
                parts.append(((row >> 7) == b, lanes(y, row & 127)))
            cur = jnp.where(parts[0][0], parts[0][1], cur)
            r, l = zat(c)
            z_ref[r, l] = cur
            after = jnp.where(parts[1][0], parts[1][1], 0.0)
            cur = jnp.where(ahead > c, after, cur)
        return cur

    cur = lax.fori_loop(0, NB // UNROLL, step, jnp.zeros((S, L), F32))
    r, l = zat(start_ref[0, NB] >> 7)
    z_ref[r, l] = cur


def expand(b, y, z_ref, posr_ref, start_ref):
    row = jnp.broadcast_to(posr_ref[pl.ds(b, 1), :], (S, L))
    c0 = start_ref[0, b] >> 7
    for t in range(2):
        c = c0 + t
        r, l = zat(c)
        y = jnp.where((row >> 7) == c, lanes(z_ref[r, l], row & 127), y)
    return y


def gather_entries(z_ref, oh_ref, pe_ref, g_ref, first, last):
    zz = jnp.concatenate(split(z_ref[...]), axis=0)
    n = QHI * S
    w = 256
    for i in range(first // w, last // w):
        col = slice(i * w, (i + 1) * w)
        g = nn(zz, oh_ref[:, col])
        q = jnp.broadcast_to(pe_ref[0:1, col] // QLO, (S, w))
        hi = g[0:S]
        lo = g[n : n + S]
        for h in range(1, QHI):
            m = q == h
            hi = jnp.where(m, g[h * S : (h + 1) * S], hi)
            lo = jnp.where(m, g[n + h * S : n + (h + 1) * S], lo)
        g_ref[:, col] = hi + lo


def scatter_entries(g_ref, oh_ref, pe_ref, lhs_ref, first, last):
    n = QHI * S
    for i in range(first // L, last // L):
        col = slice(i * L, (i + 1) * L)
        g = g_ref[:, col]
        hi = g.astype(BF16).astype(F32)
        lo = g - hi
        q = jnp.broadcast_to(pe_ref[0:1, col] // QLO, (S, L))
        for h in range(QHI):
            m = q == h
            lhs_ref[h * S : (h + 1) * S, col] = jnp.where(m, hi, 0.0).astype(BF16)
            lhs_ref[n + h * S : n + (h + 1) * S, col] = jnp.where(m, lo, 0.0).astype(BF16)
    res = nt(lhs_ref[:, first:last], oh_ref[:, first:last])
    return res[:n] + res[n:]


def hanging_values(z_ref, oh_ref, pe_ref, w_ref, g_ref, lhs_ref, hq_ref):
    gather_entries(z_ref, oh_ref, pe_ref, g_ref, 0, ME)
    g_ref[:, ME + HPAD :] = jnp.zeros((S, HE - HPAD), F32)
    for j in range(HB):
        acc = jnp.zeros((S, L), F32)
        for k in range(MASTERS):
            col = slice(k * HPAD + j * L, k * HPAD + (j + 1) * L)
            acc = acc + g_ref[:, col] * w_ref[0:1, col]
        g_ref[:, ME + j * L : ME + (j + 1) * L] = acc
    cz = scatter_entries(g_ref, oh_ref, pe_ref, lhs_ref, ME, E)
    for h in range(QHI):
        r = slice(h * S, (h + 1) * S)
        m = jnp.broadcast_to(hq_ref[h : h + 1, :], (S, QLO)) > 0.5
        z_ref[r, :] = jnp.where(m, cz[r], z_ref[r, :])


def add_to_masters(z_ref, oh_ref, pe_ref, w_ref, g_ref, lhs_ref):
    gather_entries(z_ref, oh_ref, pe_ref, g_ref, ME, E)
    for j in range(HB):
        y = g_ref[:, ME + j * L : ME + (j + 1) * L]
        for k in range(MASTERS):
            col = slice(k * HPAD + j * L, k * HPAD + (j + 1) * L)
            g_ref[:, col] = y * w_ref[0:1, col]
    z_ref[...] += scatter_entries(g_ref, oh_ref, pe_ref, lhs_ref, 0, ME)


def prepare_kernel(
    hang_ref, block_ref,
    pe_ref, w_ref, src_ref, posr_ref, hq_ref, start_ref, u_ref, left_ref, right_ref,
    ent_ref, oh_ref, a_ref, b_ref, tab_ref, z_ref, g_ref, lhs_ref, start_s, sem,
):
    for k in range(MASTERS):
        col = slice(k * HPAD, (k + 1) * HPAD)
        ent_ref[0:1, col] = hang_ref[k : k + 1, :].astype(I32)
        w_ref[0:1, col] = hang_ref[MASTERS + 1 + k : MASTERS + 2 + k, :]
    ent_ref[0:1, ME + HPAD :] = jnp.full((1, HE - HPAD), -1, I32)
    ent_ref[0:1, ME : ME + HPAD] = hang_ref[MASTERS : MASTERS + 1, :].astype(I32)
    hang_tables(ent_ref, a_ref, b_ref, tab_ref, oh_ref, pe_ref, src_ref, posr_ref, hq_ref, start_ref)
    copy = pltpu.make_async_copy(start_ref, start_s, sem)
    copy.start()
    copy.wait()
    compress(lambda b: block_ref[:, at(b)], z_ref, src_ref, start_s)
    hanging_values(z_ref, oh_ref, pe_ref, w_ref, g_ref, lhs_ref, hq_ref)

    def step(i, _):
        for k in range(UNROLL):
            b = i * UNROLL + k
            u_ref[:, at(b)] = expand(b, block_ref[:, at(b)], z_ref, posr_ref, start_s)
        return 0

    lax.fori_loop(0, NB // UNROLL, step, 0)
    left_ref[...] = u_ref[:, 0:RIM]
    right_ref[...] = u_ref[:, LOC - RIM :]


def sds(shape, dtype=F32):
    return jax.ShapeDtypeStruct(shape, dtype)


HANG_SCRATCH = [
    pltpu.VMEM((QHI * S, QLO), F32),
    pltpu.VMEM((S, E), F32),
    pltpu.VMEM((2 * QHI * S, E), BF16),
]


def prepare(hang, block):
    return pl.pallas_call(
        prepare_kernel,
        out_shape=(
            sds((1, E), I32),
            sds((1, ME)),
            sds((QB * QHI + 4, L), I32),
            sds((L, L), I32),
            sds((16, QLO)),
            sds((8, L), I32),
            sds((S, LOC)),
            sds((S, RIM)),
            sds((S, RIM)),
        ),
        in_specs=[VM] * 2,
        out_specs=(VM,) * 9,
        scratch_shapes=[
            pltpu.VMEM((1, E), I32),
            pltpu.VMEM((QLO, E), BF16),
            pltpu.VMEM((L, E), BF16),
            pltpu.VMEM((L, E), BF16),
            pltpu.VMEM((64, E), BF16),
            *HANG_SCRATCH,
            pltpu.SMEM((8, L), I32),
            pltpu.SemaphoreType.DMA,
        ],
        compiler_params=pltpu.CompilerParams(vmem_limit_bytes=VLIM),
        name="prepare",
    )(hang, block)


def pack_kernel(
    dofs_hbm, pot_hbm, scale_hbm, rows_hbm, masters_hbm, weights_hbm, count_ref,
    own_ref, hang_ref,
    dofs_ref, pot_ref, scale_ref, rows_ref, masters_ref, weights_ref, sems,
):
    moves = (
        (dofs_hbm, dofs_ref),
        (pot_hbm, pot_ref),
        (scale_hbm, scale_ref),
        (rows_hbm, rows_ref),
        (masters_hbm, masters_ref),
        (weights_hbm, weights_ref),
    )
    loads = [pltpu.make_async_copy(src, dst, sems.at[i]) for i, (src, dst) in enumerate(moves)]
    for load in loads:
        load.start()
    for load in loads:
        load.wait()
    own_ref[0:CELLS, 0:NODES] = dofs_ref[...].astype(F32)
    own_ref[0:CELLS, NPAD : NPAD + NODES] = pot_ref[...]
    scale = jnp.broadcast_to(scale_ref[...].reshape(1, CELLS), (PACK - CELLS, CELLS))
    own_ref[CELLS:PACK, 0:CELLS] = scale
    own_ref[CELLS:PACK, L : 2 * L] = jnp.full((PACK - CELLS, L), count_ref[0]).astype(F32)
    hang_ref[...] = jnp.where(iota((2 * MASTERS + 1, HPAD), 0) < MASTERS + 1, -1.0, 0.0)
    hang_ref[0:MASTERS, 0:HANG] = masters_ref[...].astype(F32)
    hang_ref[MASTERS : MASTERS + 1, 0:HANG] = rows_ref[...].reshape(1, HANG).astype(F32)
    hang_ref[MASTERS + 1 :, 0:HANG] = weights_ref[...]


def pack(dofs, pot, scale, rows, masters, weights, count):
    return pl.pallas_call(
        pack_kernel,
        out_shape=(sds((PACK, PW)), sds((2 * MASTERS + 1, HPAD))),
        in_specs=[HBM] * 6 + [SM],
        out_specs=(VM, VM),
        scratch_shapes=[
            pltpu.VMEM((CELLS, NODES), I32),
            pltpu.VMEM((CELLS, NODES), F32),
            pltpu.VMEM((CELLS,), F32),
            pltpu.VMEM((HANG,), I32),
            pltpu.VMEM((MASTERS, HANG), I32),
            pltpu.VMEM((MASTERS, HANG), F32),
            pltpu.SemaphoreType.DMA((6,)),
        ],
        compiler_params=pltpu.CompilerParams(vmem_limit_bytes=WHOLE),
        name="pack",
    )(dofs, pot, scale, rows, masters, weights, count)


def inverse(rels):
    oh = jnp.concatenate([one_hot(rel & 127, L) for rel in rels], axis=1).astype(BF16)
    rows = []
    for j, rel in enumerate(rels):
        m = jnp.broadcast_to(rel >> 7, (8, L)) == iota((8, L), 0)
        node = jnp.where(m, iota((8, L), 1) + 1, 0).astype(F32)
        zero = jnp.zeros((8, L), F32)
        rows.append(jnp.concatenate([node if i == j else zero for i in range(len(rels))], axis=1))
    return nt(jnp.concatenate(rows, axis=0).astype(BF16), oh).astype(I32) - 1


def cells_kernel(
    own_ref, left_ref, right_ref, pe_ref, dom_ref, k_hbm,
    tab_ref, pot_ref, kh_ref, kl_ref, oh_ref, base_ref,
    all_ref, meta_ref, k_ref, pad_ref, meta_s, list_s, wide_s, sem, sem_k,
):
    load = pltpu.make_async_copy(k_hbm, k_ref, sem_k)
    load.start()
    lane = iota((CELLS, L), 1)
    cell = iota((CELLS, L), 0)
    tail = NODES - 2 * L
    sources = ((own_ref, 0, None), (left_ref, -LOC, 0), (right_ref, LOC, 1))
    for i, (ref, shift, side) in enumerate(sources):
        r = slice(i * CELLS, (i + 1) * CELLS)
        lows, tops = [], []
        for j in range(NJ):
            dofs = ref[0:CELLS, j * L : (j + 1) * L] + float(shift)
            real = lane < (L if j < 2 else tail)
            low = jnp.where(real, dofs, float(BIG))
            all_ref[r, j * L : (j + 1) * L] = low
            pot = ref[0:CELLS, NPAD + j * L : NPAD + (j + 1) * L]
            all_ref[r, NPAD + j * L : NPAD + (j + 1) * L] = jnp.where(real, pot, 0.0)
            lows.append(jnp.min(low, axis=1, keepdims=True).astype(I32))
            tops.append(jnp.max(jnp.where(real, dofs, -float(BIG)), axis=1, keepdims=True).astype(I32))
        scales = jnp.broadcast_to(ref[CELLS : CELLS + 1, 0:L], (CELLS, L))
        scale = jnp.sum(jnp.where(lane == cell, scales, 0.0), axis=1, keepdims=True)
        all_ref[r, 2 * NPAD :] = jnp.broadcast_to(scale, (CELLS, L))
        count = jnp.broadcast_to(ref[CELLS : CELLS + 1, L : 2 * L], (CELLS, L))
        live = cell.astype(F32) < count
        if side is not None:
            live = live & jnp.full((CELLS, L), dom_ref[1 + side] > 0)
        low = jnp.minimum(jnp.minimum(lows[0], lows[1]), lows[2])
        top = jnp.maximum(jnp.maximum(tops[0], tops[1]), tops[2])
        used = live & (top >= RIM) & (low < RIM + LOC)
        starts = [jnp.minimum(x >> 7, EXT // L - NARROW) for x in lows]
        narrow = ((tops[0] >> 7) - starts[0] < NARROW) & ((tops[1] >> 7) - starts[1] < NARROW)
        narrow = narrow & ((tops[2] >> 7) - starts[2] < NARROW)
        base = jnp.minimum(low >> 7, EXT // L - WIDE)
        meta = jnp.where(used, jnp.where(narrow, 0, 1), -1)
        for j in range(NJ):
            meta = jnp.where(lane == 1 + j, jnp.where(narrow, starts[j], base), meta)
        meta_ref[r, :] = meta
    copy = pltpu.make_async_copy(meta_ref, meta_s, sem)
    copy.start()
    pad_ref[...] = jnp.zeros_like(pad_ref)
    load.wait()
    pad_ref[0:NODES, 0:NODES] = k_ref[...]
    kh_ref[...], kl_ref[...] = split(pad_ref[...])
    for i in range(E // L):
        col = slice(i * L, (i + 1) * L)
        oh_ref[:, col] = one_hot(pe_ref[0:1, col] & (QLO - 1), QLO).astype(BF16)
    copy.wait()

    def scan(c, counts):
        kind = meta_s[c, 0]
        n, m = counts
        list_s[n] = c
        wide_s[m] = c
        return n + jnp.where(kind == 0, 1, 0), m + jnp.where(kind == 1, 1, 0)

    n, m = lax.fori_loop(0, 3 * CELLS, scan, (0, 0), unroll=4)
    gn = (n + GROUP - 1) // GROUP
    gw = (m + GROUP - 1) // GROUP
    first = (gn + 1) * GROUP
    last = first + gw * GROUP

    def blank(i, _):
        list_s[i] = -1
        return 0

    def move(i, _):
        list_s[first + i] = wide_s[i]
        return 0

    lax.fori_loop(n, first, blank, 0)
    lax.fori_loop(0, m, move, 0)
    lax.fori_loop(first + m, last, blank, 0)
    base_ref[4 * SLOTS] = gn
    base_ref[4 * SLOTS + 1] = gw

    def one(slot):
        c = list_s[slot]
        valid = c >= 0
        c = jnp.maximum(c, 0)
        vals = all_ref[pl.ds(c, 1), :]
        rels = []
        for j in range(NJ):
            b = jnp.where(valid, meta_s[c, 1 + j], 0)
            base_ref[4 * slot + j] = b
            rel = vals[:, j * L : (j + 1) * L].astype(I32) - b * L
            rel = jnp.where(valid & (rel < WIDE * L), rel, BIG)
            rels.append(rel)
            tab_ref[slot, j : j + 1, :] = rel
            pot_ref[slot, j : j + 1, :] = vals[:, NPAD + j * L : NPAD + (j + 1) * L]
        pot_ref[slot, 3:4, :] = vals[:, 2 * NPAD :]
        inv = inverse(rels)
        for j in range(NJ):
            tab_ref[slot, 3 + 3 * j : 6 + 3 * j, :] = inv[8 * j : 8 * j + NARROW]

    def some(i, _):
        for k in range(8):
            one(i * 8 + k)
        return 0

    lax.fori_loop(0, last // 8, some, 0)


def cell_tables(own, left, right, pe, dom, stiffness):
    return pl.pallas_call(
        cells_kernel,
        out_shape=(
            sds((SLOTS, 16, L), I32),
            sds((SLOTS, 8, L)),
            sds((NPAD, NPAD), BF16),
            sds((NPAD, NPAD), BF16),
            sds((QLO, E), BF16),
            sds((4 * SLOTS + L,), I32),
        ),
        in_specs=[VM] * 4 + [SM, HBM],
        out_specs=(VM, VM, VM, VM, VM, SM),
        scratch_shapes=[
            pltpu.VMEM((3 * CELLS, PW), F32),
            pltpu.VMEM((3 * CELLS, L), I32),
            pltpu.VMEM((NODES, NODES), F32),
            pltpu.VMEM((NPAD, NPAD), F32),
            pltpu.SMEM((3 * CELLS, L), I32),
            pltpu.SMEM((SLOTS + GROUP,), I32),
            pltpu.SMEM((3 * CELLS + GROUP,), I32),
            pltpu.SemaphoreType.DMA,
            pltpu.SemaphoreType.DMA,
        ],
        compiler_params=pltpu.CompilerParams(vmem_limit_bytes=SMALL),
        name="cell_tables",
    )(own, left, right, pe, dom, stiffness)


def step_kernel(number, *refs):
    (u_ref, gl_ref, gr_ref, prev_ref, tab_ref, pot_ref, kh_ref, kl_ref,
     oh_ref, pe_ref, w_ref, src_ref, posr_ref, hq_ref, base_ref, start_ref, me_ref) = refs[:17]
    outs = refs[17 : 17 + (4 if number == 3 else 3)]
    ext_ref, acc0_ref, acc1_ref, x_ref, p_ref, z_ref, g_ref, lhs_ref = refs[17 + len(outs) :]
    accs = (acc0_ref, acc1_ref)
    ext_ref[:, 0:RIM] = jnp.where(me_ref[1] > 0, gl_ref[...], 0.0)
    ext_ref[:, RIM : RIM + LOC] = u_ref[...]
    ext_ref[:, RIM + LOC :] = jnp.where(me_ref[2] > 0, gr_ref[...], 0.0)
    for ref in accs:
        ref[...] = jnp.zeros_like(ref)
    gn = base_ref[4 * SLOTS]
    gw = base_ref[4 * SLOTS + 1]

    def load(slot, width):
        for j in range(NJ):
            b = base_ref[4 * slot + j]
            row = jnp.broadcast_to(tab_ref[slot, j : j + 1, :], (8, L))
            lo, hi = row & 127, row >> 7
            for s in range(2):
                r = slice(8 * s, 8 * s + 8)
                acc = lanes(ext_ref[r, at(b)], lo)
                for t in range(1, width):
                    acc = jnp.where(hi == t, lanes(ext_ref[r, at(b + t)], lo), acc)
                x_ref[pl.ds(pl.multiple_of((slot & (RING - 1)) * S + 8 * s, 8), 8), j * L : (j + 1) * L] = acc

    def store(slot, parity, width):
        acc_ref = accs[parity]
        scale = jnp.broadcast_to(pot_ref[slot, 3:4, :], (8, L))
        if width == NARROW:
            inv = [[tab_ref[slot, 3 + 3 * j + t : 4 + 3 * j + t, :] for t in range(width)] for j in range(NJ)]
        else:
            full = inverse([tab_ref[slot, j : j + 1, :] for j in range(NJ)])
            inv = [[full[8 * j + t : 8 * j + t + 1] for t in range(width)] for j in range(NJ)]
        for j in range(NJ):
            b = base_ref[4 * slot + j]
            col = slice(j * L, (j + 1) * L)
            pot = jnp.broadcast_to(pot_ref[slot, j : j + 1, :], (8, L))
            vals = []
            for s in range(2):
                r = pl.ds(pl.multiple_of((slot & (RING - 1)) * S + 8 * s, 8), 8)
                vals.append(scale * p_ref[r, col] + pot * x_ref[r, col])
            adds = []
            for t in range(width):
                row = jnp.broadcast_to(inv[j][t], (8, L))
                m, lo = row >= 0, row & 127
                adds.append([jnp.where(m, lanes(vals[s], lo), 0.0) for s in range(2)])
            olds = [[acc_ref[8 * s : 8 * s + 8, at(b + t)] for s in range(2)] for t in range(width)]
            for t in range(width):
                for s in range(2):
                    acc_ref[8 * s : 8 * s + 8, at(b + t)] = olds[t][s] + adds[t][s]

    def rows_of(i):
        return pl.ds(pl.multiple_of((i & 3) * (GROUP * S), GROUP * S), GROUP * S)

    def product(i):
        xh, xl = split(x_ref[rows_of(i), :])
        kh, kl = kh_ref[...], kl_ref[...]
        return nt(xh, kh) + (nt(xl, kh) + nt(xh, kl))

    def load_group(i, width):
        def four(q, _):
            for k in range(4):
                load(i * GROUP + q * 4 + k, width)
            return 0

        lax.fori_loop(0, GROUP // 4, four, 0)

    def store_group(i, width):
        def four(q, _):
            for k in range(4):
                store(i * GROUP + q * 4 + k, k % 2, width)
            return 0

        lax.fori_loop(0, GROUP // 4, four, 0)

    load_group(0, NARROW)

    def pipeline(i, _):
        prod = product(i)
        before = jnp.where(i == 0, gn, i - 1)
        for k in range(GROUP):
            store(before * GROUP + k, k % 2, NARROW)
        p_ref[rows_of(i), :] = prod
        for k in range(GROUP):
            load((i + 1) * GROUP + k, NARROW)
        return 0

    lax.fori_loop(0, gn, pipeline, 0)
    store_group(jnp.maximum(gn - 1, 0), NARROW)

    def wide(i, _):
        load_group(i, WIDE)
        p_ref[rows_of(i), :] = product(i)
        store_group(i, WIDE)
        return 0

    lax.fori_loop(gn + 1, gn + 1 + gw, wide, 0)

    def read(b):
        return acc0_ref[:, at(b + RB)] + acc1_ref[:, at(b + RB)]

    compress(read, z_ref, src_ref, start_ref)
    add_to_masters(z_ref, oh_ref, pe_ref, w_ref, g_ref, lhs_ref)
    hanging_values(z_ref, oh_ref, pe_ref, w_ref, g_ref, lhs_ref, hq_ref)
    new_ref = outs[0] if number < 3 else ext_ref

    def finish(i, _):
        for k in range(UNROLL):
            b = i * UNROLL + k
            t = expand(b, read(b), z_ref, posr_ref, start_ref)
            r = (t - CENTRE * u_ref[:, at(b)]) * ((1.0 if number == 1 else 2.0) / HALF)
            if number > 1:
                r = r - prev_ref[:, at(b)]
            new_ref[:, at(b)] = r
        return 0

    lax.fori_loop(0, NB // UNROLL, finish, 0)
    if number < 3:
        outs[1][...] = new_ref[:, 0:RIM]
        outs[2][...] = new_ref[:, LOC - RIM :]
    else:
        me = me_ref[0]
        q = LOC // 4
        for k in range(4):
            outs[k][...] = new_ref[:, pl.ds(pl.multiple_of(((me + k) & 3) * q, L), q)]


def apply_step(number, u, gl, gr, prev, cell, base, hang, start, me):
    if number == 3:
        shapes = (sds((S, LOC // 4)),) * 4
    else:
        shapes = (sds((S, LOC)), sds((S, RIM)), sds((S, RIM)))
    return pl.pallas_call(
        functools.partial(step_kernel, number),
        out_shape=shapes,
        in_specs=[VM] * 14 + [SM] * 3,
        out_specs=(VM,) * len(shapes),
        scratch_shapes=[
            pltpu.VMEM((S, EXT), F32),
            pltpu.VMEM((S, EXT), F32),
            pltpu.VMEM((S, EXT), F32),
            pltpu.VMEM((RING * S, NPAD), F32),
            pltpu.VMEM((RING * S, NPAD), F32),
            *HANG_SCRATCH,
        ],
        compiler_params=pltpu.CompilerParams(vmem_limit_bytes=VLIM),
        name=f"step{number}",
    )(u, gl, gr, prev, *cell, *hang, base, start, me)


def gram_kernel(q0_ref, q1_ref, q2_ref, q3_ref, me_ref, gram_ref, all_ref):
    me = me_ref[0]
    for k, ref in enumerate((q0_ref, q1_ref, q2_ref, q3_ref)):
        all_ref[pl.ds(pl.multiple_of(((me - k) & 3) * S, S), S), :] = ref[...]
    a = all_ref[...]
    gram_ref[...] = lax.dot_general(a, a, NT, preferred_element_type=F32, precision=lax.Precision.HIGHEST)


def gram_of(qs, me):
    n = qs[0].shape[1]
    return pl.pallas_call(
        gram_kernel,
        out_shape=(sds((4 * S, 4 * S)), sds((4 * S, n))),
        in_specs=[VM] * 4 + [SM],
        out_specs=(VM, VM),
        compiler_params=pltpu.CompilerParams(vmem_limit_bytes=VLIM),
        name="gram",
    )(*qs, me)


def basis_kernel(total, gram_ref, all_ref, me_ref, o0_ref, o1_ref, o2_ref, o3_ref, m_ref, r_ref):
    n = 4 * S
    eye = (iota((n, n), 0) == iota((n, n), 1)).astype(F32)
    m_ref[...] = jnp.concatenate([gram_ref[...], eye], 1)
    row_id = iota((n, 2 * n), 0)

    m = m_ref[...]
    diag = jnp.zeros((n, 1), F32)
    for j in range(n):
        pivot = m[j : j + 1, :]
        d = pivot[:, j : j + 1]
        f = m[:, j : j + 1] / d
        m = m - jnp.where(row_id > j, f, 0.0) * pivot
    dg = jnp.sum(jnp.where(row_id == iota((n, 2 * n), 1), m, 0.0), axis=1, keepdims=True)
    inv = m[:, n:] * lax.rsqrt(dg) * jnp.sqrt(jnp.float32(total))
    r_ref[...] = jnp.dot(inv, all_ref[...], preferred_element_type=F32, precision=lax.Precision.HIGHEST)
    me = me_ref[0]
    for k, ref in enumerate((o0_ref, o1_ref, o2_ref, o3_ref)):
        ref[...] = r_ref[pl.ds(pl.multiple_of(((me + k) & 3) * S, S), S), :]


def basis_of(gram, rows, me, total):
    n = rows.shape[1]
    return pl.pallas_call(
        functools.partial(basis_kernel, total),
        out_shape=(sds((S, n)),) * 4,
        in_specs=[VM, VM, SM],
        out_specs=(VM,) * 4,
        scratch_shapes=[pltpu.VMEM((4 * S, 8 * S), F32), pltpu.VMEM((4 * S, n), F32)],
        compiler_params=pltpu.CompilerParams(vmem_limit_bytes=VLIM),
        name="basis",
    )(gram, rows, me)


def join_kernel(q0_ref, q1_ref, q2_ref, q3_ref, me_ref, out_ref):
    me = me_ref[0]
    n = q0_ref.shape[1]
    for k, ref in enumerate((q0_ref, q1_ref, q2_ref, q3_ref)):
        out_ref[:, pl.ds(pl.multiple_of(((me - k) & 3) * n, L), n)] = ref[...]


def join(qs, me):
    return pl.pallas_call(
        join_kernel,
        out_shape=sds((S, LOC)),
        in_specs=[VM] * 4 + [SM],
        out_specs=VM,
        compiler_params=pltpu.CompilerParams(vmem_limit_bytes=VLIM),
        name="join",
    )(*qs, me)


def shift(x, axis, by):
    size = lax.axis_size(axis)
    return lax.ppermute(x, axis, [(i, (i + by) % size) for i in range(size)])


def swap(x, axis, bits):
    size = lax.axis_size(axis)
    return lax.ppermute(x, axis, [(i, i ^ bits) for i in range(size)])


def summed(g):
    g = g + swap(g, "dom", 1)
    for axis, unit in (("dom", 2), ("dom", 8), ("band", 1)):
        others = [swap(g, axis, unit * k) for k in (1, 2, 3)]
        g = (g + others[0]) + (others[1] + others[2])
    return g


def body(
    block,
    stiffness,
    cell_scale,
    potential,
    cell_dofs,
    cell_count,
    hang_rows,
    hang_masters,
    hang_weights,
):
    dom = lax.axis_index("dom")
    inside = [lax.axis_index("band"), dom > 0, dom < lax.axis_size("dom") - 1]
    me = jnp.stack([jnp.asarray(x).astype(I32) for x in inside])
    own, hanging = pack(
        cell_dofs.T, potential.T, cell_scale, hang_rows, hang_masters, hang_weights, cell_count
    )
    from_left = shift(own, "dom", 1)
    from_right = shift(own, "dom", -1)
    *hang, start, u0, first, last = prepare(hanging, block)

    def ghosts(first, last):
        return shift(last, "dom", 1), shift(first, "dom", -1)

    gl, gr = ghosts(first, last)
    *cell, base = cell_tables(own, from_left, from_right, hang[0], me, stiffness)
    args = (cell, base, hang, start, me)
    u1, first, last = apply_step(1, u0, gl, gr, u0, *args)
    gl, gr = ghosts(first, last)
    u2, first, last = apply_step(2, u1, gl, gr, u0, *args)
    gl, gr = ghosts(first, last)
    qs = apply_step(3, u2, gl, gr, u1, *args)
    qs = [qs[0]] + [shift(qs[k], "band", k) for k in (1, 2, 3)]
    gram, rows = gram_of(qs, me)
    gram = summed(gram)
    outs = basis_of(gram, rows, me, LOC * lax.axis_size("dom"))
    outs = [outs[0]] + [shift(outs[k], "band", k) for k in (1, 2, 3)]
    return join(outs, me)


def solution(mesh):
    return jax.shard_map(
        body,
        mesh=mesh,
        in_specs=(
            P("band", "dom"),
            P(),
            P("dom"),
            P(None, "dom"),
            P(None, "dom"),
            P("dom"),
            P("dom"),
            P(None, "dom"),
            P(None, "dom"),
        ),
        out_specs=P("band", "dom"),
        check_vma=False,
    )
```

```python
import functools
import jax
import jax.numpy as jnp
from jax import lax
from jax.experimental import pallas as pl
from jax.experimental.pallas import tpu as pltpu
from jax.sharding import PartitionSpec as P

RIM = 2048
NODES = 343
HANG = 864
MASTERS = 4
LOC = 13824
CELLS = 64
S = 16
L = 128
EXT = LOC + 2 * RIM
NB = LOC // L
RB = RIM // L
NPAD = 384
NJ = NPAD // L
WIDE = 7
NARROW = 3
PACK = 72
PW = 2 * NPAD + L
GROUP = 16
RING = 4 * GROUP
SLOTS = 14 * GROUP
HPAD = 896
HB = HPAD // L
ME = MASTERS * HPAD
HE = 1024
E = ME + HE
QLO = 512
QB = QLO // L
QHI = 9
BIG = 1 << 20
CENTRE = 4.5
HALF = 3.5
F32 = jnp.float32
BF16 = jnp.bfloat16
I32 = jnp.int32
VLIM = 28 * 1024 * 1024
SMALL = 20 * 1024 * 1024
WHOLE = 64 * 1024 * 1024

VM = pl.BlockSpec(memory_space=pltpu.VMEM)
SM = pl.BlockSpec(memory_space=pltpu.SMEM)
HBM = pl.BlockSpec(memory_space=pltpu.HBM)
NT = (((1,), (1,)), ((), ()))


def inside(side):
    dom = lax.axis_index("dom")
    return dom > 0 if side == 0 else dom < lax.axis_size("dom") - 1


def iota(shape, dim):
    return lax.broadcasted_iota(I32, shape, dim)


def lanes(x, idx):
    return jnp.take_along_axis(x, idx, axis=1, mode="promise_in_bounds")


def nn(a, b):
    return jnp.dot(a, b, preferred_element_type=F32)


def nt(a, b):
    return lax.dot_general(a, b, NT, preferred_element_type=F32)


def split(x):
    hi = x.astype(BF16)
    return hi, (x - hi.astype(F32)).astype(BF16)


def at(b):
    return pl.ds(pl.multiple_of(b * L, L), L)


def one_hot(row, n):
    return (jnp.broadcast_to(row, (n, row.shape[1])) == iota((n, row.shape[1]), 0)).astype(F32)


def hang_tables(ent_ref, a_ref, b_ref, lhs_ref, oh_ref, pe_ref, src_ref, posr_ref, hq_ref, start_ref):
    for i in range(E // L):
        col = slice(i * L, (i + 1) * L)
        row = ent_ref[0:1, col]
        a_ref[:, col] = one_hot(row >> 7, L).astype(BF16)
        b_ref[:, col] = one_hot(row & 127, L).astype(BF16)
    flag = nt(a_ref[...], b_ref[...]) > 0.5
    flagb = flag.astype(F32).astype(BF16)
    tri = (iota((L, L), 0) < iota((L, L), 1)).astype(F32).astype(BF16)
    low = (iota((L, L), 1) < iota((L, L), 0)).astype(F32).astype(BF16)
    total = nn(flagb, jnp.ones((L, L), BF16))
    pos = (nn(flagb, tri) + nn(low, total.astype(BF16))).astype(I32)
    posr_ref[...] = jnp.where(flag, pos, -1)
    totrow = nt(jnp.ones((8, L), BF16), flagb)
    start_ref[...] = nn(totrow.astype(BF16), tri).astype(I32)
    ph = (pos >> 7).astype(F32).astype(BF16)
    plo = (pos & 127).astype(F32).astype(BF16)
    for i in range(E // L):
        col = slice(i * L, (i + 1) * L)
        ent = ent_ref[0:1, col]
        mask = a_ref[:, col].astype(F32)
        b = b_ref[:, col]
        hi = jnp.sum(nn(ph, b) * mask, axis=0, keepdims=True)
        lo = jnp.sum(nn(plo, b) * mask, axis=0, keepdims=True)
        pe = jnp.where(ent >= 0, hi.astype(I32) * L + lo.astype(I32), BIG)
        pe_ref[0:1, col] = pe
        oh_ref[:, col] = one_hot(pe & (QLO - 1), QLO).astype(BF16)
        qm = one_hot(pe // QLO, 16)
        lhs_ref[0:16, col] = qm.astype(BF16)
        lhs_ref[16:32, col] = (qm * (ent >> 7).astype(F32)).astype(BF16)
        lhs_ref[32:48, col] = (qm * (ent & 127).astype(F32)).astype(BF16)
        lhs_ref[48:64, col] = (qm if i >= ME // L else jnp.zeros_like(qm)).astype(BF16)
    res = nt(lhs_ref[...], oh_ref[...])
    cnt = res[0:16]
    den = jnp.maximum(cnt, 1.0)
    blk = (res[16:32] / den + 0.5).astype(I32)
    lo = (res[32:48] / den + 0.5).astype(I32)
    src = jnp.where(cnt > 0.5, blk * L + lo, -1)
    for q in range(QHI):
        for t in range(QB):
            src_ref[QB * q + t : QB * q + t + 1, :] = src[q : q + 1, t * L : (t + 1) * L]
    hq_ref[...] = res[48:64]


def zat(c):
    return pl.ds(pl.multiple_of((c // QB) * S, S), S), pl.ds(pl.multiple_of((c % QB) * L, L), L)


UNROLL = 12


def compress(read, z_ref, src_ref, start_ref):
    z_ref[...] = jnp.zeros_like(z_ref)

    def step(i, cur):
        for k in range(UNROLL):
            b = i * UNROLL + k
            y = read(b)
            c = start_ref[0, b] >> 7
            ahead = start_ref[0, b + 1] >> 7
            parts = []
            for t in range(2):
                row = jnp.broadcast_to(src_ref[pl.ds(c + t, 1), :], (S, L))
                parts.append(((row >> 7) == b, lanes(y, row & 127)))
            cur = jnp.where(parts[0][0], parts[0][1], cur)
            r, l = zat(c)
            z_ref[r, l] = cur
            after = jnp.where(parts[1][0], parts[1][1], 0.0)
            cur = jnp.where(ahead > c, after, cur)
        return cur

    cur = lax.fori_loop(0, NB // UNROLL, step, jnp.zeros((S, L), F32))
    r, l = zat(start_ref[0, NB] >> 7)
    z_ref[r, l] = cur


def expand(b, y, z_ref, posr_ref, start_ref):
    row = jnp.broadcast_to(posr_ref[pl.ds(b, 1), :], (S, L))
    c0 = start_ref[0, b] >> 7
    for t in range(2):
        c = c0 + t
        r, l = zat(c)
        y = jnp.where((row >> 7) == c, lanes(z_ref[r, l], row & 127), y)
    return y


def gather_entries(z_ref, oh_ref, pe_ref, g_ref, first, last):
    zz = jnp.concatenate(split(z_ref[...]), axis=0)
    n = QHI * S
    w = 256
    for i in range(first // w, last // w):
        col = slice(i * w, (i + 1) * w)
        g = nn(zz, oh_ref[:, col])
        q = jnp.broadcast_to(pe_ref[0:1, col] // QLO, (S, w))
        hi = g[0:S]
        lo = g[n : n + S]
        for h in range(1, QHI):
            m = q == h
            hi = jnp.where(m, g[h * S : (h + 1) * S], hi)
            lo = jnp.where(m, g[n + h * S : n + (h + 1) * S], lo)
        g_ref[:, col] = hi + lo


def scatter_entries(g_ref, oh_ref, pe_ref, lhs_ref, first, last):
    n = QHI * S
    for i in range(first // L, last // L):
        col = slice(i * L, (i + 1) * L)
        g = g_ref[:, col]
        hi = g.astype(BF16).astype(F32)
        lo = g - hi
        q = jnp.broadcast_to(pe_ref[0:1, col] // QLO, (S, L))
        for h in range(QHI):
            m = q == h
            lhs_ref[h * S : (h + 1) * S, col] = jnp.where(m, hi, 0.0).astype(BF16)
            lhs_ref[n + h * S : n + (h + 1) * S, col] = jnp.where(m, lo, 0.0).astype(BF16)
    res = nt(lhs_ref[:, first:last], oh_ref[:, first:last])
    return res[:n] + res[n:]


def hanging_values(z_ref, oh_ref, pe_ref, w_ref, g_ref, lhs_ref, hq_ref):
    gather_entries(z_ref, oh_ref, pe_ref, g_ref, 0, ME)
    g_ref[:, ME + HPAD :] = jnp.zeros((S, HE - HPAD), F32)
    for j in range(HB):
        acc = jnp.zeros((S, L), F32)
        for k in range(MASTERS):
            col = slice(k * HPAD + j * L, k * HPAD + (j + 1) * L)
            acc = acc + g_ref[:, col] * w_ref[0:1, col]
        g_ref[:, ME + j * L : ME + (j + 1) * L] = acc
    cz = scatter_entries(g_ref, oh_ref, pe_ref, lhs_ref, ME, E)
    for h in range(QHI):
        r = slice(h * S, (h + 1) * S)
        m = jnp.broadcast_to(hq_ref[h : h + 1, :], (S, QLO)) > 0.5
        z_ref[r, :] = jnp.where(m, cz[r], z_ref[r, :])


def add_to_masters(z_ref, oh_ref, pe_ref, w_ref, g_ref, lhs_ref):
    gather_entries(z_ref, oh_ref, pe_ref, g_ref, ME, E)
    for j in range(HB):
        y = g_ref[:, ME + j * L : ME + (j + 1) * L]
        for k in range(MASTERS):
            col = slice(k * HPAD + j * L, k * HPAD + (j + 1) * L)
            g_ref[:, col] = y * w_ref[0:1, col]
    z_ref[...] += scatter_entries(g_ref, oh_ref, pe_ref, lhs_ref, 0, ME)


def prepare_kernel(
    hang_ref, block_ref,
    pe_ref, w_ref, src_ref, posr_ref, hq_ref, start_ref, u_ref, left_ref, right_ref,
    ent_ref, oh_ref, a_ref, b_ref, tab_ref, z_ref, g_ref, lhs_ref, start_s, sem,
):
    for k in range(MASTERS):
        col = slice(k * HPAD, (k + 1) * HPAD)
        ent_ref[0:1, col] = hang_ref[k : k + 1, :].astype(I32)
        w_ref[0:1, col] = hang_ref[MASTERS + 1 + k : MASTERS + 2 + k, :]
    ent_ref[0:1, ME + HPAD :] = jnp.full((1, HE - HPAD), -1, I32)
    ent_ref[0:1, ME : ME + HPAD] = hang_ref[MASTERS : MASTERS + 1, :].astype(I32)
    hang_tables(ent_ref, a_ref, b_ref, tab_ref, oh_ref, pe_ref, src_ref, posr_ref, hq_ref, start_ref)
    copy = pltpu.make_async_copy(start_ref, start_s, sem)
    copy.start()
    copy.wait()
    compress(lambda b: block_ref[:, at(b)], z_ref, src_ref, start_s)
    hanging_values(z_ref, oh_ref, pe_ref, w_ref, g_ref, lhs_ref, hq_ref)

    def step(i, _):
        for k in range(UNROLL):
            b = i * UNROLL + k
            u_ref[:, at(b)] = expand(b, block_ref[:, at(b)], z_ref, posr_ref, start_s)
        return 0

    lax.fori_loop(0, NB // UNROLL, step, 0)
    left_ref[...] = u_ref[:, 0:RIM]
    right_ref[...] = u_ref[:, LOC - RIM :]


def sds(shape, dtype=F32):
    return jax.ShapeDtypeStruct(shape, dtype)


HANG_SCRATCH = [
    pltpu.VMEM((QHI * S, QLO), F32),
    pltpu.VMEM((S, E), F32),
    pltpu.VMEM((2 * QHI * S, E), BF16),
]


def prepare(hang, block):
    return pl.pallas_call(
        prepare_kernel,
        out_shape=(
            sds((1, E), I32),
            sds((1, ME)),
            sds((QB * QHI + 4, L), I32),
            sds((L, L), I32),
            sds((16, QLO)),
            sds((8, L), I32),
            sds((S, LOC)),
            sds((S, RIM)),
            sds((S, RIM)),
        ),
        in_specs=[VM] * 2,
        out_specs=(VM,) * 9,
        scratch_shapes=[
            pltpu.VMEM((1, E), I32),
            pltpu.VMEM((QLO, E), BF16),
            pltpu.VMEM((L, E), BF16),
            pltpu.VMEM((L, E), BF16),
            pltpu.VMEM((64, E), BF16),
            *HANG_SCRATCH,
            pltpu.SMEM((8, L), I32),
            pltpu.SemaphoreType.DMA,
        ],
        compiler_params=pltpu.CompilerParams(vmem_limit_bytes=VLIM),
        name="prepare",
    )(hang, block)


def pack_kernel(
    dofs_hbm, pot_hbm, scale_hbm, rows_hbm, masters_hbm, weights_hbm, count_ref,
    own_ref, hang_ref,
    dofs_ref, pot_ref, scale_ref, rows_ref, masters_ref, weights_ref, sems,
):
    moves = (
        (dofs_hbm, dofs_ref),
        (pot_hbm, pot_ref),
        (scale_hbm, scale_ref),
        (rows_hbm, rows_ref),
        (masters_hbm, masters_ref),
        (weights_hbm, weights_ref),
    )
    loads = [pltpu.make_async_copy(src, dst, sems.at[i]) for i, (src, dst) in enumerate(moves)]
    for load in loads:
        load.start()
    for load in loads:
        load.wait()
    own_ref[0:CELLS, 0:NODES] = dofs_ref[...].astype(F32)
    own_ref[0:CELLS, NPAD : NPAD + NODES] = pot_ref[...]
    scale = jnp.broadcast_to(scale_ref[...].reshape(1, CELLS), (PACK - CELLS, CELLS))
    own_ref[CELLS:PACK, 0:CELLS] = scale
    own_ref[CELLS:PACK, L : 2 * L] = jnp.full((PACK - CELLS, L), count_ref[0]).astype(F32)
    hang_ref[...] = jnp.where(iota((2 * MASTERS + 1, HPAD), 0) < MASTERS + 1, -1.0, 0.0)
    hang_ref[0:MASTERS, 0:HANG] = masters_ref[...].astype(F32)
    hang_ref[MASTERS : MASTERS + 1, 0:HANG] = rows_ref[...].reshape(1, HANG).astype(F32)
    hang_ref[MASTERS + 1 :, 0:HANG] = weights_ref[...]


def pack(dofs, pot, scale, rows, masters, weights, count):
    return pl.pallas_call(
        pack_kernel,
        out_shape=(sds((PACK, PW)), sds((2 * MASTERS + 1, HPAD))),
        in_specs=[HBM] * 6 + [SM],
        out_specs=(VM, VM),
        scratch_shapes=[
            pltpu.VMEM((CELLS, NODES), I32),
            pltpu.VMEM((CELLS, NODES), F32),
            pltpu.VMEM((CELLS,), F32),
            pltpu.VMEM((HANG,), I32),
            pltpu.VMEM((MASTERS, HANG), I32),
            pltpu.VMEM((MASTERS, HANG), F32),
            pltpu.SemaphoreType.DMA((6,)),
        ],
        compiler_params=pltpu.CompilerParams(vmem_limit_bytes=WHOLE),
        name="pack",
    )(dofs, pot, scale, rows, masters, weights, count)


def inverse(rels):
    oh = jnp.concatenate([one_hot(rel & 127, L) for rel in rels], axis=1).astype(BF16)
    rows = []
    for j, rel in enumerate(rels):
        m = jnp.broadcast_to(rel >> 7, (8, L)) == iota((8, L), 0)
        node = jnp.where(m, iota((8, L), 1) + 1, 0).astype(F32)
        zero = jnp.zeros((8, L), F32)
        rows.append(jnp.concatenate([node if i == j else zero for i in range(len(rels))], axis=1))
    return nt(jnp.concatenate(rows, axis=0).astype(BF16), oh).astype(I32) - 1


def cells_kernel(
    own_ref, left_ref, right_ref, pe_ref, k_hbm,
    tab_ref, pot_ref, kh_ref, kl_ref, oh_ref, base_ref,
    all_ref, meta_ref, k_ref, pad_ref, meta_s, list_s, wide_s, sem, sem_k,
):
    load = pltpu.make_async_copy(k_hbm, k_ref, sem_k)
    load.start()
    lane = iota((CELLS, L), 1)
    cell = iota((CELLS, L), 0)
    tail = NODES - 2 * L
    sources = ((own_ref, 0, None), (left_ref, -LOC, 0), (right_ref, LOC, 1))
    for i, (ref, shift, side) in enumerate(sources):
        r = slice(i * CELLS, (i + 1) * CELLS)
        lows, tops = [], []
        for j in range(NJ):
            dofs = ref[0:CELLS, j * L : (j + 1) * L] + float(shift)
            real = lane < (L if j < 2 else tail)
            low = jnp.where(real, dofs, float(BIG))
            all_ref[r, j * L : (j + 1) * L] = low
            pot = ref[0:CELLS, NPAD + j * L : NPAD + (j + 1) * L]
            all_ref[r, NPAD + j * L : NPAD + (j + 1) * L] = jnp.where(real, pot, 0.0)
            lows.append(jnp.min(low, axis=1, keepdims=True).astype(I32))
            tops.append(jnp.max(jnp.where(real, dofs, -float(BIG)), axis=1, keepdims=True).astype(I32))
        scales = jnp.broadcast_to(ref[CELLS : CELLS + 1, 0:L], (CELLS, L))
        scale = jnp.sum(jnp.where(lane == cell, scales, 0.0), axis=1, keepdims=True)
        all_ref[r, 2 * NPAD :] = jnp.broadcast_to(scale, (CELLS, L))
        count = jnp.broadcast_to(ref[CELLS : CELLS + 1, L : 2 * L], (CELLS, L))
        live = cell.astype(F32) < count
        if side is not None:
            live = live & jnp.full((CELLS, L), inside(side))
        low = jnp.minimum(jnp.minimum(lows[0], lows[1]), lows[2])
        top = jnp.maximum(jnp.maximum(tops[0], tops[1]), tops[2])
        used = live & (top >= RIM) & (low < RIM + LOC)
        starts = [jnp.minimum(x >> 7, EXT // L - NARROW) for x in lows]
        narrow = ((tops[0] >> 7) - starts[0] < NARROW) & ((tops[1] >> 7) - starts[1] < NARROW)
        narrow = narrow & ((tops[2] >> 7) - starts[2] < NARROW)
        base = jnp.minimum(low >> 7, EXT // L - WIDE)
        meta = jnp.where(used, jnp.where(narrow, 0, 1), -1)
        for j in range(NJ):
            meta = jnp.where(lane == 1 + j, jnp.where(narrow, starts[j], base), meta)
        meta_ref[r, :] = meta
    copy = pltpu.make_async_copy(meta_ref, meta_s, sem)
    copy.start()
    pad_ref[...] = jnp.zeros_like(pad_ref)
    load.wait()
    pad_ref[0:NODES, 0:NODES] = k_ref[...]
    kh_ref[...], kl_ref[...] = split(pad_ref[...])
    for i in range(E // L):
        col = slice(i * L, (i + 1) * L)
        oh_ref[:, col] = one_hot(pe_ref[0:1, col] & (QLO - 1), QLO).astype(BF16)
    copy.wait()

    def scan(c, counts):
        kind = meta_s[c, 0]
        n, m = counts
        list_s[n] = c
        wide_s[m] = c
        return n + jnp.where(kind == 0, 1, 0), m + jnp.where(kind == 1, 1, 0)

    n, m = lax.fori_loop(0, 3 * CELLS, scan, (0, 0), unroll=4)
    gn = (n + GROUP - 1) // GROUP
    gw = (m + GROUP - 1) // GROUP
    first = (gn + 1) * GROUP
    last = first + gw * GROUP

    def blank(i, _):
        list_s[i] = -1
        return 0

    def move(i, _):
        list_s[first + i] = wide_s[i]
        return 0

    lax.fori_loop(n, first, blank, 0)
    lax.fori_loop(0, m, move, 0)
    lax.fori_loop(first + m, last, blank, 0)
    base_ref[4 * SLOTS] = gn
    base_ref[4 * SLOTS + 1] = gw

    def one(slot):
        c = list_s[slot]
        valid = c >= 0
        c = jnp.maximum(c, 0)
        vals = all_ref[pl.ds(c, 1), :]
        rels = []
        for j in range(NJ):
            b = jnp.where(valid, meta_s[c, 1 + j], 0)
            base_ref[4 * slot + j] = b
            rel = vals[:, j * L : (j + 1) * L].astype(I32) - b * L
            rel = jnp.where(valid & (rel < WIDE * L), rel, BIG)
            rels.append(rel)
            tab_ref[slot, j : j + 1, :] = rel
            pot_ref[slot, j : j + 1, :] = vals[:, NPAD + j * L : NPAD + (j + 1) * L]
        pot_ref[slot, 3:4, :] = vals[:, 2 * NPAD :]
        inv = inverse(rels)
        for j in range(NJ):
            tab_ref[slot, 3 + 3 * j : 6 + 3 * j, :] = inv[8 * j : 8 * j + NARROW]

    def some(i, _):
        for k in range(8):
            one(i * 8 + k)
        return 0

    lax.fori_loop(0, last // 8, some, 0)


def cell_tables(own, left, right, pe, stiffness):
    return pl.pallas_call(
        cells_kernel,
        out_shape=(
            sds((SLOTS, 16, L), I32),
            sds((SLOTS, 8, L)),
            sds((NPAD, NPAD), BF16),
            sds((NPAD, NPAD), BF16),
            sds((QLO, E), BF16),
            sds((4 * SLOTS + L,), I32),
        ),
        in_specs=[VM] * 4 + [HBM],
        out_specs=(VM, VM, VM, VM, VM, SM),
        scratch_shapes=[
            pltpu.VMEM((3 * CELLS, PW), F32),
            pltpu.VMEM((3 * CELLS, L), I32),
            pltpu.VMEM((NODES, NODES), F32),
            pltpu.VMEM((NPAD, NPAD), F32),
            pltpu.SMEM((3 * CELLS, L), I32),
            pltpu.SMEM((SLOTS + GROUP,), I32),
            pltpu.SMEM((3 * CELLS + GROUP,), I32),
            pltpu.SemaphoreType.DMA,
            pltpu.SemaphoreType.DMA,
        ],
        compiler_params=pltpu.CompilerParams(vmem_limit_bytes=SMALL),
        name="cell_tables",
    )(own, left, right, pe, stiffness)


def step_kernel(number, *refs):
    (u_ref, gl_ref, gr_ref, prev_ref, tab_ref, pot_ref, kh_ref, kl_ref,
     oh_ref, pe_ref, w_ref, src_ref, posr_ref, hq_ref, base_ref, start_ref) = refs[:16]
    outs = refs[16 : 16 + (4 if number == 3 else 3)]
    ext_ref, acc0_ref, acc1_ref, x_ref, p_ref, z_ref, g_ref, lhs_ref = refs[16 + len(outs) :]
    accs = (acc0_ref, acc1_ref)
    ext_ref[:, 0:RIM] = jnp.where(inside(0), gl_ref[...], 0.0)
    ext_ref[:, RIM : RIM + LOC] = u_ref[...]
    ext_ref[:, RIM + LOC :] = jnp.where(inside(1), gr_ref[...], 0.0)
    for ref in accs:
        ref[...] = jnp.zeros_like(ref)
    gn = base_ref[4 * SLOTS]
    gw = base_ref[4 * SLOTS + 1]

    def load(slot, width):
        for j in range(NJ):
            b = base_ref[4 * slot + j]
            row = jnp.broadcast_to(tab_ref[slot, j : j + 1, :], (8, L))
            lo, hi = row & 127, row >> 7
            for s in range(2):
                r = slice(8 * s, 8 * s + 8)
                acc = lanes(ext_ref[r, at(b)], lo)
                for t in range(1, width):
                    acc = jnp.where(hi == t, lanes(ext_ref[r, at(b + t)], lo), acc)
                x_ref[pl.ds(pl.multiple_of((slot & (RING - 1)) * S + 8 * s, 8), 8), j * L : (j + 1) * L] = acc

    def store(slot, parity, width):
        acc_ref = accs[parity]
        scale = jnp.broadcast_to(pot_ref[slot, 3:4, :], (8, L))
        if width == NARROW:
            inv = [[tab_ref[slot, 3 + 3 * j + t : 4 + 3 * j + t, :] for t in range(width)] for j in range(NJ)]
        else:
            full = inverse([tab_ref[slot, j : j + 1, :] for j in range(NJ)])
            inv = [[full[8 * j + t : 8 * j + t + 1] for t in range(width)] for j in range(NJ)]
        for j in range(NJ):
            b = base_ref[4 * slot + j]
            col = slice(j * L, (j + 1) * L)
            pot = jnp.broadcast_to(pot_ref[slot, j : j + 1, :], (8, L))
            vals = []
            for s in range(2):
                r = pl.ds(pl.multiple_of((slot & (RING - 1)) * S + 8 * s, 8), 8)
                vals.append(scale * p_ref[r, col] + pot * x_ref[r, col])
            adds = []
            for t in range(width):
                row = jnp.broadcast_to(inv[j][t], (8, L))
                m, lo = row >= 0, row & 127
                adds.append([jnp.where(m, lanes(vals[s], lo), 0.0) for s in range(2)])
            olds = [[acc_ref[8 * s : 8 * s + 8, at(b + t)] for s in range(2)] for t in range(width)]
            for t in range(width):
                for s in range(2):
                    acc_ref[8 * s : 8 * s + 8, at(b + t)] = olds[t][s] + adds[t][s]

    def rows_of(i):
        return pl.ds(pl.multiple_of((i & 3) * (GROUP * S), GROUP * S), GROUP * S)

    def product(i):
        xh, xl = split(x_ref[rows_of(i), :])
        kh, kl = kh_ref[...], kl_ref[...]
        return nt(xh, kh) + (nt(xl, kh) + nt(xh, kl))

    def load_group(i, width, n):
        def some(q, _):
            for k in range(n):
                load(i * GROUP + q * n + k, width)
            return 0

        lax.fori_loop(0, GROUP // n, some, 0)

    def store_group(i, width, n):
        def some(q, _):
            for k in range(n):
                store(i * GROUP + q * n + k, k % 2, width)
            return 0

        lax.fori_loop(0, GROUP // n, some, 0)

    load_group(0, NARROW, 4)

    def pipeline(i, _):
        prod = product(i)
        before = jnp.where(i == 0, gn, i - 1)
        for k in range(GROUP):
            store(before * GROUP + k, k % 2, NARROW)
        p_ref[rows_of(i), :] = prod
        for k in range(GROUP):
            load((i + 1) * GROUP + k, NARROW)
        return 0

    lax.fori_loop(0, gn, pipeline, 0)
    store_group(jnp.maximum(gn - 1, 0), NARROW, 4)

    def wide(i, _):
        load_group(i, WIDE, 1)
        p_ref[rows_of(i), :] = product(i)
        store_group(i, WIDE, 1)
        return 0

    lax.fori_loop(gn + 1, gn + 1 + gw, wide, 0)

    def read(b):
        return acc0_ref[:, at(b + RB)] + acc1_ref[:, at(b + RB)]

    compress(read, z_ref, src_ref, start_ref)
    add_to_masters(z_ref, oh_ref, pe_ref, w_ref, g_ref, lhs_ref)
    hanging_values(z_ref, oh_ref, pe_ref, w_ref, g_ref, lhs_ref, hq_ref)
    new_ref = outs[0] if number < 3 else ext_ref

    def finish(i, _):
        for k in range(UNROLL):
            b = i * UNROLL + k
            t = expand(b, read(b), z_ref, posr_ref, start_ref)
            r = (t - CENTRE * u_ref[:, at(b)]) * ((1.0 if number == 1 else 2.0) / HALF)
            if number > 1:
                r = r - prev_ref[:, at(b)]
            new_ref[:, at(b)] = r
        return 0

    lax.fori_loop(0, NB // UNROLL, finish, 0)
    if number < 3:
        outs[1][...] = new_ref[:, 0:RIM]
        outs[2][...] = new_ref[:, LOC - RIM :]
    else:
        me = lax.axis_index("band")
        q = LOC // 4
        for k in range(4):
            outs[k][...] = new_ref[:, pl.ds(pl.multiple_of(((me + k) & 3) * q, L), q)]


def apply_step(number, u, gl, gr, prev, cell, base, hang, start):
    if number == 3:
        shapes = (sds((S, LOC // 4)),) * 4
    else:
        shapes = (sds((S, LOC)), sds((S, RIM)), sds((S, RIM)))
    return pl.pallas_call(
        functools.partial(step_kernel, number),
        out_shape=shapes,
        in_specs=[VM] * 14 + [SM] * 2,
        out_specs=(VM,) * len(shapes),
        scratch_shapes=[
            pltpu.VMEM((S, EXT), F32),
            pltpu.VMEM((S, EXT), F32),
            pltpu.VMEM((S, EXT), F32),
            pltpu.VMEM((RING * S, NPAD), F32),
            pltpu.VMEM((RING * S, NPAD), F32),
            *HANG_SCRATCH,
        ],
        compiler_params=pltpu.CompilerParams(vmem_limit_bytes=VLIM),
        name=f"step{number}",
    )(u, gl, gr, prev, *cell, *hang, base, start)


def gram_kernel(q0_ref, q1_ref, q2_ref, q3_ref, gram_ref, all_ref):
    me = lax.axis_index("band")
    for k, ref in enumerate((q0_ref, q1_ref, q2_ref, q3_ref)):
        all_ref[pl.ds(pl.multiple_of(((me - k) & 3) * S, S), S), :] = ref[...]
    a = all_ref[...]
    gram_ref[...] = lax.dot_general(a, a, NT, preferred_element_type=F32, precision=lax.Precision.HIGHEST)


def gram_of(qs):
    n = qs[0].shape[1]
    return pl.pallas_call(
        gram_kernel,
        out_shape=(sds((4 * S, 4 * S)), sds((4 * S, n))),
        in_specs=[VM] * 4,
        out_specs=(VM, VM),
        compiler_params=pltpu.CompilerParams(vmem_limit_bytes=VLIM),
        name="gram",
    )(*qs)


def basis_kernel(total, gram_ref, all_ref, o0_ref, o1_ref, o2_ref, o3_ref, m_ref, r_ref):
    n = 4 * S
    eye = (iota((n, n), 0) == iota((n, n), 1)).astype(F32)
    m_ref[...] = jnp.concatenate([gram_ref[...], eye], 1)
    row_id = iota((n, 2 * n), 0)

    m = m_ref[...]
    for j in range(n):
        pivot = m[j : j + 1, :]
        scaled = pivot * (1.0 / pivot[:, j : j + 1])
        m = m - jnp.where(row_id > j, m[:, j : j + 1], 0.0) * scaled
    dg = jnp.sum(jnp.where(row_id == iota((n, 2 * n), 1), m, 0.0), axis=1, keepdims=True)
    inv = m[:, n:] * lax.rsqrt(dg) * jnp.sqrt(jnp.float32(total))
    r_ref[...] = jnp.dot(inv, all_ref[...], preferred_element_type=F32, precision=lax.Precision.HIGHEST)
    me = lax.axis_index("band")
    for k, ref in enumerate((o0_ref, o1_ref, o2_ref, o3_ref)):
        ref[...] = r_ref[pl.ds(pl.multiple_of(((me + k) & 3) * S, S), S), :]


def basis_of(gram, rows, total):
    n = rows.shape[1]
    return pl.pallas_call(
        functools.partial(basis_kernel, total),
        out_shape=(sds((S, n)),) * 4,
        in_specs=[VM, VM],
        out_specs=(VM,) * 4,
        scratch_shapes=[pltpu.VMEM((4 * S, 8 * S), F32), pltpu.VMEM((4 * S, n), F32)],
        compiler_params=pltpu.CompilerParams(vmem_limit_bytes=VLIM),
        name="basis",
    )(gram, rows)


def join_kernel(q0_ref, q1_ref, q2_ref, q3_ref, out_ref):
    me = lax.axis_index("band")
    n = q0_ref.shape[1]
    for k, ref in enumerate((q0_ref, q1_ref, q2_ref, q3_ref)):
        out_ref[:, pl.ds(pl.multiple_of(((me - k) & 3) * n, L), n)] = ref[...]


def join(qs):
    return pl.pallas_call(
        join_kernel,
        out_shape=sds((S, LOC)),
        in_specs=[VM] * 4,
        out_specs=VM,
        compiler_params=pltpu.CompilerParams(vmem_limit_bytes=VLIM),
        name="join",
    )(*qs)


def shift(x, axis, by):
    size = lax.axis_size(axis)
    return lax.ppermute(x, axis, [(i, (i + by) % size) for i in range(size)])


def swap(x, axis, bits):
    size = lax.axis_size(axis)
    return lax.ppermute(x, axis, [(i, i ^ bits) for i in range(size)])


def summed(g):
    g = g + swap(g, "dom", 1)
    for axis, unit in (("dom", 2), ("dom", 8), ("band", 1)):
        others = [swap(g, axis, unit * k) for k in (1, 2, 3)]
        g = (g + others[0]) + (others[1] + others[2])
    return g


def body(
    block,
    stiffness,
    cell_scale,
    potential,
    cell_dofs,
    cell_count,
    hang_rows,
    hang_masters,
    hang_weights,
):
    own, hanging = pack(
        cell_dofs.T, potential.T, cell_scale, hang_rows, hang_masters, hang_weights, cell_count
    )
    from_left = shift(own, "dom", 1)
    from_right = shift(own, "dom", -1)
    *hang, start, u0, first, last = prepare(hanging, block)

    def ghosts(first, last):
        return shift(last, "dom", 1), shift(first, "dom", -1)

    gl, gr = ghosts(first, last)
    *cell, base = cell_tables(own, from_left, from_right, hang[0], stiffness)
    args = (cell, base, hang, start)
    u1, first, last = apply_step(1, u0, gl, gr, u0, *args)
    gl, gr = ghosts(first, last)
    u2, first, last = apply_step(2, u1, gl, gr, u0, *args)
    gl, gr = ghosts(first, last)
    qs = apply_step(3, u2, gl, gr, u1, *args)
    qs = [qs[0]] + [shift(qs[k], "band", k) for k in (1, 2, 3)]
    gram, rows = gram_of(qs)
    gram = summed(gram)
    outs = basis_of(gram, rows, LOC * lax.axis_size("dom"))
    outs = [outs[0]] + [shift(outs[k], "band", k) for k in (1, 2, 3)]
    return join(outs)


def solution(mesh):
    return jax.shard_map(
        body,
        mesh=mesh,
        in_specs=(
            P("band", "dom"),
            P(),
            P("dom"),
            P(None, "dom"),
            P(None, "dom"),
            P("dom"),
            P("dom"),
            P(None, "dom"),
            P(None, "dom"),
        ),
        out_specs=P("band", "dom"),
        check_vma=False,
    )
```

```python
import functools
import jax
import jax.numpy as jnp
from jax import lax
from jax.experimental import pallas as pl
from jax.experimental.pallas import tpu as pltpu
from jax.sharding import PartitionSpec as P

RIM = 2048
NODES = 343
HANG = 864
MASTERS = 4
LOC = 13824
CELLS = 64
S = 16
L = 128
EXT = LOC + 2 * RIM
NB = LOC // L
RB = RIM // L
NPAD = 384
NJ = NPAD // L
WIDE = 7
NARROW = 3
PACK = 72
PW = 2 * NPAD + L
GROUP = 8
SLOTS = 28 * GROUP
HPAD = 896
HB = HPAD // L
ME = MASTERS * HPAD
HE = 1024
E = ME + HE
QLO = 512
QB = QLO // L
QHI = 9
BIG = 1 << 20
CENTRE = 4.5
HALF = 3.5
F32 = jnp.float32
BF16 = jnp.bfloat16
I32 = jnp.int32
VLIM = 28 * 1024 * 1024
SMALL = 20 * 1024 * 1024
WHOLE = 64 * 1024 * 1024

VM = pl.BlockSpec(memory_space=pltpu.VMEM)
SM = pl.BlockSpec(memory_space=pltpu.SMEM)
HBM = pl.BlockSpec(memory_space=pltpu.HBM)
NT = (((1,), (1,)), ((), ()))


def inside(side):
    dom = lax.axis_index("dom")
    return dom > 0 if side == 0 else dom < lax.axis_size("dom") - 1


def iota(shape, dim):
    return lax.broadcasted_iota(I32, shape, dim)


def lanes(x, idx):
    return jnp.take_along_axis(x, idx, axis=1, mode="promise_in_bounds")


def nn(a, b):
    return jnp.dot(a, b, preferred_element_type=F32)


def nt(a, b):
    return lax.dot_general(a, b, NT, preferred_element_type=F32)


def split(x):
    hi = x.astype(BF16)
    return hi, (x - hi.astype(F32)).astype(BF16)


def at(b):
    return pl.ds(pl.multiple_of(b * L, L), L)


def one_hot(row, n):
    return (jnp.broadcast_to(row, (n, row.shape[1])) == iota((n, row.shape[1]), 0)).astype(F32)


def hang_tables(ent_ref, a_ref, b_ref, lhs_ref, oh_ref, pe_ref, src_ref, posr_ref, hq_ref, start_ref):
    for i in range(E // L):
        col = slice(i * L, (i + 1) * L)
        row = ent_ref[0:1, col]
        a_ref[:, col] = one_hot(row >> 7, L).astype(BF16)
        b_ref[:, col] = one_hot(row & 127, L).astype(BF16)
    flag = nt(a_ref[...], b_ref[...]) > 0.5
    flagb = flag.astype(F32).astype(BF16)
    tri = (iota((L, L), 0) < iota((L, L), 1)).astype(F32).astype(BF16)
    low = (iota((L, L), 1) < iota((L, L), 0)).astype(F32).astype(BF16)
    total = nn(flagb, jnp.ones((L, L), BF16))
    pos = (nn(flagb, tri) + nn(low, total.astype(BF16))).astype(I32)
    posr_ref[...] = jnp.where(flag, pos, -1)
    totrow = nt(jnp.ones((8, L), BF16), flagb)
    start_ref[...] = nn(totrow.astype(BF16), tri).astype(I32)
    ph = (pos >> 7).astype(F32).astype(BF16)
    plo = (pos & 127).astype(F32).astype(BF16)
    for i in range(E // L):
        col = slice(i * L, (i + 1) * L)
        ent = ent_ref[0:1, col]
        mask = a_ref[:, col].astype(F32)
        b = b_ref[:, col]
        hi = jnp.sum(nn(ph, b) * mask, axis=0, keepdims=True)
        lo = jnp.sum(nn(plo, b) * mask, axis=0, keepdims=True)
        pe = jnp.where(ent >= 0, hi.astype(I32) * L + lo.astype(I32), BIG)
        pe_ref[0:1, col] = pe
        oh_ref[:, col] = one_hot(pe & (QLO - 1), QLO).astype(BF16)
        qm = one_hot(pe // QLO, 16)
        lhs_ref[0:16, col] = qm.astype(BF16)
        lhs_ref[16:32, col] = (qm * (ent >> 7).astype(F32)).astype(BF16)
        lhs_ref[32:48, col] = (qm * (ent & 127).astype(F32)).astype(BF16)
        lhs_ref[48:64, col] = (qm if i >= ME // L else jnp.zeros_like(qm)).astype(BF16)
    res = nt(lhs_ref[...], oh_ref[...])
    cnt = res[0:16]
    den = jnp.maximum(cnt, 1.0)
    blk = (res[16:32] / den + 0.5).astype(I32)
    lo = (res[32:48] / den + 0.5).astype(I32)
    src = jnp.where(cnt > 0.5, blk * L + lo, -1)
    for q in range(QHI):
        for t in range(QB):
            src_ref[QB * q + t : QB * q + t + 1, :] = src[q : q + 1, t * L : (t + 1) * L]
    hq_ref[...] = res[48:64]


def zat(c):
    return pl.ds(pl.multiple_of((c // QB) * S, S), S), pl.ds(pl.multiple_of((c % QB) * L, L), L)


UNROLL = 12


def compress(read, z_ref, src_ref, start_ref):
    z_ref[...] = jnp.zeros_like(z_ref)

    def step(i, cur):
        for k in range(UNROLL):
            b = i * UNROLL + k
            y = read(b)
            c = start_ref[0, b] >> 7
            ahead = start_ref[0, b + 1] >> 7
            parts = []
            for t in range(2):
                row = jnp.broadcast_to(src_ref[pl.ds(c + t, 1), :], (S, L))
                parts.append(((row >> 7) == b, lanes(y, row & 127)))
            cur = jnp.where(parts[0][0], parts[0][1], cur)
            r, l = zat(c)
            z_ref[r, l] = cur
            after = jnp.where(parts[1][0], parts[1][1], 0.0)
            cur = jnp.where(ahead > c, after, cur)
        return cur

    cur = lax.fori_loop(0, NB // UNROLL, step, jnp.zeros((S, L), F32))
    r, l = zat(start_ref[0, NB] >> 7)
    z_ref[r, l] = cur


def expand(b, y, z_ref, posr_ref, start_ref):
    row = jnp.broadcast_to(posr_ref[pl.ds(b, 1), :], (S, L))
    c0 = start_ref[0, b] >> 7
    for t in range(2):
        c = c0 + t
        r, l = zat(c)
        y = jnp.where((row >> 7) == c, lanes(z_ref[r, l], row & 127), y)
    return y


def gather_entries(z_ref, oh_ref, pe_ref, g_ref, first, last):
    zz = jnp.concatenate(split(z_ref[...]), axis=0)
    n = QHI * S
    w = 256
    for i in range(first // w, last // w):
        col = slice(i * w, (i + 1) * w)
        g = nn(zz, oh_ref[:, col])
        q = jnp.broadcast_to(pe_ref[0:1, col] // QLO, (S, w))
        hi = g[0:S]
        lo = g[n : n + S]
        for h in range(1, QHI):
            m = q == h
            hi = jnp.where(m, g[h * S : (h + 1) * S], hi)
            lo = jnp.where(m, g[n + h * S : n + (h + 1) * S], lo)
        g_ref[:, col] = hi + lo


def scatter_entries(g_ref, oh_ref, pe_ref, lhs_ref, first, last):
    n = QHI * S
    for i in range(first // L, last // L):
        col = slice(i * L, (i + 1) * L)
        g = g_ref[:, col]
        hi = g.astype(BF16).astype(F32)
        lo = g - hi
        q = jnp.broadcast_to(pe_ref[0:1, col] // QLO, (S, L))
        for h in range(QHI):
            m = q == h
            lhs_ref[h * S : (h + 1) * S, col] = jnp.where(m, hi, 0.0).astype(BF16)
            lhs_ref[n + h * S : n + (h + 1) * S, col] = jnp.where(m, lo, 0.0).astype(BF16)
    res = nt(lhs_ref[:, first:last], oh_ref[:, first:last])
    return res[:n] + res[n:]


def hanging_values(z_ref, oh_ref, pe_ref, w_ref, g_ref, lhs_ref, hq_ref):
    gather_entries(z_ref, oh_ref, pe_ref, g_ref, 0, ME)
    g_ref[:, ME + HPAD :] = jnp.zeros((S, HE - HPAD), F32)
    for j in range(HB):
        acc = jnp.zeros((S, L), F32)
        for k in range(MASTERS):
            col = slice(k * HPAD + j * L, k * HPAD + (j + 1) * L)
            acc = acc + g_ref[:, col] * w_ref[0:1, col]
        g_ref[:, ME + j * L : ME + (j + 1) * L] = acc
    cz = scatter_entries(g_ref, oh_ref, pe_ref, lhs_ref, ME, E)
    for h in range(QHI):
        r = slice(h * S, (h + 1) * S)
        m = jnp.broadcast_to(hq_ref[h : h + 1, :], (S, QLO)) > 0.5
        z_ref[r, :] = jnp.where(m, cz[r], z_ref[r, :])


def add_to_masters(z_ref, oh_ref, pe_ref, w_ref, g_ref, lhs_ref):
    gather_entries(z_ref, oh_ref, pe_ref, g_ref, ME, E)
    for j in range(HB):
        y = g_ref[:, ME + j * L : ME + (j + 1) * L]
        for k in range(MASTERS):
            col = slice(k * HPAD + j * L, k * HPAD + (j + 1) * L)
            g_ref[:, col] = y * w_ref[0:1, col]
    z_ref[...] += scatter_entries(g_ref, oh_ref, pe_ref, lhs_ref, 0, ME)


def prepare_kernel(
    hang_ref, block_ref,
    pe_ref, w_ref, src_ref, posr_ref, hq_ref, start_ref, u_ref, left_ref, right_ref,
    ent_ref, oh_ref, a_ref, b_ref, tab_ref, z_ref, g_ref, lhs_ref, start_s, sem,
):
    for k in range(MASTERS):
        col = slice(k * HPAD, (k + 1) * HPAD)
        ent_ref[0:1, col] = hang_ref[k : k + 1, :].astype(I32)
        w_ref[0:1, col] = hang_ref[MASTERS + 1 + k : MASTERS + 2 + k, :]
    ent_ref[0:1, ME + HPAD :] = jnp.full((1, HE - HPAD), -1, I32)
    ent_ref[0:1, ME : ME + HPAD] = hang_ref[MASTERS : MASTERS + 1, :].astype(I32)
    hang_tables(ent_ref, a_ref, b_ref, tab_ref, oh_ref, pe_ref, src_ref, posr_ref, hq_ref, start_ref)
    copy = pltpu.make_async_copy(start_ref, start_s, sem)
    copy.start()
    copy.wait()
    compress(lambda b: block_ref[:, at(b)], z_ref, src_ref, start_s)
    hanging_values(z_ref, oh_ref, pe_ref, w_ref, g_ref, lhs_ref, hq_ref)

    def step(i, _):
        for k in range(UNROLL):
            b = i * UNROLL + k
            u_ref[:, at(b)] = expand(b, block_ref[:, at(b)], z_ref, posr_ref, start_s)
        return 0

    lax.fori_loop(0, NB // UNROLL, step, 0)
    left_ref[...] = u_ref[:, 0:RIM]
    right_ref[...] = u_ref[:, LOC - RIM :]


def sds(shape, dtype=F32):
    return jax.ShapeDtypeStruct(shape, dtype)


HANG_SCRATCH = [
    pltpu.VMEM((QHI * S, QLO), F32),
    pltpu.VMEM((S, E), F32),
    pltpu.VMEM((2 * QHI * S, E), BF16),
]


def prepare(hang, block):
    return pl.pallas_call(
        prepare_kernel,
        out_shape=(
            sds((1, E), I32),
            sds((1, ME)),
            sds((QB * QHI + 4, L), I32),
            sds((L, L), I32),
            sds((16, QLO)),
            sds((8, L), I32),
            sds((S, LOC)),
            sds((S, RIM)),
            sds((S, RIM)),
        ),
        in_specs=[VM] * 2,
        out_specs=(VM,) * 9,
        scratch_shapes=[
            pltpu.VMEM((1, E), I32),
            pltpu.VMEM((QLO, E), BF16),
            pltpu.VMEM((L, E), BF16),
            pltpu.VMEM((L, E), BF16),
            pltpu.VMEM((64, E), BF16),
            *HANG_SCRATCH,
            pltpu.SMEM((8, L), I32),
            pltpu.SemaphoreType.DMA,
        ],
        compiler_params=pltpu.CompilerParams(vmem_limit_bytes=VLIM),
        name="prepare",
    )(hang, block)


def pack_kernel(
    dofs_hbm, pot_hbm, scale_hbm, rows_hbm, masters_hbm, weights_hbm, count_ref,
    own_ref, hang_ref,
    dofs_ref, pot_ref, scale_ref, rows_ref, masters_ref, weights_ref, sems,
):
    moves = (
        (dofs_hbm, dofs_ref),
        (pot_hbm, pot_ref),
        (scale_hbm, scale_ref),
        (rows_hbm, rows_ref),
        (masters_hbm, masters_ref),
        (weights_hbm, weights_ref),
    )
    loads = [pltpu.make_async_copy(src, dst, sems.at[i]) for i, (src, dst) in enumerate(moves)]
    for load in loads:
        load.start()
    for load in loads:
        load.wait()
    own_ref[0:CELLS, 0:NODES] = dofs_ref[...].astype(F32)
    own_ref[0:CELLS, NPAD : NPAD + NODES] = pot_ref[...]
    scale = jnp.broadcast_to(scale_ref[...].reshape(1, CELLS), (PACK - CELLS, CELLS))
    own_ref[CELLS:PACK, 0:CELLS] = scale
    own_ref[CELLS:PACK, L : 2 * L] = jnp.full((PACK - CELLS, L), count_ref[0]).astype(F32)
    hang_ref[...] = jnp.where(iota((2 * MASTERS + 1, HPAD), 0) < MASTERS + 1, -1.0, 0.0)
    hang_ref[0:MASTERS, 0:HANG] = masters_ref[...].astype(F32)
    hang_ref[MASTERS : MASTERS + 1, 0:HANG] = rows_ref[...].reshape(1, HANG).astype(F32)
    hang_ref[MASTERS + 1 :, 0:HANG] = weights_ref[...]


def pack(dofs, pot, scale, rows, masters, weights, count):
    return pl.pallas_call(
        pack_kernel,
        out_shape=(sds((PACK, PW)), sds((2 * MASTERS + 1, HPAD))),
        in_specs=[HBM] * 6 + [SM],
        out_specs=(VM, VM),
        scratch_shapes=[
            pltpu.VMEM((CELLS, NODES), I32),
            pltpu.VMEM((CELLS, NODES), F32),
            pltpu.VMEM((CELLS,), F32),
            pltpu.VMEM((HANG,), I32),
            pltpu.VMEM((MASTERS, HANG), I32),
            pltpu.VMEM((MASTERS, HANG), F32),
            pltpu.SemaphoreType.DMA((6,)),
        ],
        compiler_params=pltpu.CompilerParams(vmem_limit_bytes=WHOLE),
        name="pack",
    )(dofs, pot, scale, rows, masters, weights, count)


def inverse(rels):
    oh = jnp.concatenate([one_hot(rel & 127, L) for rel in rels], axis=1).astype(BF16)
    rows = []
    for j, rel in enumerate(rels):
        m = jnp.broadcast_to(rel >> 7, (8, L)) == iota((8, L), 0)
        node = jnp.where(m, iota((8, L), 1) + 1, 0).astype(F32)
        zero = jnp.zeros((8, L), F32)
        rows.append(jnp.concatenate([node if i == j else zero for i in range(len(rels))], axis=1))
    return nt(jnp.concatenate(rows, axis=0).astype(BF16), oh).astype(I32) - 1


def cells_kernel(
    own_ref, left_ref, right_ref, pe_ref, k_hbm,
    tab_ref, pot_ref, kh_ref, kl_ref, oh_ref, base_ref,
    all_ref, meta_ref, k_ref, pad_ref, meta_s, list_s, wide_s, sem, sem_k,
):
    load = pltpu.make_async_copy(k_hbm, k_ref, sem_k)
    load.start()
    lane = iota((CELLS, L), 1)
    cell = iota((CELLS, L), 0)
    tail = NODES - 2 * L
    sources = ((own_ref, 0, None), (left_ref, -LOC, 0), (right_ref, LOC, 1))
    for i, (ref, shift, side) in enumerate(sources):
        r = slice(i * CELLS, (i + 1) * CELLS)
        lows, tops = [], []
        for j in range(NJ):
            dofs = ref[0:CELLS, j * L : (j + 1) * L] + float(shift)
            real = lane < (L if j < 2 else tail)
            low = jnp.where(real, dofs, float(BIG))
            all_ref[r, j * L : (j + 1) * L] = low
            pot = ref[0:CELLS, NPAD + j * L : NPAD + (j + 1) * L]
            all_ref[r, NPAD + j * L : NPAD + (j + 1) * L] = jnp.where(real, pot, 0.0)
            lows.append(jnp.min(low, axis=1, keepdims=True).astype(I32))
            tops.append(jnp.max(jnp.where(real, dofs, -float(BIG)), axis=1, keepdims=True).astype(I32))
        scales = jnp.broadcast_to(ref[CELLS : CELLS + 1, 0:L], (CELLS, L))
        scale = jnp.sum(jnp.where(lane == cell, scales, 0.0), axis=1, keepdims=True)
        all_ref[r, 2 * NPAD :] = jnp.broadcast_to(scale, (CELLS, L))
        count = jnp.broadcast_to(ref[CELLS : CELLS + 1, L : 2 * L], (CELLS, L))
        live = cell.astype(F32) < count
        if side is not None:
            live = live & jnp.full((CELLS, L), inside(side))
        low = jnp.minimum(jnp.minimum(lows[0], lows[1]), lows[2])
        top = jnp.maximum(jnp.maximum(tops[0], tops[1]), tops[2])
        used = live & (top >= RIM) & (low < RIM + LOC)
        starts = [jnp.minimum(x >> 7, EXT // L - NARROW) for x in lows]
        narrow = ((tops[0] >> 7) - starts[0] < NARROW) & ((tops[1] >> 7) - starts[1] < NARROW)
        narrow = narrow & ((tops[2] >> 7) - starts[2] < NARROW)
        base = jnp.minimum(low >> 7, EXT // L - WIDE)
        meta = jnp.where(used, jnp.where(narrow, 0, 1), -1)
        for j in range(NJ):
            meta = jnp.where(lane == 1 + j, jnp.where(narrow, starts[j], base), meta)
        meta_ref[r, :] = meta
    copy = pltpu.make_async_copy(meta_ref, meta_s, sem)
    copy.start()
    pad_ref[...] = jnp.zeros_like(pad_ref)
    load.wait()
    pad_ref[0:NODES, 0:NODES] = k_ref[...]
    kh_ref[...], kl_ref[...] = split(pad_ref[...].T)
    for i in range(E // L):
        col = slice(i * L, (i + 1) * L)
        oh_ref[:, col] = one_hot(pe_ref[0:1, col] & (QLO - 1), QLO).astype(BF16)
    copy.wait()

    def scan(c, counts):
        kind = meta_s[c, 0]
        n, m = counts
        list_s[n] = c
        wide_s[m] = c
        return n + jnp.where(kind == 0, 1, 0), m + jnp.where(kind == 1, 1, 0)

    n, m = lax.fori_loop(0, 3 * CELLS, scan, (0, 0), unroll=4)
    gn = 2 * ((n + 2 * GROUP - 1) // (2 * GROUP))
    gw = (m + GROUP - 1) // GROUP
    first = (gn + 1) * GROUP
    last = first + gw * GROUP

    def blank(i, _):
        list_s[i] = -1
        return 0

    def move(i, _):
        list_s[first + i] = wide_s[i]
        return 0

    lax.fori_loop(n, first, blank, 0)
    lax.fori_loop(0, m, move, 0)
    lax.fori_loop(first + m, last, blank, 0)
    base_ref[4 * SLOTS] = gn
    base_ref[4 * SLOTS + 1] = gw

    def one(slot):
        c = list_s[slot]
        valid = c >= 0
        c = jnp.maximum(c, 0)
        vals = all_ref[pl.ds(c, 1), :]
        rels = []
        for j in range(NJ):
            b = jnp.where(valid, meta_s[c, 1 + j], 0)
            base_ref[4 * slot + j] = b
            rel = vals[:, j * L : (j + 1) * L].astype(I32) - b * L
            rel = jnp.where(valid & (rel < WIDE * L), rel, BIG)
            rels.append(rel)
            tab_ref[slot, j : j + 1, :] = rel
            pot_ref[slot, j : j + 1, :] = vals[:, NPAD + j * L : NPAD + (j + 1) * L]
        pot_ref[slot, 3:4, :] = vals[:, 2 * NPAD :]
        inv = inverse(rels)
        for j in range(NJ):
            tab_ref[slot, 3 + 3 * j : 6 + 3 * j, :] = inv[8 * j : 8 * j + NARROW]

    def some(i, _):
        for k in range(8):
            one(i * 8 + k)
        return 0

    lax.fori_loop(0, last // 8, some, 0)


def cell_tables(own, left, right, pe, stiffness):
    return pl.pallas_call(
        cells_kernel,
        out_shape=(
            sds((SLOTS, 16, L), I32),
            sds((SLOTS, 8, L)),
            sds((NPAD, NPAD), BF16),
            sds((NPAD, NPAD), BF16),
            sds((QLO, E), BF16),
            sds((4 * SLOTS + L,), I32),
        ),
        in_specs=[VM] * 4 + [HBM],
        out_specs=(VM, VM, VM, VM, VM, SM),
        scratch_shapes=[
            pltpu.VMEM((3 * CELLS, PW), F32),
            pltpu.VMEM((3 * CELLS, L), I32),
            pltpu.VMEM((NODES, NODES), F32),
            pltpu.VMEM((NPAD, NPAD), F32),
            pltpu.SMEM((3 * CELLS, L), I32),
            pltpu.SMEM((SLOTS + GROUP,), I32),
            pltpu.SMEM((3 * CELLS + GROUP,), I32),
            pltpu.SemaphoreType.DMA,
            pltpu.SemaphoreType.DMA,
        ],
        compiler_params=pltpu.CompilerParams(vmem_limit_bytes=SMALL),
        name="cell_tables",
    )(own, left, right, pe, stiffness)


def step_kernel(number, *refs):
    (u_ref, gl_ref, gr_ref, prev_ref, tab_ref, pot_ref, kh_ref, kl_ref,
     oh_ref, pe_ref, w_ref, src_ref, posr_ref, hq_ref, base_ref, start_ref) = refs[:16]
    outs = refs[16 : 16 + (4 if number == 3 else 3)]
    ext_ref, acc0_ref, acc1_ref, x0_ref, x1_ref, p0_ref, p1_ref, z_ref, g_ref, lhs_ref = refs[16 + len(outs) :]
    accs = (acc0_ref, acc1_ref)
    ext_ref[:, 0:RIM] = jnp.where(inside(0), gl_ref[...], 0.0)
    ext_ref[:, RIM : RIM + LOC] = u_ref[...]
    ext_ref[:, RIM + LOC :] = jnp.where(inside(1), gr_ref[...], 0.0)
    for ref in accs:
        ref[...] = jnp.zeros_like(ref)
    gn = base_ref[4 * SLOTS]
    gw = base_ref[4 * SLOTS + 1]

    def rows8(k, s):
        return pl.ds(k * S + 8 * s, 8) if isinstance(k, int) else pl.ds(pl.multiple_of(k * S + 8 * s, 8), 8)

    def load(x_ref, group, k, width):
        slot = group * GROUP + k
        for j in range(NJ):
            b = base_ref[4 * slot + j]
            row = jnp.broadcast_to(tab_ref[slot, j : j + 1, :], (8, L))
            lo, hi = row & 127, row >> 7
            for s in range(2):
                r = slice(8 * s, 8 * s + 8)
                acc = lanes(ext_ref[r, at(b)], lo)
                for t in range(1, width):
                    acc = jnp.where(hi == t, lanes(ext_ref[r, at(b + t)], lo), acc)
                x_ref[rows8(k, s), j * L : (j + 1) * L] = acc

    def store(p_ref, group, k, width):
        slot = group * GROUP + k
        acc_ref = accs[k % 2 if isinstance(k, int) else 0]
        if width == NARROW:
            inv = [[tab_ref[slot, 3 + 3 * j + t : 4 + 3 * j + t, :] for t in range(width)] for j in range(NJ)]
        else:
            full = inverse([tab_ref[slot, j : j + 1, :] for j in range(NJ)])
            inv = [[full[8 * j + t : 8 * j + t + 1] for t in range(width)] for j in range(NJ)]
        for j in range(NJ):
            b = base_ref[4 * slot + j]
            vals = [p_ref[rows8(k, s), j * L : (j + 1) * L] for s in range(2)]
            adds = []
            for t in range(width):
                row = jnp.broadcast_to(inv[j][t], (8, L))
                m, lo = row >= 0, row & 127
                adds.append([jnp.where(m, lanes(vals[s], lo), 0.0) for s in range(2)])
            olds = [[acc_ref[8 * s : 8 * s + 8, at(b + t)] for s in range(2)] for t in range(width)]
            for t in range(width):
                for s in range(2):
                    acc_ref[8 * s : 8 * s + 8, at(b + t)] = olds[t][s] + adds[t][s]

    def product(x_ref, p_ref, group):
        n = GROUP * S
        x = x_ref[...]
        xh, xl = split(x)
        both = nn(jnp.concatenate([xh, xl], 0), kh_ref[...])
        prod = both[:n] + (both[n:] + nn(xh, kl_ref[...]))
        for k in range(GROUP):
            slot = group * GROUP + k
            r = slice(k * S, (k + 1) * S)
            scale = jnp.broadcast_to(pot_ref[slot, 3:4, :], (S, L))
            for j in range(NJ):
                col = slice(j * L, (j + 1) * L)
                pot = jnp.broadcast_to(pot_ref[slot, j : j + 1, :], (S, L))
                p_ref[r, col] = scale * prod[r, col] + pot * x[r, col]

    def load_group(x_ref, group, width, n):
        def some(q, _):
            for k in range(n):
                load(x_ref, group, q * n + k, width)
            return 0

        lax.fori_loop(0, GROUP // n, some, 0)

    load_group(x0_ref, 0, NARROW, 4)

    def pipeline(i, _):
        g = 2 * i
        product(x0_ref, p0_ref, g)
        before = jnp.where(i == 0, gn, g - 1)
        for k in range(GROUP):
            store(p1_ref, before, k, NARROW)
            load(x1_ref, g + 1, k, NARROW)
        product(x1_ref, p1_ref, g + 1)
        for k in range(GROUP):
            store(p0_ref, g, k, NARROW)
            load(x0_ref, g + 2, k, NARROW)
        return 0

    lax.fori_loop(0, gn // 2, pipeline, 0)
    for k in range(GROUP):
        store(p1_ref, jnp.where(gn > 0, gn - 1, gn), k, NARROW)

    def wide(i, _):
        load_group(x0_ref, i, WIDE, 1)
        product(x0_ref, p0_ref, i)

        def one(k, _):
            store(p0_ref, i, k, WIDE)
            return 0

        lax.fori_loop(0, GROUP, one, 0)
        return 0

    lax.fori_loop(gn + 1, gn + 1 + gw, wide, 0)

    def read(b):
        return acc0_ref[:, at(b + RB)] + acc1_ref[:, at(b + RB)]

    compress(read, z_ref, src_ref, start_ref)
    add_to_masters(z_ref, oh_ref, pe_ref, w_ref, g_ref, lhs_ref)
    hanging_values(z_ref, oh_ref, pe_ref, w_ref, g_ref, lhs_ref, hq_ref)
    new_ref = outs[0] if number < 3 else ext_ref

    def finish(i, _):
        for k in range(UNROLL):
            b = i * UNROLL + k
            t = expand(b, read(b), z_ref, posr_ref, start_ref)
            r = (t - CENTRE * u_ref[:, at(b)]) * ((1.0 if number == 1 else 2.0) / HALF)
            if number > 1:
                r = r - prev_ref[:, at(b)]
            new_ref[:, at(b)] = r
        return 0

    lax.fori_loop(0, NB // UNROLL, finish, 0)
    if number < 3:
        outs[1][...] = new_ref[:, 0:RIM]
        outs[2][...] = new_ref[:, LOC - RIM :]
    else:
        me = lax.axis_index("band")
        q = LOC // 4
        for k in range(4):
            outs[k][...] = new_ref[:, pl.ds(pl.multiple_of(((me + k) & 3) * q, L), q)]


def apply_step(number, u, gl, gr, prev, cell, base, hang, start):
    if number == 3:
        shapes = (sds((S, LOC // 4)),) * 4
    else:
        shapes = (sds((S, LOC)), sds((S, RIM)), sds((S, RIM)))
    return pl.pallas_call(
        functools.partial(step_kernel, number),
        out_shape=shapes,
        in_specs=[VM] * 14 + [SM] * 2,
        out_specs=(VM,) * len(shapes),
        scratch_shapes=[
            pltpu.VMEM((S, EXT), F32),
            pltpu.VMEM((S, EXT), F32),
            pltpu.VMEM((S, EXT), F32),
            *[pltpu.VMEM((GROUP * S, NPAD), F32)] * 4,
            *HANG_SCRATCH,
        ],
        compiler_params=pltpu.CompilerParams(vmem_limit_bytes=VLIM),
        name=f"step{number}",
    )(u, gl, gr, prev, *cell, *hang, base, start)


def gram_kernel(q0_ref, q1_ref, q2_ref, q3_ref, gram_ref, all_ref):
    me = lax.axis_index("band")
    for k, ref in enumerate((q0_ref, q1_ref, q2_ref, q3_ref)):
        all_ref[pl.ds(pl.multiple_of(((me - k) & 3) * S, S), S), :] = ref[...]
    a = all_ref[...]
    gram_ref[...] = lax.dot_general(a, a, NT, preferred_element_type=F32, precision=lax.Precision.HIGHEST)


def gram_of(qs):
    n = qs[0].shape[1]
    return pl.pallas_call(
        gram_kernel,
        out_shape=(sds((4 * S, 4 * S)), sds((4 * S, n))),
        in_specs=[VM] * 4,
        out_specs=(VM, VM),
        compiler_params=pltpu.CompilerParams(vmem_limit_bytes=VLIM),
        name="gram",
    )(*qs)


def basis_kernel(total, gram_ref, all_ref, o0_ref, o1_ref, o2_ref, o3_ref, m_ref, r_ref):
    n = 4 * S
    eye = (iota((n, n), 0) == iota((n, n), 1)).astype(F32)
    m_ref[...] = jnp.concatenate([gram_ref[...], eye], 1)
    row_id = iota((n, 2 * n), 0)

    m = m_ref[...]
    for j in range(n):
        pivot = m[j : j + 1, :]
        scaled = pivot * (1.0 / pivot[:, j : j + 1])
        m = m - jnp.where(row_id > j, m[:, j : j + 1], 0.0) * scaled
    dg = jnp.sum(jnp.where(row_id == iota((n, 2 * n), 1), m, 0.0), axis=1, keepdims=True)
    inv = m[:, n:] * lax.rsqrt(dg) * jnp.sqrt(jnp.float32(total))
    r_ref[...] = jnp.dot(inv, all_ref[...], preferred_element_type=F32, precision=lax.Precision.HIGHEST)
    me = lax.axis_index("band")
    for k, ref in enumerate((o0_ref, o1_ref, o2_ref, o3_ref)):
        ref[...] = r_ref[pl.ds(pl.multiple_of(((me + k) & 3) * S, S), S), :]


def basis_of(gram, rows, total):
    n = rows.shape[1]
    return pl.pallas_call(
        functools.partial(basis_kernel, total),
        out_shape=(sds((S, n)),) * 4,
        in_specs=[VM, VM],
        out_specs=(VM,) * 4,
        scratch_shapes=[pltpu.VMEM((4 * S, 8 * S), F32), pltpu.VMEM((4 * S, n), F32)],
        compiler_params=pltpu.CompilerParams(vmem_limit_bytes=VLIM),
        name="basis",
    )(gram, rows)


def join_kernel(q0_ref, q1_ref, q2_ref, q3_ref, out_ref):
    me = lax.axis_index("band")
    n = q0_ref.shape[1]
    for k, ref in enumerate((q0_ref, q1_ref, q2_ref, q3_ref)):
        out_ref[:, pl.ds(pl.multiple_of(((me - k) & 3) * n, L), n)] = ref[...]


def join(qs):
    return pl.pallas_call(
        join_kernel,
        out_shape=sds((S, LOC)),
        in_specs=[VM] * 4,
        out_specs=VM,
        compiler_params=pltpu.CompilerParams(vmem_limit_bytes=VLIM),
        name="join",
    )(*qs)


def shift(x, axis, by):
    size = lax.axis_size(axis)
    return lax.ppermute(x, axis, [(i, (i + by) % size) for i in range(size)])


def swap(x, axis, bits):
    size = lax.axis_size(axis)
    return lax.ppermute(x, axis, [(i, i ^ bits) for i in range(size)])


def summed(g):
    g = g + swap(g, "dom", 1)
    for axis, unit in (("dom", 2), ("dom", 8), ("band", 1)):
        others = [swap(g, axis, unit * k) for k in (1, 2, 3)]
        g = (g + others[0]) + (others[1] + others[2])
    return g


def body(
    block,
    stiffness,
    cell_scale,
    potential,
    cell_dofs,
    cell_count,
    hang_rows,
    hang_masters,
    hang_weights,
):
    own, hanging = pack(
        cell_dofs.T, potential.T, cell_scale, hang_rows, hang_masters, hang_weights, cell_count
    )
    from_left = shift(own, "dom", 1)
    from_right = shift(own, "dom", -1)
    *hang, start, u0, first, last = prepare(hanging, block)

    def ghosts(first, last):
        return shift(last, "dom", 1), shift(first, "dom", -1)

    gl, gr = ghosts(first, last)
    *cell, base = cell_tables(own, from_left, from_right, hang[0], stiffness)
    args = (cell, base, hang, start)
    u1, first, last = apply_step(1, u0, gl, gr, u0, *args)
    gl, gr = ghosts(first, last)
    u2, first, last = apply_step(2, u1, gl, gr, u0, *args)
    gl, gr = ghosts(first, last)
    qs = apply_step(3, u2, gl, gr, u1, *args)
    qs = [qs[0]] + [shift(qs[k], "band", k) for k in (1, 2, 3)]
    gram, rows = gram_of(qs)
    gram = summed(gram)
    outs = basis_of(gram, rows, LOC * lax.axis_size("dom"))
    outs = [outs[0]] + [shift(outs[k], "band", k) for k in (1, 2, 3)]
    return join(outs)


def solution(mesh):
    return jax.shard_map(
        body,
        mesh=mesh,
        in_specs=(
            P("band", "dom"),
            P(),
            P("dom"),
            P(None, "dom"),
            P(None, "dom"),
            P("dom"),
            P("dom"),
            P(None, "dom"),
            P(None, "dom"),
        ),
        out_specs=P("band", "dom"),
        check_vma=False,
    )
```

```python
import functools
import jax
import jax.numpy as jnp
from jax import lax
from jax.experimental import pallas as pl
from jax.experimental.pallas import tpu as pltpu
from jax.sharding import PartitionSpec as P

RIM = 2048
EDGE = 768
NODES = 343
HANG = 864
MASTERS = 4
LOC = 13824
CELLS = 64
S = 16
L = 128
EXT = LOC + 2 * RIM
NB = LOC // L
RB = RIM // L
NPAD = 384
NJ = NPAD // L
WIDE = 7
NARROW = 3
PACK = 72
PW = 2 * NPAD + L
GROUP = 8
SLOTS = 28 * GROUP
HPAD = 896
HB = HPAD // L
ME = MASTERS * HPAD
HE = 1024
E = ME + HE
QLO = 512
QB = QLO // L
QHI = 9
BIG = 1 << 20
CENTRE = 4.5
HALF = 3.5
F32 = jnp.float32
BF16 = jnp.bfloat16
I32 = jnp.int32
VLIM = 28 * 1024 * 1024
SMALL = 20 * 1024 * 1024
WHOLE = 64 * 1024 * 1024

VM = pl.BlockSpec(memory_space=pltpu.VMEM)
SM = pl.BlockSpec(memory_space=pltpu.SMEM)
HBM = pl.BlockSpec(memory_space=pltpu.HBM)
NT = (((1,), (1,)), ((), ()))


def inside(side):
    dom = lax.axis_index("dom")
    return dom > 0 if side == 0 else dom < lax.axis_size("dom") - 1


def iota(shape, dim):
    return lax.broadcasted_iota(I32, shape, dim)


def lanes(x, idx):
    return jnp.take_along_axis(x, idx, axis=1, mode="promise_in_bounds")


def nn(a, b):
    return jnp.dot(a, b, preferred_element_type=F32)


def nt(a, b):
    return lax.dot_general(a, b, NT, preferred_element_type=F32)


def split(x):
    hi = x.astype(BF16)
    return hi, (x - hi.astype(F32)).astype(BF16)


def at(b):
    return pl.ds(pl.multiple_of(b * L, L), L)


def blocks(b, n):
    return pl.ds(pl.multiple_of(b * L, L), n * L)


def one_hot(row, n):
    return (jnp.broadcast_to(row, (n, row.shape[1])) == iota((n, row.shape[1]), 0)).astype(F32)


def hang_tables(ent_ref, a_ref, b_ref, lhs_ref, oh_ref, pe_ref, src_ref, posr_ref, hq_ref, start_ref):
    for i in range(E // L):
        col = slice(i * L, (i + 1) * L)
        row = ent_ref[0:1, col]
        a_ref[:, col] = one_hot(row >> 7, L).astype(BF16)
        b_ref[:, col] = one_hot(row & 127, L).astype(BF16)
    flag = nt(a_ref[...], b_ref[...]) > 0.5
    flagb = flag.astype(F32).astype(BF16)
    tri = (iota((L, L), 0) < iota((L, L), 1)).astype(F32).astype(BF16)
    low = (iota((L, L), 1) < iota((L, L), 0)).astype(F32).astype(BF16)
    total = nn(flagb, jnp.ones((L, L), BF16))
    pos = (nn(flagb, tri) + nn(low, total.astype(BF16))).astype(I32)
    posr_ref[...] = jnp.where(flag, pos, -1)
    totrow = nt(jnp.ones((8, L), BF16), flagb)
    start_ref[...] = nn(totrow.astype(BF16), tri).astype(I32)
    ph = (pos >> 7).astype(F32).astype(BF16)
    plo = (pos & 127).astype(F32).astype(BF16)
    for i in range(E // L):
        col = slice(i * L, (i + 1) * L)
        ent = ent_ref[0:1, col]
        mask = a_ref[:, col].astype(F32)
        b = b_ref[:, col]
        hi = jnp.sum(nn(ph, b) * mask, axis=0, keepdims=True)
        lo = jnp.sum(nn(plo, b) * mask, axis=0, keepdims=True)
        pe = jnp.where(ent >= 0, hi.astype(I32) * L + lo.astype(I32), BIG)
        pe_ref[0:1, col] = pe
        oh_ref[:, col] = one_hot(pe & (QLO - 1), QLO).astype(BF16)
        qm = one_hot(pe // QLO, 16)
        lhs_ref[0:16, col] = qm.astype(BF16)
        lhs_ref[16:32, col] = (qm * (ent >> 7).astype(F32)).astype(BF16)
        lhs_ref[32:48, col] = (qm * (ent & 127).astype(F32)).astype(BF16)
        lhs_ref[48:64, col] = (qm if i >= ME // L else jnp.zeros_like(qm)).astype(BF16)
    res = nt(lhs_ref[...], oh_ref[...])
    cnt = res[0:16]
    den = jnp.maximum(cnt, 1.0)
    blk = (res[16:32] / den + 0.5).astype(I32)
    lo = (res[32:48] / den + 0.5).astype(I32)
    src = jnp.where(cnt > 0.5, blk * L + lo, -1)
    for q in range(QHI):
        for t in range(QB):
            src_ref[QB * q + t : QB * q + t + 1, :] = src[q : q + 1, t * L : (t + 1) * L]
    hq_ref[...] = res[48:64]


def zat(c):
    return pl.ds(pl.multiple_of((c // QB) * S, S), S), pl.ds(pl.multiple_of((c % QB) * L, L), L)


UNROLL = 12


def compress(read, z_ref, src_ref, start_ref):
    z_ref[...] = jnp.zeros_like(z_ref)

    def step(i, cur):
        for k in range(UNROLL):
            b = i * UNROLL + k
            y = read(b)
            c = start_ref[0, b] >> 7
            ahead = start_ref[0, b + 1] >> 7
            parts = []
            for t in range(2):
                row = jnp.broadcast_to(src_ref[pl.ds(c + t, 1), :], (S, L))
                parts.append(((row >> 7) == b, lanes(y, row & 127)))
            cur = jnp.where(parts[0][0], parts[0][1], cur)
            r, l = zat(c)
            z_ref[r, l] = cur
            after = jnp.where(parts[1][0], parts[1][1], 0.0)
            cur = jnp.where(ahead > c, after, cur)
        return cur

    cur = lax.fori_loop(0, NB // UNROLL, step, jnp.zeros((S, L), F32))
    r, l = zat(start_ref[0, NB] >> 7)
    z_ref[r, l] = cur


def expand(b, y, z_ref, posr_ref, start_ref):
    row = jnp.broadcast_to(posr_ref[pl.ds(b, 1), :], (S, L))
    c0 = start_ref[0, b] >> 7
    for t in range(2):
        c = c0 + t
        r, l = zat(c)
        y = jnp.where((row >> 7) == c, lanes(z_ref[r, l], row & 127), y)
    return y


def gather_entries(z_ref, oh_ref, pe_ref, g_ref, first, last):
    zz = jnp.concatenate(split(z_ref[...]), axis=0)
    n = QHI * S
    w = 256
    for i in range(first // w, last // w):
        col = slice(i * w, (i + 1) * w)
        g = nn(zz, oh_ref[:, col])
        q = jnp.broadcast_to(pe_ref[0:1, col] // QLO, (S, w))
        hi = g[0:S]
        lo = g[n : n + S]
        for h in range(1, QHI):
            m = q == h
            hi = jnp.where(m, g[h * S : (h + 1) * S], hi)
            lo = jnp.where(m, g[n + h * S : n + (h + 1) * S], lo)
        g_ref[:, col] = hi + lo


def scatter_entries(g_ref, oh_ref, pe_ref, lhs_ref, first, last):
    n = QHI * S
    for i in range(first // L, last // L):
        col = slice(i * L, (i + 1) * L)
        g = g_ref[:, col]
        hi = g.astype(BF16).astype(F32)
        lo = g - hi
        q = jnp.broadcast_to(pe_ref[0:1, col] // QLO, (S, L))
        for h in range(QHI):
            m = q == h
            lhs_ref[h * S : (h + 1) * S, col] = jnp.where(m, hi, 0.0).astype(BF16)
            lhs_ref[n + h * S : n + (h + 1) * S, col] = jnp.where(m, lo, 0.0).astype(BF16)
    res = nt(lhs_ref[:, first:last], oh_ref[:, first:last])
    return res[:n] + res[n:]


def hanging_values(z_ref, oh_ref, pe_ref, w_ref, g_ref, lhs_ref, hq_ref):
    gather_entries(z_ref, oh_ref, pe_ref, g_ref, 0, ME)
    g_ref[:, ME + HPAD :] = jnp.zeros((S, HE - HPAD), F32)
    for j in range(HB):
        acc = jnp.zeros((S, L), F32)
        for k in range(MASTERS):
            col = slice(k * HPAD + j * L, k * HPAD + (j + 1) * L)
            acc = acc + g_ref[:, col] * w_ref[0:1, col]
        g_ref[:, ME + j * L : ME + (j + 1) * L] = acc
    cz = scatter_entries(g_ref, oh_ref, pe_ref, lhs_ref, ME, E)
    for h in range(QHI):
        r = slice(h * S, (h + 1) * S)
        m = jnp.broadcast_to(hq_ref[h : h + 1, :], (S, QLO)) > 0.5
        z_ref[r, :] = jnp.where(m, cz[r], z_ref[r, :])


def add_to_masters(z_ref, oh_ref, pe_ref, w_ref, g_ref, lhs_ref):
    gather_entries(z_ref, oh_ref, pe_ref, g_ref, ME, E)
    for j in range(HB):
        y = g_ref[:, ME + j * L : ME + (j + 1) * L]
        for k in range(MASTERS):
            col = slice(k * HPAD + j * L, k * HPAD + (j + 1) * L)
            g_ref[:, col] = y * w_ref[0:1, col]
    z_ref[...] += scatter_entries(g_ref, oh_ref, pe_ref, lhs_ref, 0, ME)


def prepare_kernel(
    hang_ref, block_ref,
    pe_ref, w_ref, src_ref, posr_ref, hq_ref, start_ref, u_ref, left_ref, right_ref,
    ent_ref, oh_ref, a_ref, b_ref, tab_ref, z_ref, g_ref, lhs_ref, start_s, sem,
):
    for k in range(MASTERS):
        col = slice(k * HPAD, (k + 1) * HPAD)
        ent_ref[0:1, col] = hang_ref[k : k + 1, :].astype(I32)
        w_ref[0:1, col] = hang_ref[MASTERS + 1 + k : MASTERS + 2 + k, :]
    ent_ref[0:1, ME + HPAD :] = jnp.full((1, HE - HPAD), -1, I32)
    ent_ref[0:1, ME : ME + HPAD] = hang_ref[MASTERS : MASTERS + 1, :].astype(I32)
    hang_tables(ent_ref, a_ref, b_ref, tab_ref, oh_ref, pe_ref, src_ref, posr_ref, hq_ref, start_ref)
    copy = pltpu.make_async_copy(start_ref, start_s, sem)
    copy.start()
    copy.wait()
    compress(lambda b: block_ref[:, at(b)], z_ref, src_ref, start_s)
    hanging_values(z_ref, oh_ref, pe_ref, w_ref, g_ref, lhs_ref, hq_ref)

    def step(i, _):
        for k in range(UNROLL):
            b = i * UNROLL + k
            u_ref[:, at(b)] = expand(b, block_ref[:, at(b)], z_ref, posr_ref, start_s)
        return 0

    lax.fori_loop(0, NB // UNROLL, step, 0)
    left_ref[...] = u_ref[:, 0:EDGE]
    right_ref[...] = u_ref[:, LOC - EDGE :]


def sds(shape, dtype=F32):
    return jax.ShapeDtypeStruct(shape, dtype)


HANG_SCRATCH = [
    pltpu.VMEM((QHI * S, QLO), F32),
    pltpu.VMEM((S, E), F32),
    pltpu.VMEM((2 * QHI * S, E), BF16),
]


def prepare(hang, block):
    return pl.pallas_call(
        prepare_kernel,
        out_shape=(
            sds((1, E), I32),
            sds((1, ME)),
            sds((QB * QHI + 4, L), I32),
            sds((L, L), I32),
            sds((16, QLO)),
            sds((8, L), I32),
            sds((S, LOC)),
            sds((S, EDGE)),
            sds((S, EDGE)),
        ),
        in_specs=[VM] * 2,
        out_specs=(VM,) * 9,
        scratch_shapes=[
            pltpu.VMEM((1, E), I32),
            pltpu.VMEM((QLO, E), BF16),
            pltpu.VMEM((L, E), BF16),
            pltpu.VMEM((L, E), BF16),
            pltpu.VMEM((64, E), BF16),
            *HANG_SCRATCH,
            pltpu.SMEM((8, L), I32),
            pltpu.SemaphoreType.DMA,
        ],
        compiler_params=pltpu.CompilerParams(vmem_limit_bytes=VLIM),
        name="prepare",
    )(hang, block)


def pack_kernel(
    dofs_hbm, pot_hbm, scale_hbm, rows_hbm, masters_hbm, weights_hbm, count_ref,
    own_ref, hang_ref,
    dofs_ref, pot_ref, scale_ref, rows_ref, masters_ref, weights_ref, sems,
):
    moves = (
        (dofs_hbm, dofs_ref),
        (pot_hbm, pot_ref),
        (scale_hbm, scale_ref),
        (rows_hbm, rows_ref),
        (masters_hbm, masters_ref),
        (weights_hbm, weights_ref),
    )
    loads = [pltpu.make_async_copy(src, dst, sems.at[i]) for i, (src, dst) in enumerate(moves)]
    for load in loads:
        load.start()
    for load in loads:
        load.wait()
    own_ref[0:CELLS, 0:NODES] = dofs_ref[...].astype(F32)
    own_ref[0:CELLS, NPAD : NPAD + NODES] = pot_ref[...]
    scale = jnp.broadcast_to(scale_ref[...].reshape(1, CELLS), (PACK - CELLS, CELLS))
    own_ref[CELLS:PACK, 0:CELLS] = scale
    own_ref[CELLS:PACK, L : 2 * L] = jnp.full((PACK - CELLS, L), count_ref[0]).astype(F32)
    hang_ref[...] = jnp.where(iota((2 * MASTERS + 1, HPAD), 0) < MASTERS + 1, -1.0, 0.0)
    hang_ref[0:MASTERS, 0:HANG] = masters_ref[...].astype(F32)
    hang_ref[MASTERS : MASTERS + 1, 0:HANG] = rows_ref[...].reshape(1, HANG).astype(F32)
    hang_ref[MASTERS + 1 :, 0:HANG] = weights_ref[...]


def pack(dofs, pot, scale, rows, masters, weights, count):
    return pl.pallas_call(
        pack_kernel,
        out_shape=(sds((PACK, PW)), sds((2 * MASTERS + 1, HPAD))),
        in_specs=[HBM] * 6 + [SM],
        out_specs=(VM, VM),
        scratch_shapes=[
            pltpu.VMEM((CELLS, NODES), I32),
            pltpu.VMEM((CELLS, NODES), F32),
            pltpu.VMEM((CELLS,), F32),
            pltpu.VMEM((HANG,), I32),
            pltpu.VMEM((MASTERS, HANG), I32),
            pltpu.VMEM((MASTERS, HANG), F32),
            pltpu.SemaphoreType.DMA((6,)),
        ],
        compiler_params=pltpu.CompilerParams(vmem_limit_bytes=WHOLE),
        name="pack",
    )(dofs, pot, scale, rows, masters, weights, count)


def inverse(rels):
    oh = jnp.concatenate([one_hot(rel & 127, L) for rel in rels], axis=1).astype(BF16)
    rows = []
    for j, rel in enumerate(rels):
        m = jnp.broadcast_to(rel >> 7, (8, L)) == iota((8, L), 0)
        node = jnp.where(m, iota((8, L), 1) + 1, 0).astype(F32)
        zero = jnp.zeros((8, L), F32)
        rows.append(jnp.concatenate([node if i == j else zero for i in range(len(rels))], axis=1))
    return nt(jnp.concatenate(rows, axis=0).astype(BF16), oh).astype(I32) - 1


def cells_kernel(
    own_ref, left_ref, right_ref, pe_ref, k_hbm,
    tab_ref, pot_ref, kh_ref, kl_ref, oh_ref, base_ref,
    all_ref, meta_ref, k_ref, pad_ref, meta_s, list_s, wide_s, sem, sem_k,
):
    load = pltpu.make_async_copy(k_hbm, k_ref, sem_k)
    load.start()
    lane = iota((CELLS, L), 1)
    cell = iota((CELLS, L), 0)
    tail = NODES - 2 * L
    sources = ((own_ref, 0, None), (left_ref, -LOC, 0), (right_ref, LOC, 1))
    for i, (ref, shift, side) in enumerate(sources):
        r = slice(i * CELLS, (i + 1) * CELLS)
        lows, tops = [], []
        for j in range(NJ):
            dofs = ref[0:CELLS, j * L : (j + 1) * L] + float(shift)
            real = lane < (L if j < 2 else tail)
            low = jnp.where(real, dofs, float(BIG))
            all_ref[r, j * L : (j + 1) * L] = low
            pot = ref[0:CELLS, NPAD + j * L : NPAD + (j + 1) * L]
            all_ref[r, NPAD + j * L : NPAD + (j + 1) * L] = jnp.where(real, pot, 0.0)
            lows.append(jnp.min(low, axis=1, keepdims=True).astype(I32))
            tops.append(jnp.max(jnp.where(real, dofs, -float(BIG)), axis=1, keepdims=True).astype(I32))
        scales = jnp.broadcast_to(ref[CELLS : CELLS + 1, 0:L], (CELLS, L))
        scale = jnp.sum(jnp.where(lane == cell, scales, 0.0), axis=1, keepdims=True)
        all_ref[r, 2 * NPAD :] = jnp.broadcast_to(scale, (CELLS, L))
        count = jnp.broadcast_to(ref[CELLS : CELLS + 1, L : 2 * L], (CELLS, L))
        live = cell.astype(F32) < count
        if side is not None:
            live = live & jnp.full((CELLS, L), inside(side))
        low = jnp.minimum(jnp.minimum(lows[0], lows[1]), lows[2])
        top = jnp.maximum(jnp.maximum(tops[0], tops[1]), tops[2])
        used = live & (top >= RIM) & (low < RIM + LOC)
        starts = [jnp.minimum(x >> 7, EXT // L - NARROW) for x in lows]
        narrow = ((tops[0] >> 7) - starts[0] < NARROW) & ((tops[1] >> 7) - starts[1] < NARROW)
        narrow = narrow & ((tops[2] >> 7) - starts[2] < NARROW)
        base = jnp.minimum(low >> 7, EXT // L - WIDE)
        meta = jnp.where(used, jnp.where(narrow, 0, 1), -1)
        for j in range(NJ):
            meta = jnp.where(lane == 1 + j, jnp.where(narrow, starts[j], base), meta)
        meta_ref[r, :] = meta
    copy = pltpu.make_async_copy(meta_ref, meta_s, sem)
    copy.start()
    pad_ref[...] = jnp.zeros_like(pad_ref)
    load.wait()
    pad_ref[0:NODES, 0:NODES] = k_ref[...]
    kh_ref[...], kl_ref[...] = split(pad_ref[...].T)
    for i in range(E // L):
        col = slice(i * L, (i + 1) * L)
        oh_ref[:, col] = one_hot(pe_ref[0:1, col] & (QLO - 1), QLO).astype(BF16)
    copy.wait()

    def scan(c, counts):
        kind = meta_s[c, 0]
        n, m = counts
        list_s[n] = c
        wide_s[m] = c
        return n + jnp.where(kind == 0, 1, 0), m + jnp.where(kind == 1, 1, 0)

    n, m = lax.fori_loop(0, 3 * CELLS, scan, (0, 0), unroll=4)
    gn = 2 * ((n + 2 * GROUP - 1) // (2 * GROUP))
    gw = (m + GROUP - 1) // GROUP
    first = (gn + 1) * GROUP
    last = first + gw * GROUP

    def blank(i, _):
        list_s[i] = -1
        return 0

    def move(i, _):
        list_s[first + i] = wide_s[i]
        return 0

    lax.fori_loop(n, first, blank, 0)
    lax.fori_loop(0, m, move, 0)
    lax.fori_loop(first + m, last, blank, 0)
    base_ref[4 * SLOTS] = gn
    base_ref[4 * SLOTS + 1] = gw

    def one(slot):
        c = list_s[slot]
        valid = c >= 0
        c = jnp.maximum(c, 0)
        vals = all_ref[pl.ds(c, 1), :]
        rels = []
        for j in range(NJ):
            b = jnp.where(valid, meta_s[c, 1 + j], 0)
            base_ref[4 * slot + j] = b
            rel = vals[:, j * L : (j + 1) * L].astype(I32) - b * L
            rel = jnp.where(valid & (rel < WIDE * L), rel, BIG)
            rels.append(rel)
            tab_ref[slot, j : j + 1, :] = rel
            pot_ref[slot, j : j + 1, :] = vals[:, NPAD + j * L : NPAD + (j + 1) * L]
        pot_ref[slot, 3:4, :] = vals[:, 2 * NPAD :]
        inv = inverse(rels)
        for j in range(NJ):
            tab_ref[slot, 3 + 3 * j : 6 + 3 * j, :] = inv[8 * j : 8 * j + NARROW]

    def some(i, _):
        for k in range(8):
            one(i * 8 + k)
        return 0

    lax.fori_loop(0, last // 8, some, 0)


def cell_tables(own, left, right, pe, stiffness):
    return pl.pallas_call(
        cells_kernel,
        out_shape=(
            sds((SLOTS, 16, L), I32),
            sds((SLOTS, 8, L)),
            sds((NPAD, NPAD), BF16),
            sds((NPAD, NPAD), BF16),
            sds((QLO, E), BF16),
            sds((4 * SLOTS + L,), I32),
        ),
        in_specs=[VM] * 4 + [HBM],
        out_specs=(VM, VM, VM, VM, VM, SM),
        scratch_shapes=[
            pltpu.VMEM((3 * CELLS, PW), F32),
            pltpu.VMEM((3 * CELLS, L), I32),
            pltpu.VMEM((NODES, NODES), F32),
            pltpu.VMEM((NPAD, NPAD), F32),
            pltpu.SMEM((3 * CELLS, L), I32),
            pltpu.SMEM((SLOTS + GROUP,), I32),
            pltpu.SMEM((3 * CELLS + GROUP,), I32),
            pltpu.SemaphoreType.DMA,
            pltpu.SemaphoreType.DMA,
        ],
        compiler_params=pltpu.CompilerParams(vmem_limit_bytes=SMALL),
        name="cell_tables",
    )(own, left, right, pe, stiffness)


def step_kernel(number, *refs):
    (u_ref, gl_ref, gr_ref, prev_ref, tab_ref, pot_ref, kh_ref, kl_ref,
     oh_ref, pe_ref, w_ref, src_ref, posr_ref, hq_ref, base_ref, start_ref) = refs[:16]
    outs = refs[16 : 16 + (4 if number == 3 else 3)]
    ext_ref, acc0_ref, acc1_ref, x0_ref, x1_ref, p0_ref, p1_ref, z_ref, g_ref, lhs_ref = refs[16 + len(outs) :]
    accs = (acc0_ref, acc1_ref)
    ext_ref[:, 0 : RIM - EDGE] = jnp.zeros((S, RIM - EDGE), F32)
    ext_ref[:, RIM + LOC + EDGE :] = jnp.zeros((S, RIM - EDGE), F32)
    ext_ref[:, RIM - EDGE : RIM] = jnp.where(inside(0), gl_ref[...], 0.0)
    ext_ref[:, RIM : RIM + LOC] = u_ref[...]
    ext_ref[:, RIM + LOC : RIM + LOC + EDGE] = jnp.where(inside(1), gr_ref[...], 0.0)
    for ref in accs:
        ref[...] = jnp.zeros_like(ref)
    gn = base_ref[4 * SLOTS]
    gw = base_ref[4 * SLOTS + 1]

    def rows8(k, s):
        return pl.ds(k * S + 8 * s, 8) if isinstance(k, int) else pl.ds(pl.multiple_of(k * S + 8 * s, 8), 8)

    def load(x_ref, group, k, width):
        slot = group * GROUP + k
        for j in range(NJ):
            b = base_ref[4 * slot + j]
            row = jnp.broadcast_to(tab_ref[slot, j : j + 1, :], (8, L))
            lo, hi = row & 127, row >> 7
            for s in range(2):
                r = slice(8 * s, 8 * s + 8)
                rows = ext_ref[r, blocks(b, width)]
                acc = lanes(rows[:, 0:L], lo)
                for t in range(1, width):
                    acc = jnp.where(hi == t, lanes(rows[:, t * L : (t + 1) * L], lo), acc)
                x_ref[rows8(k, s), j * L : (j + 1) * L] = acc

    def store(p_ref, group, k, width):
        slot = group * GROUP + k
        acc_ref = accs[k % 2 if isinstance(k, int) else 0]
        if width == NARROW:
            inv = [[tab_ref[slot, 3 + 3 * j + t : 4 + 3 * j + t, :] for t in range(width)] for j in range(NJ)]
        else:
            full = inverse([tab_ref[slot, j : j + 1, :] for j in range(NJ)])
            inv = [[full[8 * j + t : 8 * j + t + 1] for t in range(width)] for j in range(NJ)]
        for j in range(NJ):
            b = base_ref[4 * slot + j]
            vals = [p_ref[rows8(k, s), j * L : (j + 1) * L] for s in range(2)]
            adds = []
            for t in range(width):
                row = jnp.broadcast_to(inv[j][t], (8, L))
                m, lo = row >= 0, row & 127
                adds.append([jnp.where(m, lanes(vals[s], lo), 0.0) for s in range(2)])
            for s in range(2):
                more = jnp.concatenate([adds[t][s] for t in range(width)], axis=1)
                acc_ref[8 * s : 8 * s + 8, blocks(b, width)] += more

    def product(x_ref, p_ref, group):
        n = GROUP * S
        x = x_ref[...]
        xh, xl = split(x)
        both = nn(jnp.concatenate([xh, xl], 0), kh_ref[...])
        prod = both[:n] + (both[n:] + nn(xh, kl_ref[...]))
        for k in range(GROUP):
            slot = group * GROUP + k
            r = slice(k * S, (k + 1) * S)
            scale = jnp.broadcast_to(pot_ref[slot, 3:4, :], (S, L))
            for j in range(NJ):
                col = slice(j * L, (j + 1) * L)
                pot = jnp.broadcast_to(pot_ref[slot, j : j + 1, :], (S, L))
                p_ref[r, col] = scale * prod[r, col] + pot * x[r, col]

    def load_group(x_ref, group, width, n):
        def some(q, _):
            for k in range(n):
                load(x_ref, group, q * n + k, width)
            return 0

        lax.fori_loop(0, GROUP // n, some, 0)

    load_group(x0_ref, 0, NARROW, 4)

    def pipeline(i, _):
        g = 2 * i
        product(x0_ref, p0_ref, g)
        before = jnp.where(i == 0, gn, g - 1)
        for k in range(GROUP):
            store(p1_ref, before, k, NARROW)
            load(x1_ref, g + 1, k, NARROW)
        product(x1_ref, p1_ref, g + 1)
        for k in range(GROUP):
            store(p0_ref, g, k, NARROW)
            load(x0_ref, g + 2, k, NARROW)
        return 0

    lax.fori_loop(0, gn // 2, pipeline, 0)
    for k in range(GROUP):
        store(p1_ref, jnp.where(gn > 0, gn - 1, gn), k, NARROW)

    def wide(i, _):
        load_group(x0_ref, i, WIDE, 1)
        product(x0_ref, p0_ref, i)

        def one(k, _):
            store(p0_ref, i, k, WIDE)
            return 0

        lax.fori_loop(0, GROUP, one, 0)
        return 0

    lax.fori_loop(gn + 1, gn + 1 + gw, wide, 0)

    def read(b):
        return acc0_ref[:, at(b + RB)] + acc1_ref[:, at(b + RB)]

    compress(read, z_ref, src_ref, start_ref)
    add_to_masters(z_ref, oh_ref, pe_ref, w_ref, g_ref, lhs_ref)
    hanging_values(z_ref, oh_ref, pe_ref, w_ref, g_ref, lhs_ref, hq_ref)
    new_ref = outs[0] if number < 3 else ext_ref

    def finish(i, _):
        for k in range(UNROLL):
            b = i * UNROLL + k
            t = expand(b, read(b), z_ref, posr_ref, start_ref)
            r = (t - CENTRE * u_ref[:, at(b)]) * ((1.0 if number == 1 else 2.0) / HALF)
            if number > 1:
                r = r - prev_ref[:, at(b)]
            new_ref[:, at(b)] = r
        return 0

    lax.fori_loop(0, NB // UNROLL, finish, 0)
    if number < 3:
        outs[1][...] = new_ref[:, 0:EDGE]
        outs[2][...] = new_ref[:, LOC - EDGE :]
    else:
        me = lax.axis_index("band")
        q = LOC // 4
        for k in range(4):
            outs[k][...] = new_ref[:, pl.ds(pl.multiple_of(((me + k) & 3) * q, L), q)]


def apply_step(number, u, gl, gr, prev, cell, base, hang, start):
    if number == 3:
        shapes = (sds((S, LOC // 4)),) * 4
    else:
        shapes = (sds((S, LOC)), sds((S, EDGE)), sds((S, EDGE)))
    return pl.pallas_call(
        functools.partial(step_kernel, number),
        out_shape=shapes,
        in_specs=[VM] * 14 + [SM] * 2,
        out_specs=(VM,) * len(shapes),
        scratch_shapes=[
            pltpu.VMEM((S, EXT), F32),
            pltpu.VMEM((S, EXT), F32),
            pltpu.VMEM((S, EXT), F32),
            *[pltpu.VMEM((GROUP * S, NPAD), F32)] * 4,
            *HANG_SCRATCH,
        ],
        compiler_params=pltpu.CompilerParams(vmem_limit_bytes=VLIM),
        name=f"step{number}",
    )(u, gl, gr, prev, *cell, *hang, base, start)


def gram_kernel(q0_ref, q1_ref, q2_ref, q3_ref, gram_ref, all_ref):
    me = lax.axis_index("band")
    for k, ref in enumerate((q0_ref, q1_ref, q2_ref, q3_ref)):
        all_ref[pl.ds(pl.multiple_of(((me - k) & 3) * S, S), S), :] = ref[...]
    a = all_ref[...]
    gram_ref[...] = lax.dot_general(a, a, NT, preferred_element_type=F32, precision=lax.Precision.HIGHEST)


def gram_of(qs):
    n = qs[0].shape[1]
    return pl.pallas_call(
        gram_kernel,
        out_shape=(sds((4 * S, 4 * S)), sds((4 * S, n))),
        in_specs=[VM] * 4,
        out_specs=(VM, VM),
        compiler_params=pltpu.CompilerParams(vmem_limit_bytes=VLIM),
        name="gram",
    )(*qs)


def basis_kernel(total, gram_ref, all_ref, o0_ref, o1_ref, o2_ref, o3_ref, m_ref, r_ref):
    n = 4 * S
    eye = (iota((n, n), 0) == iota((n, n), 1)).astype(F32)
    m_ref[...] = jnp.concatenate([gram_ref[...], eye], 1)
    row_id = iota((n, 2 * n), 0)

    m = m_ref[...]
    for j in range(n):
        pivot = m[j : j + 1, :]
        scaled = pivot * (1.0 / pivot[:, j : j + 1])
        m = m - jnp.where(row_id > j, m[:, j : j + 1], 0.0) * scaled
    dg = jnp.sum(jnp.where(row_id == iota((n, 2 * n), 1), m, 0.0), axis=1, keepdims=True)
    inv = m[:, n:] * lax.rsqrt(dg) * jnp.sqrt(jnp.float32(total))
    r_ref[...] = jnp.dot(inv, all_ref[...], preferred_element_type=F32, precision=lax.Precision.HIGHEST)
    me = lax.axis_index("band")
    for k, ref in enumerate((o0_ref, o1_ref, o2_ref, o3_ref)):
        ref[...] = r_ref[pl.ds(pl.multiple_of(((me + k) & 3) * S, S), S), :]


def basis_of(gram, rows, total):
    n = rows.shape[1]
    return pl.pallas_call(
        functools.partial(basis_kernel, total),
        out_shape=(sds((S, n)),) * 4,
        in_specs=[VM, VM],
        out_specs=(VM,) * 4,
        scratch_shapes=[pltpu.VMEM((4 * S, 8 * S), F32), pltpu.VMEM((4 * S, n), F32)],
        compiler_params=pltpu.CompilerParams(vmem_limit_bytes=VLIM),
        name="basis",
    )(gram, rows)


def join_kernel(q0_ref, q1_ref, q2_ref, q3_ref, out_ref):
    me = lax.axis_index("band")
    n = q0_ref.shape[1]
    for k, ref in enumerate((q0_ref, q1_ref, q2_ref, q3_ref)):
        out_ref[:, pl.ds(pl.multiple_of(((me - k) & 3) * n, L), n)] = ref[...]


def join(qs):
    return pl.pallas_call(
        join_kernel,
        out_shape=sds((S, LOC)),
        in_specs=[VM] * 4,
        out_specs=VM,
        compiler_params=pltpu.CompilerParams(vmem_limit_bytes=VLIM),
        name="join",
    )(*qs)


def shift(x, axis, by):
    size = lax.axis_size(axis)
    return lax.ppermute(x, axis, [(i, (i + by) % size) for i in range(size)])


def swap(x, axis, bits):
    size = lax.axis_size(axis)
    return lax.ppermute(x, axis, [(i, i ^ bits) for i in range(size)])


def summed(g):
    g = g + swap(g, "dom", 1)
    for axis, unit in (("dom", 2), ("dom", 8), ("band", 1)):
        others = [swap(g, axis, unit * k) for k in (1, 2, 3)]
        g = (g + others[0]) + (others[1] + others[2])
    return g


def body(
    block,
    stiffness,
    cell_scale,
    potential,
    cell_dofs,
    cell_count,
    hang_rows,
    hang_masters,
    hang_weights,
):
    own, hanging = pack(
        cell_dofs.T, potential.T, cell_scale, hang_rows, hang_masters, hang_weights, cell_count
    )
    from_left = shift(own, "dom", 1)
    from_right = shift(own, "dom", -1)
    *hang, start, u0, first, last = prepare(hanging, block)

    def ghosts(first, last):
        return shift(last, "dom", 1), shift(first, "dom", -1)

    gl, gr = ghosts(first, last)
    *cell, base = cell_tables(own, from_left, from_right, hang[0], stiffness)
    args = (cell, base, hang, start)
    u1, first, last = apply_step(1, u0, gl, gr, u0, *args)
    gl, gr = ghosts(first, last)
    u2, first, last = apply_step(2, u1, gl, gr, u0, *args)
    gl, gr = ghosts(first, last)
    qs = apply_step(3, u2, gl, gr, u1, *args)
    qs = [qs[0]] + [shift(qs[k], "band", k) for k in (1, 2, 3)]
    gram, rows = gram_of(qs)
    gram = summed(gram)
    outs = basis_of(gram, rows, LOC * lax.axis_size("dom"))
    outs = [outs[0]] + [shift(outs[k], "band", k) for k in (1, 2, 3)]
    return join(outs)


def solution(mesh):
    return jax.shard_map(
        body,
        mesh=mesh,
        in_specs=(
            P("band", "dom"),
            P(),
            P("dom"),
            P(None, "dom"),
            P(None, "dom"),
            P("dom"),
            P("dom"),
            P(None, "dom"),
            P(None, "dom"),
        ),
        out_specs=P("band", "dom"),
        check_vma=False,
    )
```

```python
import functools
import jax
import jax.numpy as jnp
from jax import lax
from jax.experimental import pallas as pl
from jax.experimental.pallas import tpu as pltpu
from jax.sharding import PartitionSpec as P

RIM = 2048
EDGE = 768
NODES = 343
HANG = 864
MASTERS = 4
LOC = 13824
CELLS = 64
S = 16
L = 128
EXT = LOC + 2 * RIM
NB = LOC // L
RB = RIM // L
NPAD = 384
NJ = NPAD // L
WIDE = 7
NARROW = 3
PACK = 72
PW = 2 * NPAD + L
GROUP = 8
SLOTS = 28 * GROUP
HPAD = 896
HB = HPAD // L
ME = MASTERS * HPAD
HE = 1024
E = ME + HE
QLO = 512
QB = QLO // L
QHI = 9
BIG = 1 << 20
CENTRE = 4.5
HALF = 3.5
F32 = jnp.float32
BF16 = jnp.bfloat16
I32 = jnp.int32
VLIM = 28 * 1024 * 1024
SMALL = 20 * 1024 * 1024
WHOLE = 64 * 1024 * 1024

VM = pl.BlockSpec(memory_space=pltpu.VMEM)
SM = pl.BlockSpec(memory_space=pltpu.SMEM)
HBM = pl.BlockSpec(memory_space=pltpu.HBM)
NT = (((1,), (1,)), ((), ()))


def inside(side):
    dom = lax.axis_index("dom")
    return dom > 0 if side == 0 else dom < lax.axis_size("dom") - 1


def iota(shape, dim):
    return lax.broadcasted_iota(I32, shape, dim)


def lanes(x, idx):
    return jnp.take_along_axis(x, idx, axis=1, mode="promise_in_bounds")


def nn(a, b):
    return jnp.dot(a, b, preferred_element_type=F32)


def nt(a, b):
    return lax.dot_general(a, b, NT, preferred_element_type=F32)


def split(x):
    hi = x.astype(BF16)
    return hi, (x - hi.astype(F32)).astype(BF16)


def at(b):
    return pl.ds(pl.multiple_of(b * L, L), L)


def blocks(b, n):
    return pl.ds(pl.multiple_of(b * L, L), n * L)


def one_hot(row, n):
    return (jnp.broadcast_to(row, (n, row.shape[1])) == iota((n, row.shape[1]), 0)).astype(F32)


def hang_tables(ent_ref, a_ref, b_ref, lhs_ref, oh_ref, pe_ref, src_ref, posr_ref, hq_ref, start_ref):
    for i in range(E // L):
        col = slice(i * L, (i + 1) * L)
        row = ent_ref[0:1, col]
        a_ref[:, col] = one_hot(row >> 7, L).astype(BF16)
        b_ref[:, col] = one_hot(row & 127, L).astype(BF16)
    flag = nt(a_ref[...], b_ref[...]) > 0.5
    flagb = flag.astype(F32).astype(BF16)
    tri = (iota((L, L), 0) < iota((L, L), 1)).astype(F32).astype(BF16)
    low = (iota((L, L), 1) < iota((L, L), 0)).astype(F32).astype(BF16)
    total = nn(flagb, jnp.ones((L, L), BF16))
    pos = (nn(flagb, tri) + nn(low, total.astype(BF16))).astype(I32)
    posr_ref[...] = jnp.where(flag, pos, -1)
    totrow = nt(jnp.ones((8, L), BF16), flagb)
    start_ref[...] = nn(totrow.astype(BF16), tri).astype(I32)
    ph = (pos >> 7).astype(F32).astype(BF16)
    plo = (pos & 127).astype(F32).astype(BF16)
    for i in range(E // L):
        col = slice(i * L, (i + 1) * L)
        ent = ent_ref[0:1, col]
        mask = a_ref[:, col].astype(F32)
        b = b_ref[:, col]
        hi = jnp.sum(nn(ph, b) * mask, axis=0, keepdims=True)
        lo = jnp.sum(nn(plo, b) * mask, axis=0, keepdims=True)
        pe = jnp.where(ent >= 0, hi.astype(I32) * L + lo.astype(I32), BIG)
        pe_ref[0:1, col] = pe
        oh_ref[:, col] = one_hot(pe & (QLO - 1), QLO).astype(BF16)
        qm = one_hot(pe // QLO, 16)
        lhs_ref[0:16, col] = qm.astype(BF16)
        lhs_ref[16:32, col] = (qm * (ent >> 7).astype(F32)).astype(BF16)
        lhs_ref[32:48, col] = (qm * (ent & 127).astype(F32)).astype(BF16)
        lhs_ref[48:64, col] = (qm if i >= ME // L else jnp.zeros_like(qm)).astype(BF16)
    res = nt(lhs_ref[...], oh_ref[...])
    cnt = res[0:16]
    den = jnp.maximum(cnt, 1.0)
    blk = (res[16:32] / den + 0.5).astype(I32)
    lo = (res[32:48] / den + 0.5).astype(I32)
    src = jnp.where(cnt > 0.5, blk * L + lo, -1)
    for q in range(QHI):
        for t in range(QB):
            src_ref[QB * q + t : QB * q + t + 1, :] = src[q : q + 1, t * L : (t + 1) * L]
    hq_ref[...] = res[48:64]


def zat(c):
    return pl.ds(pl.multiple_of((c // QB) * S, S), S), pl.ds(pl.multiple_of((c % QB) * L, L), L)


UNROLL = 18


def compress(read, z_ref, src_ref, start_ref):
    z_ref[...] = jnp.zeros_like(z_ref)

    def step(i, cur):
        for k in range(UNROLL):
            b = i * UNROLL + k
            y = read(b)
            c = start_ref[0, b] >> 7
            ahead = start_ref[0, b + 1] >> 7
            parts = []
            for t in range(2):
                row = jnp.broadcast_to(src_ref[pl.ds(c + t, 1), :], (S, L))
                parts.append(((row >> 7) == b, lanes(y, row & 127)))
            cur = jnp.where(parts[0][0], parts[0][1], cur)
            r, l = zat(c)
            z_ref[r, l] = cur
            after = jnp.where(parts[1][0], parts[1][1], 0.0)
            cur = jnp.where(ahead > c, after, cur)
        return cur

    cur = lax.fori_loop(0, NB // UNROLL, step, jnp.zeros((S, L), F32))
    r, l = zat(start_ref[0, NB] >> 7)
    z_ref[r, l] = cur


def expand(b, y, z_ref, posr_ref, start_ref):
    row = jnp.broadcast_to(posr_ref[pl.ds(b, 1), :], (S, L))
    c0 = start_ref[0, b] >> 7
    for t in range(2):
        c = c0 + t
        r, l = zat(c)
        y = jnp.where((row >> 7) == c, lanes(z_ref[r, l], row & 127), y)
    return y


def gather_entries(z_ref, oh_ref, pe_ref, g_ref, first, last):
    zz = jnp.concatenate(split(z_ref[...]), axis=0)
    n = QHI * S
    w = 256
    for i in range(first // w, last // w):
        col = slice(i * w, (i + 1) * w)
        g = nn(zz, oh_ref[:, col])
        q = jnp.broadcast_to(pe_ref[0:1, col] // QLO, (S, w))
        hi = g[0:S]
        lo = g[n : n + S]
        for h in range(1, QHI):
            m = q == h
            hi = jnp.where(m, g[h * S : (h + 1) * S], hi)
            lo = jnp.where(m, g[n + h * S : n + (h + 1) * S], lo)
        g_ref[:, col] = hi + lo


def scatter_entries(g_ref, oh_ref, pe_ref, lhs_ref, first, last):
    n = QHI * S
    for i in range(first // L, last // L):
        col = slice(i * L, (i + 1) * L)
        g = g_ref[:, col]
        hi = g.astype(BF16).astype(F32)
        lo = g - hi
        q = jnp.broadcast_to(pe_ref[0:1, col] // QLO, (S, L))
        for h in range(QHI):
            m = q == h
            lhs_ref[h * S : (h + 1) * S, col] = jnp.where(m, hi, 0.0).astype(BF16)
            lhs_ref[n + h * S : n + (h + 1) * S, col] = jnp.where(m, lo, 0.0).astype(BF16)
    res = nt(lhs_ref[:, first:last], oh_ref[:, first:last])
    return res[:n] + res[n:]


def hanging_values(z_ref, oh_ref, pe_ref, w_ref, g_ref, lhs_ref, hq_ref):
    gather_entries(z_ref, oh_ref, pe_ref, g_ref, 0, ME)
    g_ref[:, ME + HPAD :] = jnp.zeros((S, HE - HPAD), F32)
    for j in range(HB):
        acc = jnp.zeros((S, L), F32)
        for k in range(MASTERS):
            col = slice(k * HPAD + j * L, k * HPAD + (j + 1) * L)
            acc = acc + g_ref[:, col] * w_ref[0:1, col]
        g_ref[:, ME + j * L : ME + (j + 1) * L] = acc
    cz = scatter_entries(g_ref, oh_ref, pe_ref, lhs_ref, ME, E)
    for h in range(QHI):
        r = slice(h * S, (h + 1) * S)
        m = jnp.broadcast_to(hq_ref[h : h + 1, :], (S, QLO)) > 0.5
        z_ref[r, :] = jnp.where(m, cz[r], z_ref[r, :])


def add_to_masters(z_ref, oh_ref, pe_ref, w_ref, g_ref, lhs_ref):
    gather_entries(z_ref, oh_ref, pe_ref, g_ref, ME, E)
    for j in range(HB):
        y = g_ref[:, ME + j * L : ME + (j + 1) * L]
        for k in range(MASTERS):
            col = slice(k * HPAD + j * L, k * HPAD + (j + 1) * L)
            g_ref[:, col] = y * w_ref[0:1, col]
    z_ref[...] += scatter_entries(g_ref, oh_ref, pe_ref, lhs_ref, 0, ME)


def prepare_kernel(
    hang_ref, block_ref,
    pe_ref, w_ref, src_ref, posr_ref, hq_ref, start_ref, u_ref, left_ref, right_ref,
    ent_ref, oh_ref, a_ref, b_ref, tab_ref, z_ref, g_ref, lhs_ref, start_s, sem,
):
    for k in range(MASTERS):
        col = slice(k * HPAD, (k + 1) * HPAD)
        ent_ref[0:1, col] = hang_ref[k : k + 1, :].astype(I32)
        w_ref[0:1, col] = hang_ref[MASTERS + 1 + k : MASTERS + 2 + k, :]
    ent_ref[0:1, ME + HPAD :] = jnp.full((1, HE - HPAD), -1, I32)
    ent_ref[0:1, ME : ME + HPAD] = hang_ref[MASTERS : MASTERS + 1, :].astype(I32)
    hang_tables(ent_ref, a_ref, b_ref, tab_ref, oh_ref, pe_ref, src_ref, posr_ref, hq_ref, start_ref)
    copy = pltpu.make_async_copy(start_ref, start_s, sem)
    copy.start()
    copy.wait()
    compress(lambda b: block_ref[:, at(b)], z_ref, src_ref, start_s)
    hanging_values(z_ref, oh_ref, pe_ref, w_ref, g_ref, lhs_ref, hq_ref)

    def step(i, _):
        for k in range(UNROLL):
            b = i * UNROLL + k
            u_ref[:, at(b)] = expand(b, block_ref[:, at(b)], z_ref, posr_ref, start_s)
        return 0

    lax.fori_loop(0, NB // UNROLL, step, 0)
    left_ref[...] = u_ref[:, 0:EDGE]
    right_ref[...] = u_ref[:, LOC - EDGE :]


def sds(shape, dtype=F32):
    return jax.ShapeDtypeStruct(shape, dtype)


HANG_SCRATCH = [
    pltpu.VMEM((QHI * S, QLO), F32),
    pltpu.VMEM((S, E), F32),
    pltpu.VMEM((2 * QHI * S, E), BF16),
]


def prepare(hang, block):
    return pl.pallas_call(
        prepare_kernel,
        out_shape=(
            sds((1, E), I32),
            sds((1, ME)),
            sds((QB * QHI + 4, L), I32),
            sds((L, L), I32),
            sds((16, QLO)),
            sds((8, L), I32),
            sds((S, LOC)),
            sds((S, EDGE)),
            sds((S, EDGE)),
        ),
        in_specs=[VM] * 2,
        out_specs=(VM,) * 9,
        scratch_shapes=[
            pltpu.VMEM((1, E), I32),
            pltpu.VMEM((QLO, E), BF16),
            pltpu.VMEM((L, E), BF16),
            pltpu.VMEM((L, E), BF16),
            pltpu.VMEM((64, E), BF16),
            *HANG_SCRATCH,
            pltpu.SMEM((8, L), I32),
            pltpu.SemaphoreType.DMA,
        ],
        compiler_params=pltpu.CompilerParams(vmem_limit_bytes=VLIM),
        name="prepare",
    )(hang, block)


def pack_kernel(
    dofs_hbm, pot_hbm, scale_hbm, rows_hbm, masters_hbm, weights_hbm, count_ref,
    own_ref, hang_ref,
    dofs_ref, pot_ref, scale_ref, rows_ref, masters_ref, weights_ref, sems,
):
    moves = (
        (dofs_hbm, dofs_ref),
        (pot_hbm, pot_ref),
        (scale_hbm, scale_ref),
        (rows_hbm, rows_ref),
        (masters_hbm, masters_ref),
        (weights_hbm, weights_ref),
    )
    loads = [pltpu.make_async_copy(src, dst, sems.at[i]) for i, (src, dst) in enumerate(moves)]
    for load in loads:
        load.start()
    for load in loads:
        load.wait()
    own_ref[0:CELLS, 0:NODES] = dofs_ref[...].astype(F32)
    own_ref[0:CELLS, NPAD : NPAD + NODES] = pot_ref[...]
    scale = jnp.broadcast_to(scale_ref[...].reshape(1, CELLS), (PACK - CELLS, CELLS))
    own_ref[CELLS:PACK, 0:CELLS] = scale
    own_ref[CELLS:PACK, L : 2 * L] = jnp.full((PACK - CELLS, L), count_ref[0]).astype(F32)
    hang_ref[...] = jnp.where(iota((2 * MASTERS + 1, HPAD), 0) < MASTERS + 1, -1.0, 0.0)
    hang_ref[0:MASTERS, 0:HANG] = masters_ref[...].astype(F32)
    hang_ref[MASTERS : MASTERS + 1, 0:HANG] = rows_ref[...].reshape(1, HANG).astype(F32)
    hang_ref[MASTERS + 1 :, 0:HANG] = weights_ref[...]


def pack(dofs, pot, scale, rows, masters, weights, count):
    return pl.pallas_call(
        pack_kernel,
        out_shape=(sds((PACK, PW)), sds((2 * MASTERS + 1, HPAD))),
        in_specs=[HBM] * 6 + [SM],
        out_specs=(VM, VM),
        scratch_shapes=[
            pltpu.VMEM((CELLS, NODES), I32),
            pltpu.VMEM((CELLS, NODES), F32),
            pltpu.VMEM((CELLS,), F32),
            pltpu.VMEM((HANG,), I32),
            pltpu.VMEM((MASTERS, HANG), I32),
            pltpu.VMEM((MASTERS, HANG), F32),
            pltpu.SemaphoreType.DMA((6,)),
        ],
        compiler_params=pltpu.CompilerParams(vmem_limit_bytes=WHOLE),
        name="pack",
    )(dofs, pot, scale, rows, masters, weights, count)


def inverse(rels):
    oh = jnp.concatenate([one_hot(rel & 127, L) for rel in rels], axis=1).astype(BF16)
    rows = []
    for j, rel in enumerate(rels):
        m = jnp.broadcast_to(rel >> 7, (8, L)) == iota((8, L), 0)
        node = jnp.where(m, iota((8, L), 1) + 1, 0).astype(F32)
        zero = jnp.zeros((8, L), F32)
        rows.append(jnp.concatenate([node if i == j else zero for i in range(len(rels))], axis=1))
    return nt(jnp.concatenate(rows, axis=0).astype(BF16), oh).astype(I32) - 1


def cells_kernel(
    own_ref, left_ref, right_ref, pe_ref, k_hbm,
    tab_ref, pot_ref, kh_ref, kl_ref, oh_ref, base_ref,
    all_ref, meta_ref, k_ref, pad_ref, meta_s, list_s, wide_s, sem, sem_k,
):
    load = pltpu.make_async_copy(k_hbm, k_ref, sem_k)
    load.start()
    lane = iota((CELLS, L), 1)
    cell = iota((CELLS, L), 0)
    tail = NODES - 2 * L
    sources = ((own_ref, 0, None), (left_ref, -LOC, 0), (right_ref, LOC, 1))
    for i, (ref, shift, side) in enumerate(sources):
        r = slice(i * CELLS, (i + 1) * CELLS)
        lows, tops = [], []
        for j in range(NJ):
            dofs = ref[0:CELLS, j * L : (j + 1) * L] + float(shift)
            real = lane < (L if j < 2 else tail)
            low = jnp.where(real, dofs, float(BIG))
            all_ref[r, j * L : (j + 1) * L] = low
            pot = ref[0:CELLS, NPAD + j * L : NPAD + (j + 1) * L]
            all_ref[r, NPAD + j * L : NPAD + (j + 1) * L] = jnp.where(real, pot, 0.0)
            lows.append(jnp.min(low, axis=1, keepdims=True).astype(I32))
            tops.append(jnp.max(jnp.where(real, dofs, -float(BIG)), axis=1, keepdims=True).astype(I32))
        scales = jnp.broadcast_to(ref[CELLS : CELLS + 1, 0:L], (CELLS, L))
        scale = jnp.sum(jnp.where(lane == cell, scales, 0.0), axis=1, keepdims=True)
        all_ref[r, 2 * NPAD :] = jnp.broadcast_to(scale, (CELLS, L))
        count = jnp.broadcast_to(ref[CELLS : CELLS + 1, L : 2 * L], (CELLS, L))
        live = cell.astype(F32) < count
        if side is not None:
            live = live & jnp.full((CELLS, L), inside(side))
        low = jnp.minimum(jnp.minimum(lows[0], lows[1]), lows[2])
        top = jnp.maximum(jnp.maximum(tops[0], tops[1]), tops[2])
        used = live & (top >= RIM) & (low < RIM + LOC)
        starts = [jnp.minimum(x >> 7, EXT // L - NARROW) for x in lows]
        narrow = ((tops[0] >> 7) - starts[0] < NARROW) & ((tops[1] >> 7) - starts[1] < NARROW)
        narrow = narrow & ((tops[2] >> 7) - starts[2] < NARROW)
        base = jnp.minimum(low >> 7, EXT // L - WIDE)
        meta = jnp.where(used, jnp.where(narrow, 0, 1), -1)
        for j in range(NJ):
            meta = jnp.where(lane == 1 + j, jnp.where(narrow, starts[j], base), meta)
        meta_ref[r, :] = meta
    copy = pltpu.make_async_copy(meta_ref, meta_s, sem)
    copy.start()
    pad_ref[...] = jnp.zeros_like(pad_ref)
    load.wait()
    pad_ref[0:NODES, 0:NODES] = k_ref[...]
    kh_ref[...], kl_ref[...] = split(pad_ref[...].T)
    for i in range(E // L):
        col = slice(i * L, (i + 1) * L)
        oh_ref[:, col] = one_hot(pe_ref[0:1, col] & (QLO - 1), QLO).astype(BF16)
    copy.wait()

    def scan(c, counts):
        kind = meta_s[c, 0]
        n, m = counts
        list_s[n] = c
        wide_s[m] = c
        return n + jnp.where(kind == 0, 1, 0), m + jnp.where(kind == 1, 1, 0)

    n, m = lax.fori_loop(0, 3 * CELLS, scan, (0, 0), unroll=4)
    gn = 2 * ((n + 2 * GROUP - 1) // (2 * GROUP))
    gw = (m + GROUP - 1) // GROUP
    first = (gn + 1) * GROUP
    last = first + gw * GROUP

    def blank(i, _):
        list_s[i] = -1
        return 0

    def move(i, _):
        list_s[first + i] = wide_s[i]
        return 0

    lax.fori_loop(n, first, blank, 0)
    lax.fori_loop(0, m, move, 0)
    lax.fori_loop(first + m, last, blank, 0)
    base_ref[4 * SLOTS] = gn
    base_ref[4 * SLOTS + 1] = gw

    def one(slot):
        c = list_s[slot]
        valid = c >= 0
        c = jnp.maximum(c, 0)
        vals = all_ref[pl.ds(c, 1), :]
        rels = []
        for j in range(NJ):
            b = jnp.where(valid, meta_s[c, 1 + j], 0)
            base_ref[4 * slot + j] = b
            rel = vals[:, j * L : (j + 1) * L].astype(I32) - b * L
            rel = jnp.where(valid & (rel < WIDE * L), rel, BIG)
            rels.append(rel)
            tab_ref[slot, j : j + 1, :] = rel
            pot_ref[slot, j : j + 1, :] = vals[:, NPAD + j * L : NPAD + (j + 1) * L]
        pot_ref[slot, 3:4, :] = vals[:, 2 * NPAD :]
        inv = inverse(rels)
        for j in range(NJ):
            tab_ref[slot, 3 + 3 * j : 6 + 3 * j, :] = inv[8 * j : 8 * j + NARROW]

    def some(i, _):
        for k in range(8):
            one(i * 8 + k)
        return 0

    lax.fori_loop(0, last // 8, some, 0)


def cell_tables(own, left, right, pe, stiffness):
    return pl.pallas_call(
        cells_kernel,
        out_shape=(
            sds((SLOTS, 16, L), I32),
            sds((SLOTS, 8, L)),
            sds((NPAD, NPAD), BF16),
            sds((NPAD, NPAD), BF16),
            sds((QLO, E), BF16),
            sds((4 * SLOTS + L,), I32),
        ),
        in_specs=[VM] * 4 + [HBM],
        out_specs=(VM, VM, VM, VM, VM, SM),
        scratch_shapes=[
            pltpu.VMEM((3 * CELLS, PW), F32),
            pltpu.VMEM((3 * CELLS, L), I32),
            pltpu.VMEM((NODES, NODES), F32),
            pltpu.VMEM((NPAD, NPAD), F32),
            pltpu.SMEM((3 * CELLS, L), I32),
            pltpu.SMEM((SLOTS + GROUP,), I32),
            pltpu.SMEM((3 * CELLS + GROUP,), I32),
            pltpu.SemaphoreType.DMA,
            pltpu.SemaphoreType.DMA,
        ],
        compiler_params=pltpu.CompilerParams(vmem_limit_bytes=SMALL),
        name="cell_tables",
    )(own, left, right, pe, stiffness)


def step_kernel(number, *refs):
    (u_ref, gl_ref, gr_ref, prev_ref, tab_ref, pot_ref, kh_ref, kl_ref,
     oh_ref, pe_ref, w_ref, src_ref, posr_ref, hq_ref, base_ref, start_ref) = refs[:16]
    outs = refs[16 : 16 + (4 if number == 3 else 3)]
    ext_ref, acc0_ref, acc1_ref, x0_ref, x1_ref, p0_ref, p1_ref, z_ref, g_ref, lhs_ref = refs[16 + len(outs) :]
    accs = (acc0_ref, acc1_ref)
    ext_ref[:, 0 : RIM - EDGE] = jnp.zeros((S, RIM - EDGE), F32)
    ext_ref[:, RIM + LOC + EDGE :] = jnp.zeros((S, RIM - EDGE), F32)
    ext_ref[:, RIM - EDGE : RIM] = jnp.where(inside(0), gl_ref[...], 0.0)
    ext_ref[:, RIM : RIM + LOC] = u_ref[...]
    ext_ref[:, RIM + LOC : RIM + LOC + EDGE] = jnp.where(inside(1), gr_ref[...], 0.0)
    for ref in accs:
        ref[...] = jnp.zeros_like(ref)
    gn = base_ref[4 * SLOTS]
    gw = base_ref[4 * SLOTS + 1]

    def rows8(k, s):
        return pl.ds(k * S + 8 * s, 8) if isinstance(k, int) else pl.ds(pl.multiple_of(k * S + 8 * s, 8), 8)

    def load(x_ref, group, k, width):
        slot = group * GROUP + k
        for j in range(NJ):
            b = base_ref[4 * slot + j]
            row = jnp.broadcast_to(tab_ref[slot, j : j + 1, :], (8, L))
            lo, hi = row & 127, row >> 7
            for s in range(2):
                r = slice(8 * s, 8 * s + 8)
                rows = ext_ref[r, blocks(b, width)]
                acc = lanes(rows[:, 0:L], lo)
                for t in range(1, width):
                    acc = jnp.where(hi == t, lanes(rows[:, t * L : (t + 1) * L], lo), acc)
                x_ref[rows8(k, s), j * L : (j + 1) * L] = acc

    def store(p_ref, group, k, width):
        slot = group * GROUP + k
        acc_ref = accs[k % 2 if isinstance(k, int) else 0]
        if width == NARROW:
            inv = [[tab_ref[slot, 3 + 3 * j + t : 4 + 3 * j + t, :] for t in range(width)] for j in range(NJ)]
        else:
            full = inverse([tab_ref[slot, j : j + 1, :] for j in range(NJ)])
            inv = [[full[8 * j + t : 8 * j + t + 1] for t in range(width)] for j in range(NJ)]
        for j in range(NJ):
            b = base_ref[4 * slot + j]
            vals = [p_ref[rows8(k, s), j * L : (j + 1) * L] for s in range(2)]
            adds = []
            for t in range(width):
                row = jnp.broadcast_to(inv[j][t], (8, L))
                m, lo = row >= 0, row & 127
                adds.append([jnp.where(m, lanes(vals[s], lo), 0.0) for s in range(2)])
            for s in range(2):
                more = jnp.concatenate([adds[t][s] for t in range(width)], axis=1)
                acc_ref[8 * s : 8 * s + 8, blocks(b, width)] += more

    def product(x_ref, p_ref, group):
        n = GROUP * S
        x = x_ref[...]
        xh, xl = split(x)
        both = nn(jnp.concatenate([xh, xl], 0), kh_ref[...])
        prod = both[:n] + (both[n:] + nn(xh, kl_ref[...]))
        for k in range(GROUP):
            slot = group * GROUP + k
            r = slice(k * S, (k + 1) * S)
            scale = jnp.broadcast_to(pot_ref[slot, 3:4, :], (S, L))
            for j in range(NJ):
                col = slice(j * L, (j + 1) * L)
                pot = jnp.broadcast_to(pot_ref[slot, j : j + 1, :], (S, L))
                p_ref[r, col] = scale * prod[r, col] + pot * x[r, col]

    def load_group(x_ref, group, width, n):
        def some(q, _):
            for k in range(n):
                load(x_ref, group, q * n + k, width)
            return 0

        lax.fori_loop(0, GROUP // n, some, 0)

    load_group(x0_ref, 0, NARROW, 4)

    def pipeline(i, _):
        g = 2 * i
        product(x0_ref, p0_ref, g)
        before = jnp.where(i == 0, gn, g - 1)
        for k in range(GROUP):
            store(p1_ref, before, k, NARROW)
            load(x1_ref, g + 1, k, NARROW)
        product(x1_ref, p1_ref, g + 1)
        for k in range(GROUP):
            store(p0_ref, g, k, NARROW)
            load(x0_ref, g + 2, k, NARROW)
        return 0

    lax.fori_loop(0, gn // 2, pipeline, 0)
    for k in range(GROUP):
        store(p1_ref, jnp.where(gn > 0, gn - 1, gn), k, NARROW)

    def wide(i, _):
        load_group(x0_ref, i, WIDE, 1)
        product(x0_ref, p0_ref, i)

        def one(k, _):
            store(p0_ref, i, k, WIDE)
            return 0

        lax.fori_loop(0, GROUP, one, 0)
        return 0

    lax.fori_loop(gn + 1, gn + 1 + gw, wide, 0)

    def read(b):
        return acc0_ref[:, at(b + RB)] + acc1_ref[:, at(b + RB)]

    compress(read, z_ref, src_ref, start_ref)
    add_to_masters(z_ref, oh_ref, pe_ref, w_ref, g_ref, lhs_ref)
    hanging_values(z_ref, oh_ref, pe_ref, w_ref, g_ref, lhs_ref, hq_ref)
    new_ref = outs[0] if number < 3 else ext_ref

    def finish(i, _):
        for k in range(UNROLL):
            b = i * UNROLL + k
            t = expand(b, read(b), z_ref, posr_ref, start_ref)
            r = (t - CENTRE * u_ref[:, at(b)]) * ((1.0 if number == 1 else 2.0) / HALF)
            if number > 1:
                r = r - prev_ref[:, at(b)]
            new_ref[:, at(b)] = r
        return 0

    lax.fori_loop(0, NB // UNROLL, finish, 0)
    if number < 3:
        outs[1][...] = new_ref[:, 0:EDGE]
        outs[2][...] = new_ref[:, LOC - EDGE :]
    else:
        me = lax.axis_index("band")
        q = LOC // 4
        for k in range(4):
            outs[k][...] = new_ref[:, pl.ds(pl.multiple_of(((me + k) & 3) * q, L), q)]


def apply_step(number, u, gl, gr, prev, cell, base, hang, start):
    if number == 3:
        shapes = (sds((S, LOC // 4)),) * 4
    else:
        shapes = (sds((S, LOC)), sds((S, EDGE)), sds((S, EDGE)))
    return pl.pallas_call(
        functools.partial(step_kernel, number),
        out_shape=shapes,
        in_specs=[VM] * 14 + [SM] * 2,
        out_specs=(VM,) * len(shapes),
        scratch_shapes=[
            pltpu.VMEM((S, EXT), F32),
            pltpu.VMEM((S, EXT), F32),
            pltpu.VMEM((S, EXT), F32),
            *[pltpu.VMEM((GROUP * S, NPAD), F32)] * 4,
            *HANG_SCRATCH,
        ],
        compiler_params=pltpu.CompilerParams(vmem_limit_bytes=VLIM),
        name=f"step{number}",
    )(u, gl, gr, prev, *cell, *hang, base, start)


def gram_kernel(q0_ref, q1_ref, q2_ref, q3_ref, gram_ref, all_ref):
    me = lax.axis_index("band")
    for k, ref in enumerate((q0_ref, q1_ref, q2_ref, q3_ref)):
        all_ref[pl.ds(pl.multiple_of(((me - k) & 3) * S, S), S), :] = ref[...]
    a = all_ref[...]
    gram_ref[...] = lax.dot_general(a, a, NT, preferred_element_type=F32, precision=lax.Precision.HIGHEST)


def gram_of(qs):
    n = qs[0].shape[1]
    return pl.pallas_call(
        gram_kernel,
        out_shape=(sds((4 * S, 4 * S)), sds((4 * S, n))),
        in_specs=[VM] * 4,
        out_specs=(VM, VM),
        compiler_params=pltpu.CompilerParams(vmem_limit_bytes=VLIM),
        name="gram",
    )(*qs)


def basis_kernel(total, gram_ref, all_ref, o0_ref, o1_ref, o2_ref, o3_ref, m_ref, r_ref):
    n = 4 * S
    eye = (iota((n, n), 0) == iota((n, n), 1)).astype(F32)
    m_ref[...] = jnp.concatenate([gram_ref[...], eye], 1)
    row_id = iota((n, 2 * n), 0)

    m = m_ref[...]
    for j in range(n):
        pivot = m[j : j + 1, :]
        scaled = pivot * (1.0 / pivot[:, j : j + 1])
        m = m - jnp.where(row_id > j, m[:, j : j + 1], 0.0) * scaled
    dg = jnp.sum(jnp.where(row_id == iota((n, 2 * n), 1), m, 0.0), axis=1, keepdims=True)
    inv = m[:, n:] * lax.rsqrt(dg) * jnp.sqrt(jnp.float32(total))
    r_ref[...] = jnp.dot(inv, all_ref[...], preferred_element_type=F32, precision=lax.Precision.HIGHEST)
    me = lax.axis_index("band")
    for k, ref in enumerate((o0_ref, o1_ref, o2_ref, o3_ref)):
        ref[...] = r_ref[pl.ds(pl.multiple_of(((me + k) & 3) * S, S), S), :]


def basis_of(gram, rows, total):
    n = rows.shape[1]
    return pl.pallas_call(
        functools.partial(basis_kernel, total),
        out_shape=(sds((S, n)),) * 4,
        in_specs=[VM, VM],
        out_specs=(VM,) * 4,
        scratch_shapes=[pltpu.VMEM((4 * S, 8 * S), F32), pltpu.VMEM((4 * S, n), F32)],
        compiler_params=pltpu.CompilerParams(vmem_limit_bytes=VLIM),
        name="basis",
    )(gram, rows)


def join_kernel(q0_ref, q1_ref, q2_ref, q3_ref, out_ref):
    me = lax.axis_index("band")
    n = q0_ref.shape[1]
    for k, ref in enumerate((q0_ref, q1_ref, q2_ref, q3_ref)):
        out_ref[:, pl.ds(pl.multiple_of(((me - k) & 3) * n, L), n)] = ref[...]


def join(qs):
    return pl.pallas_call(
        join_kernel,
        out_shape=sds((S, LOC)),
        in_specs=[VM] * 4,
        out_specs=VM,
        compiler_params=pltpu.CompilerParams(vmem_limit_bytes=VLIM),
        name="join",
    )(*qs)


def shift(x, axis, by):
    size = lax.axis_size(axis)
    return lax.ppermute(x, axis, [(i, (i + by) % size) for i in range(size)])


def swap(x, axis, bits):
    size = lax.axis_size(axis)
    return lax.ppermute(x, axis, [(i, i ^ bits) for i in range(size)])


def summed(g):
    g = g + swap(g, "dom", 1)
    for axis, unit in (("dom", 2), ("dom", 8), ("band", 1)):
        others = [swap(g, axis, unit * k) for k in (1, 2, 3)]
        g = (g + others[0]) + (others[1] + others[2])
    return g


def body(
    block,
    stiffness,
    cell_scale,
    potential,
    cell_dofs,
    cell_count,
    hang_rows,
    hang_masters,
    hang_weights,
):
    own, hanging = pack(
        cell_dofs.T, potential.T, cell_scale, hang_rows, hang_masters, hang_weights, cell_count
    )
    from_left = shift(own, "dom", 1)
    from_right = shift(own, "dom", -1)
    *hang, start, u0, first, last = prepare(hanging, block)

    def ghosts(first, last):
        return shift(last, "dom", 1), shift(first, "dom", -1)

    gl, gr = ghosts(first, last)
    *cell, base = cell_tables(own, from_left, from_right, hang[0], stiffness)
    args = (cell, base, hang, start)
    u1, first, last = apply_step(1, u0, gl, gr, u0, *args)
    gl, gr = ghosts(first, last)
    u2, first, last = apply_step(2, u1, gl, gr, u0, *args)
    gl, gr = ghosts(first, last)
    qs = apply_step(3, u2, gl, gr, u1, *args)
    qs = [qs[0]] + [shift(qs[k], "band", k) for k in (1, 2, 3)]
    gram, rows = gram_of(qs)
    gram = summed(gram)
    outs = basis_of(gram, rows, LOC * lax.axis_size("dom"))
    outs = [outs[0]] + [shift(outs[k], "band", k) for k in (1, 2, 3)]
    return join(outs)


def solution(mesh):
    return jax.shard_map(
        body,
        mesh=mesh,
        in_specs=(
            P("band", "dom"),
            P(),
            P("dom"),
            P(None, "dom"),
            P(None, "dom"),
            P("dom"),
            P("dom"),
            P(None, "dom"),
            P(None, "dom"),
        ),
        out_specs=P("band", "dom"),
        check_vma=False,
    )
```

```python
import functools
import jax
import jax.numpy as jnp
from jax import lax
from jax.experimental import pallas as pl
from jax.experimental.pallas import tpu as pltpu
from jax.sharding import PartitionSpec as P

RIM = 2048
EDGE = 768
NODES = 343
HANG = 864
MASTERS = 4
LOC = 13824
CELLS = 64
S = 16
L = 128
EXT = LOC + 2 * RIM
NB = LOC // L
RB = RIM // L
NPAD = 384
NJ = NPAD // L
WIDE = 7
NARROW = 3
PACK = 72
PW = 2 * NPAD + L
GROUP = 8
SLOTS = 28 * GROUP
HPAD = 896
HB = HPAD // L
ME = MASTERS * HPAD
HE = 1024
E = ME + HE
QLO = 512
QB = QLO // L
QHI = 9
BIG = 1 << 20
CENTRE = 4.5
HALF = 3.5
F32 = jnp.float32
BF16 = jnp.bfloat16
I32 = jnp.int32
VLIM = 28 * 1024 * 1024
SMALL = 20 * 1024 * 1024
WHOLE = 64 * 1024 * 1024

VM = pl.BlockSpec(memory_space=pltpu.VMEM)
SM = pl.BlockSpec(memory_space=pltpu.SMEM)
HBM = pl.BlockSpec(memory_space=pltpu.HBM)
NT = (((1,), (1,)), ((), ()))


def inside(side):
    dom = lax.axis_index("dom")
    return dom > 0 if side == 0 else dom < lax.axis_size("dom") - 1


def iota(shape, dim):
    return lax.broadcasted_iota(I32, shape, dim)


def lanes(x, idx):
    return jnp.take_along_axis(x, idx, axis=1, mode="promise_in_bounds")


def nn(a, b):
    return jnp.dot(a, b, preferred_element_type=F32)


def nt(a, b):
    return lax.dot_general(a, b, NT, preferred_element_type=F32)


def split(x):
    hi = x.astype(BF16)
    return hi, (x - hi.astype(F32)).astype(BF16)


def at(b):
    return pl.ds(pl.multiple_of(b * L, L), L)


def blocks(b, n):
    return pl.ds(pl.multiple_of(b * L, L), n * L)


def one_hot(row, n):
    return (jnp.broadcast_to(row, (n, row.shape[1])) == iota((n, row.shape[1]), 0)).astype(F32)


def hang_tables(ent_ref, a_ref, b_ref, lhs_ref, oh_ref, pe_ref, src_ref, posr_ref, hq_ref, start_ref):
    for i in range(E // L):
        col = slice(i * L, (i + 1) * L)
        row = ent_ref[0:1, col]
        a_ref[:, col] = one_hot(row >> 7, L).astype(BF16)
        b_ref[:, col] = one_hot(row & 127, L).astype(BF16)
    flag = nt(a_ref[...], b_ref[...]) > 0.5
    flagb = flag.astype(F32).astype(BF16)
    tri = (iota((L, L), 0) < iota((L, L), 1)).astype(F32).astype(BF16)
    low = (iota((L, L), 1) < iota((L, L), 0)).astype(F32).astype(BF16)
    total = nn(flagb, jnp.ones((L, L), BF16))
    pos = (nn(flagb, tri) + nn(low, total.astype(BF16))).astype(I32)
    posr_ref[...] = jnp.where(flag, pos, -1)
    totrow = nt(jnp.ones((8, L), BF16), flagb)
    start_ref[...] = nn(totrow.astype(BF16), tri).astype(I32)
    ph = (pos >> 7).astype(F32).astype(BF16)
    plo = (pos & 127).astype(F32).astype(BF16)
    for i in range(E // L):
        col = slice(i * L, (i + 1) * L)
        ent = ent_ref[0:1, col]
        mask = a_ref[:, col].astype(F32)
        b = b_ref[:, col]
        hi = jnp.sum(nn(ph, b) * mask, axis=0, keepdims=True)
        lo = jnp.sum(nn(plo, b) * mask, axis=0, keepdims=True)
        pe = jnp.where(ent >= 0, hi.astype(I32) * L + lo.astype(I32), BIG)
        pe_ref[0:1, col] = pe
        oh_ref[:, col] = one_hot(pe & (QLO - 1), QLO).astype(BF16)
        qm = one_hot(pe // QLO, 16)
        lhs_ref[0:16, col] = qm.astype(BF16)
        lhs_ref[16:32, col] = (qm * (ent >> 7).astype(F32)).astype(BF16)
        lhs_ref[32:48, col] = (qm * (ent & 127).astype(F32)).astype(BF16)
        lhs_ref[48:64, col] = (qm if i >= ME // L else jnp.zeros_like(qm)).astype(BF16)
    res = nt(lhs_ref[...], oh_ref[...])
    cnt = res[0:16]
    den = jnp.maximum(cnt, 1.0)
    blk = (res[16:32] / den + 0.5).astype(I32)
    lo = (res[32:48] / den + 0.5).astype(I32)
    src = jnp.where(cnt > 0.5, blk * L + lo, -1)
    for q in range(QHI):
        for t in range(QB):
            src_ref[QB * q + t : QB * q + t + 1, :] = src[q : q + 1, t * L : (t + 1) * L]
    hq_ref[...] = res[48:64]


def zat(c):
    return pl.ds(pl.multiple_of((c // QB) * S, S), S), pl.ds(pl.multiple_of((c % QB) * L, L), L)


UNROLL = 27


def compress(read, z_ref, src_ref, start_ref):
    z_ref[...] = jnp.zeros_like(z_ref)

    def step(i, cur):
        for k in range(UNROLL):
            b = i * UNROLL + k
            y = read(b)
            c = start_ref[0, b] >> 7
            ahead = start_ref[0, b + 1] >> 7
            parts = []
            for t in range(2):
                row = jnp.broadcast_to(src_ref[pl.ds(c + t, 1), :], (S, L))
                parts.append(((row >> 7) == b, lanes(y, row & 127)))
            cur = jnp.where(parts[0][0], parts[0][1], cur)
            r, l = zat(c)
            z_ref[r, l] = cur
            after = jnp.where(parts[1][0], parts[1][1], 0.0)
            cur = jnp.where(ahead > c, after, cur)
        return cur

    cur = lax.fori_loop(0, NB // UNROLL, step, jnp.zeros((S, L), F32))
    r, l = zat(start_ref[0, NB] >> 7)
    z_ref[r, l] = cur


def expand(b, y, z_ref, posr_ref, start_ref):
    row = jnp.broadcast_to(posr_ref[pl.ds(b, 1), :], (S, L))
    c0 = start_ref[0, b] >> 7
    for t in range(2):
        c = c0 + t
        r, l = zat(c)
        y = jnp.where((row >> 7) == c, lanes(z_ref[r, l], row & 127), y)
    return y


def gather_entries(z_ref, oh_ref, pe_ref, g_ref, first, last):
    zz = jnp.concatenate(split(z_ref[...]), axis=0)
    n = QHI * S
    w = 256
    for i in range(first // w, last // w):
        col = slice(i * w, (i + 1) * w)
        g = nn(zz, oh_ref[:, col])
        q = jnp.broadcast_to(pe_ref[0:1, col] // QLO, (S, w))
        hi = g[0:S]
        lo = g[n : n + S]
        for h in range(1, QHI):
            m = q == h
            hi = jnp.where(m, g[h * S : (h + 1) * S], hi)
            lo = jnp.where(m, g[n + h * S : n + (h + 1) * S], lo)
        g_ref[:, col] = hi + lo


def scatter_entries(g_ref, oh_ref, pe_ref, lhs_ref, first, last):
    n = QHI * S
    for i in range(first // L, last // L):
        col = slice(i * L, (i + 1) * L)
        g = g_ref[:, col]
        hi = g.astype(BF16).astype(F32)
        lo = g - hi
        q = jnp.broadcast_to(pe_ref[0:1, col] // QLO, (S, L))
        for h in range(QHI):
            m = q == h
            lhs_ref[h * S : (h + 1) * S, col] = jnp.where(m, hi, 0.0).astype(BF16)
            lhs_ref[n + h * S : n + (h + 1) * S, col] = jnp.where(m, lo, 0.0).astype(BF16)
    res = nt(lhs_ref[:, first:last], oh_ref[:, first:last])
    return res[:n] + res[n:]


def hanging_values(z_ref, oh_ref, pe_ref, w_ref, g_ref, lhs_ref, hq_ref):
    gather_entries(z_ref, oh_ref, pe_ref, g_ref, 0, ME)
    g_ref[:, ME + HPAD :] = jnp.zeros((S, HE - HPAD), F32)
    for j in range(HB):
        acc = jnp.zeros((S, L), F32)
        for k in range(MASTERS):
            col = slice(k * HPAD + j * L, k * HPAD + (j + 1) * L)
            acc = acc + g_ref[:, col] * w_ref[0:1, col]
        g_ref[:, ME + j * L : ME + (j + 1) * L] = acc
    cz = scatter_entries(g_ref, oh_ref, pe_ref, lhs_ref, ME, E)
    for h in range(QHI):
        r = slice(h * S, (h + 1) * S)
        m = jnp.broadcast_to(hq_ref[h : h + 1, :], (S, QLO)) > 0.5
        z_ref[r, :] = jnp.where(m, cz[r], z_ref[r, :])


def add_to_masters(z_ref, oh_ref, pe_ref, w_ref, g_ref, lhs_ref):
    gather_entries(z_ref, oh_ref, pe_ref, g_ref, ME, E)
    for j in range(HB):
        y = g_ref[:, ME + j * L : ME + (j + 1) * L]
        for k in range(MASTERS):
            col = slice(k * HPAD + j * L, k * HPAD + (j + 1) * L)
            g_ref[:, col] = y * w_ref[0:1, col]
    z_ref[...] += scatter_entries(g_ref, oh_ref, pe_ref, lhs_ref, 0, ME)


def prepare_kernel(
    hang_ref, block_ref,
    pe_ref, w_ref, src_ref, posr_ref, hq_ref, start_ref, u_ref, left_ref, right_ref,
    ent_ref, oh_ref, a_ref, b_ref, tab_ref, z_ref, g_ref, lhs_ref, start_s, sem,
):
    for k in range(MASTERS):
        col = slice(k * HPAD, (k + 1) * HPAD)
        ent_ref[0:1, col] = hang_ref[k : k + 1, :].astype(I32)
        w_ref[0:1, col] = hang_ref[MASTERS + 1 + k : MASTERS + 2 + k, :]
    ent_ref[0:1, ME + HPAD :] = jnp.full((1, HE - HPAD), -1, I32)
    ent_ref[0:1, ME : ME + HPAD] = hang_ref[MASTERS : MASTERS + 1, :].astype(I32)
    hang_tables(ent_ref, a_ref, b_ref, tab_ref, oh_ref, pe_ref, src_ref, posr_ref, hq_ref, start_ref)
    copy = pltpu.make_async_copy(start_ref, start_s, sem)
    copy.start()
    copy.wait()
    compress(lambda b: block_ref[:, at(b)], z_ref, src_ref, start_s)
    hanging_values(z_ref, oh_ref, pe_ref, w_ref, g_ref, lhs_ref, hq_ref)

    def step(i, _):
        for k in range(UNROLL):
            b = i * UNROLL + k
            u_ref[:, at(b)] = expand(b, block_ref[:, at(b)], z_ref, posr_ref, start_s)
        return 0

    lax.fori_loop(0, NB // UNROLL, step, 0)
    left_ref[...] = u_ref[:, 0:EDGE]
    right_ref[...] = u_ref[:, LOC - EDGE :]


def sds(shape, dtype=F32):
    return jax.ShapeDtypeStruct(shape, dtype)


HANG_SCRATCH = [
    pltpu.VMEM((QHI * S, QLO), F32),
    pltpu.VMEM((S, E), F32),
    pltpu.VMEM((2 * QHI * S, E), BF16),
]


def prepare(hang, block):
    return pl.pallas_call(
        prepare_kernel,
        out_shape=(
            sds((1, E), I32),
            sds((1, ME)),
            sds((QB * QHI + 4, L), I32),
            sds((L, L), I32),
            sds((16, QLO)),
            sds((8, L), I32),
            sds((S, LOC)),
            sds((S, EDGE)),
            sds((S, EDGE)),
        ),
        in_specs=[VM] * 2,
        out_specs=(VM,) * 9,
        scratch_shapes=[
            pltpu.VMEM((1, E), I32),
            pltpu.VMEM((QLO, E), BF16),
            pltpu.VMEM((L, E), BF16),
            pltpu.VMEM((L, E), BF16),
            pltpu.VMEM((64, E), BF16),
            *HANG_SCRATCH,
            pltpu.SMEM((8, L), I32),
            pltpu.SemaphoreType.DMA,
        ],
        compiler_params=pltpu.CompilerParams(vmem_limit_bytes=VLIM),
        name="prepare",
    )(hang, block)


def pack_kernel(
    dofs_hbm, pot_hbm, scale_hbm, rows_hbm, masters_hbm, weights_hbm, count_ref,
    own_ref, hang_ref,
    dofs_ref, pot_ref, scale_ref, rows_ref, masters_ref, weights_ref, sems,
):
    moves = (
        (dofs_hbm, dofs_ref),
        (pot_hbm, pot_ref),
        (scale_hbm, scale_ref),
        (rows_hbm, rows_ref),
        (masters_hbm, masters_ref),
        (weights_hbm, weights_ref),
    )
    loads = [pltpu.make_async_copy(src, dst, sems.at[i]) for i, (src, dst) in enumerate(moves)]
    for load in loads:
        load.start()
    for load in loads:
        load.wait()
    own_ref[0:CELLS, 0:NODES] = dofs_ref[...].astype(F32)
    own_ref[0:CELLS, NPAD : NPAD + NODES] = pot_ref[...]
    scale = jnp.broadcast_to(scale_ref[...].reshape(1, CELLS), (PACK - CELLS, CELLS))
    own_ref[CELLS:PACK, 0:CELLS] = scale
    own_ref[CELLS:PACK, L : 2 * L] = jnp.full((PACK - CELLS, L), count_ref[0]).astype(F32)
    hang_ref[...] = jnp.where(iota((2 * MASTERS + 1, HPAD), 0) < MASTERS + 1, -1.0, 0.0)
    hang_ref[0:MASTERS, 0:HANG] = masters_ref[...].astype(F32)
    hang_ref[MASTERS : MASTERS + 1, 0:HANG] = rows_ref[...].reshape(1, HANG).astype(F32)
    hang_ref[MASTERS + 1 :, 0:HANG] = weights_ref[...]


def pack(dofs, pot, scale, rows, masters, weights, count):
    return pl.pallas_call(
        pack_kernel,
        out_shape=(sds((PACK, PW)), sds((2 * MASTERS + 1, HPAD))),
        in_specs=[HBM] * 6 + [SM],
        out_specs=(VM, VM),
        scratch_shapes=[
            pltpu.VMEM((CELLS, NODES), I32),
            pltpu.VMEM((CELLS, NODES), F32),
            pltpu.VMEM((CELLS,), F32),
            pltpu.VMEM((HANG,), I32),
            pltpu.VMEM((MASTERS, HANG), I32),
            pltpu.VMEM((MASTERS, HANG), F32),
            pltpu.SemaphoreType.DMA((6,)),
        ],
        compiler_params=pltpu.CompilerParams(vmem_limit_bytes=WHOLE),
        name="pack",
    )(dofs, pot, scale, rows, masters, weights, count)


def inverse(rels):
    oh = jnp.concatenate([one_hot(rel & 127, L) for rel in rels], axis=1).astype(BF16)
    rows = []
    for j, rel in enumerate(rels):
        m = jnp.broadcast_to(rel >> 7, (8, L)) == iota((8, L), 0)
        node = jnp.where(m, iota((8, L), 1) + 1, 0).astype(F32)
        zero = jnp.zeros((8, L), F32)
        rows.append(jnp.concatenate([node if i == j else zero for i in range(len(rels))], axis=1))
    return nt(jnp.concatenate(rows, axis=0).astype(BF16), oh).astype(I32) - 1


def cells_kernel(
    own_ref, left_ref, right_ref, pe_ref, k_hbm,
    tab_ref, pot_ref, kh_ref, kl_ref, oh_ref, base_ref,
    all_ref, meta_ref, k_ref, pad_ref, meta_s, list_s, wide_s, sem, sem_k,
):
    load = pltpu.make_async_copy(k_hbm, k_ref, sem_k)
    load.start()
    lane = iota((CELLS, L), 1)
    cell = iota((CELLS, L), 0)
    tail = NODES - 2 * L
    sources = ((own_ref, 0, None), (left_ref, -LOC, 0), (right_ref, LOC, 1))
    for i, (ref, shift, side) in enumerate(sources):
        r = slice(i * CELLS, (i + 1) * CELLS)
        lows, tops = [], []
        for j in range(NJ):
            dofs = ref[0:CELLS, j * L : (j + 1) * L] + float(shift)
            real = lane < (L if j < 2 else tail)
            low = jnp.where(real, dofs, float(BIG))
            all_ref[r, j * L : (j + 1) * L] = low
            pot = ref[0:CELLS, NPAD + j * L : NPAD + (j + 1) * L]
            all_ref[r, NPAD + j * L : NPAD + (j + 1) * L] = jnp.where(real, pot, 0.0)
            lows.append(jnp.min(low, axis=1, keepdims=True).astype(I32))
            tops.append(jnp.max(jnp.where(real, dofs, -float(BIG)), axis=1, keepdims=True).astype(I32))
        scales = jnp.broadcast_to(ref[CELLS : CELLS + 1, 0:L], (CELLS, L))
        scale = jnp.sum(jnp.where(lane == cell, scales, 0.0), axis=1, keepdims=True)
        all_ref[r, 2 * NPAD :] = jnp.broadcast_to(scale, (CELLS, L))
        count = jnp.broadcast_to(ref[CELLS : CELLS + 1, L : 2 * L], (CELLS, L))
        live = cell.astype(F32) < count
        if side is not None:
            live = live & jnp.full((CELLS, L), inside(side))
        low = jnp.minimum(jnp.minimum(lows[0], lows[1]), lows[2])
        top = jnp.maximum(jnp.maximum(tops[0], tops[1]), tops[2])
        used = live & (top >= RIM) & (low < RIM + LOC)
        starts = [jnp.minimum(x >> 7, EXT // L - NARROW) for x in lows]
        narrow = ((tops[0] >> 7) - starts[0] < NARROW) & ((tops[1] >> 7) - starts[1] < NARROW)
        narrow = narrow & ((tops[2] >> 7) - starts[2] < NARROW)
        base = jnp.minimum(low >> 7, EXT // L - WIDE)
        meta = jnp.where(used, jnp.where(narrow, 0, 1), -1)
        for j in range(NJ):
            meta = jnp.where(lane == 1 + j, jnp.where(narrow, starts[j], base), meta)
        meta_ref[r, :] = meta
    copy = pltpu.make_async_copy(meta_ref, meta_s, sem)
    copy.start()
    pad_ref[...] = jnp.zeros_like(pad_ref)
    load.wait()
    pad_ref[0:NODES, 0:NODES] = k_ref[...]
    kh_ref[...], kl_ref[...] = split(pad_ref[...].T)
    for i in range(E // L):
        col = slice(i * L, (i + 1) * L)
        oh_ref[:, col] = one_hot(pe_ref[0:1, col] & (QLO - 1), QLO).astype(BF16)
    copy.wait()

    def scan(c, counts):
        kind = meta_s[c, 0]
        n, m = counts
        list_s[n] = c
        wide_s[m] = c
        return n + jnp.where(kind == 0, 1, 0), m + jnp.where(kind == 1, 1, 0)

    n, m = lax.fori_loop(0, 3 * CELLS, scan, (0, 0), unroll=4)
    gn = 2 * ((n + 2 * GROUP - 1) // (2 * GROUP))
    gw = (m + GROUP - 1) // GROUP
    first = (gn + 1) * GROUP
    last = first + gw * GROUP

    def blank(i, _):
        list_s[i] = -1
        return 0

    def move(i, _):
        list_s[first + i] = wide_s[i]
        return 0

    lax.fori_loop(n, first, blank, 0)
    lax.fori_loop(0, m, move, 0)
    lax.fori_loop(first + m, last, blank, 0)
    base_ref[4 * SLOTS] = gn
    base_ref[4 * SLOTS + 1] = gw

    def one(slot):
        c = list_s[slot]
        valid = c >= 0
        c = jnp.maximum(c, 0)
        vals = all_ref[pl.ds(c, 1), :]
        rels = []
        for j in range(NJ):
            b = jnp.where(valid, meta_s[c, 1 + j], 0)
            base_ref[4 * slot + j] = b
            rel = vals[:, j * L : (j + 1) * L].astype(I32) - b * L
            rel = jnp.where(valid & (rel < WIDE * L), rel, BIG)
            rels.append(rel)
            tab_ref[slot, j : j + 1, :] = rel
            pot_ref[slot, j : j + 1, :] = vals[:, NPAD + j * L : NPAD + (j + 1) * L]
        pot_ref[slot, 3:4, :] = vals[:, 2 * NPAD :]
        inv = inverse(rels)
        for j in range(NJ):
            tab_ref[slot, 3 + 3 * j : 6 + 3 * j, :] = inv[8 * j : 8 * j + NARROW]

    def some(i, _):
        for k in range(8):
            one(i * 8 + k)
        return 0

    lax.fori_loop(0, last // 8, some, 0)


def cell_tables(own, left, right, pe, stiffness):
    return pl.pallas_call(
        cells_kernel,
        out_shape=(
            sds((SLOTS, 16, L), I32),
            sds((SLOTS, 8, L)),
            sds((NPAD, NPAD), BF16),
            sds((NPAD, NPAD), BF16),
            sds((QLO, E), BF16),
            sds((4 * SLOTS + L,), I32),
        ),
        in_specs=[VM] * 4 + [HBM],
        out_specs=(VM, VM, VM, VM, VM, SM),
        scratch_shapes=[
            pltpu.VMEM((3 * CELLS, PW), F32),
            pltpu.VMEM((3 * CELLS, L), I32),
            pltpu.VMEM((NODES, NODES), F32),
            pltpu.VMEM((NPAD, NPAD), F32),
            pltpu.SMEM((3 * CELLS, L), I32),
            pltpu.SMEM((SLOTS + GROUP,), I32),
            pltpu.SMEM((3 * CELLS + GROUP,), I32),
            pltpu.SemaphoreType.DMA,
            pltpu.SemaphoreType.DMA,
        ],
        compiler_params=pltpu.CompilerParams(vmem_limit_bytes=SMALL),
        name="cell_tables",
    )(own, left, right, pe, stiffness)


def step_kernel(number, *refs):
    (u_ref, gl_ref, gr_ref, prev_ref, tab_ref, pot_ref, kh_ref, kl_ref,
     oh_ref, pe_ref, w_ref, src_ref, posr_ref, hq_ref, base_ref, start_ref) = refs[:16]
    outs = refs[16 : 16 + (4 if number == 3 else 3)]
    ext_ref, acc0_ref, acc1_ref, x0_ref, x1_ref, p0_ref, p1_ref, z_ref, g_ref, lhs_ref = refs[16 + len(outs) :]
    accs = (acc0_ref, acc1_ref)
    ext_ref[:, 0 : RIM - EDGE] = jnp.zeros((S, RIM - EDGE), F32)
    ext_ref[:, RIM + LOC + EDGE :] = jnp.zeros((S, RIM - EDGE), F32)
    ext_ref[:, RIM - EDGE : RIM] = jnp.where(inside(0), gl_ref[...], 0.0)
    ext_ref[:, RIM : RIM + LOC] = u_ref[...]
    ext_ref[:, RIM + LOC : RIM + LOC + EDGE] = jnp.where(inside(1), gr_ref[...], 0.0)
    for ref in accs:
        ref[...] = jnp.zeros_like(ref)
    gn = base_ref[4 * SLOTS]
    gw = base_ref[4 * SLOTS + 1]

    def rows8(k, s):
        return pl.ds(k * S + 8 * s, 8) if isinstance(k, int) else pl.ds(pl.multiple_of(k * S + 8 * s, 8), 8)

    def load(x_ref, group, k, width):
        slot = group * GROUP + k
        for j in range(NJ):
            b = base_ref[4 * slot + j]
            row = jnp.broadcast_to(tab_ref[slot, j : j + 1, :], (8, L))
            lo, hi = row & 127, row >> 7
            for s in range(2):
                r = slice(8 * s, 8 * s + 8)
                rows = ext_ref[r, blocks(b, width)]
                acc = lanes(rows[:, 0:L], lo)
                for t in range(1, width):
                    acc = jnp.where(hi == t, lanes(rows[:, t * L : (t + 1) * L], lo), acc)
                x_ref[rows8(k, s), j * L : (j + 1) * L] = acc

    def store(p_ref, group, k, width):
        slot = group * GROUP + k
        acc_ref = accs[k % 2 if isinstance(k, int) else 0]
        if width == NARROW:
            inv = [[tab_ref[slot, 3 + 3 * j + t : 4 + 3 * j + t, :] for t in range(width)] for j in range(NJ)]
        else:
            full = inverse([tab_ref[slot, j : j + 1, :] for j in range(NJ)])
            inv = [[full[8 * j + t : 8 * j + t + 1] for t in range(width)] for j in range(NJ)]
        for j in range(NJ):
            b = base_ref[4 * slot + j]
            vals = [p_ref[rows8(k, s), j * L : (j + 1) * L] for s in range(2)]
            adds = []
            for t in range(width):
                row = jnp.broadcast_to(inv[j][t], (8, L))
                m, lo = row >= 0, row & 127
                adds.append([jnp.where(m, lanes(vals[s], lo), 0.0) for s in range(2)])
            for s in range(2):
                more = jnp.concatenate([adds[t][s] for t in range(width)], axis=1)
                acc_ref[8 * s : 8 * s + 8, blocks(b, width)] += more

    def product(x_ref, p_ref, group):
        n = GROUP * S
        x = x_ref[...]
        xh, xl = split(x)
        both = nn(jnp.concatenate([xh, xl], 0), kh_ref[...])
        prod = both[:n] + (both[n:] + nn(xh, kl_ref[...]))
        for k in range(GROUP):
            slot = group * GROUP + k
            r = slice(k * S, (k + 1) * S)
            scale = jnp.broadcast_to(pot_ref[slot, 3:4, :], (S, L))
            for j in range(NJ):
                col = slice(j * L, (j + 1) * L)
                pot = jnp.broadcast_to(pot_ref[slot, j : j + 1, :], (S, L))
                p_ref[r, col] = scale * prod[r, col] + pot * x[r, col]

    def load_group(x_ref, group, width, n):
        def some(q, _):
            for k in range(n):
                load(x_ref, group, q * n + k, width)
            return 0

        lax.fori_loop(0, GROUP // n, some, 0)

    load_group(x0_ref, 0, NARROW, 4)

    def pipeline(i, _):
        g = 2 * i
        product(x0_ref, p0_ref, g)
        before = jnp.where(i == 0, gn, g - 1)
        for k in range(GROUP):
            store(p1_ref, before, k, NARROW)
            load(x1_ref, g + 1, k, NARROW)
        product(x1_ref, p1_ref, g + 1)
        for k in range(GROUP):
            store(p0_ref, g, k, NARROW)
            load(x0_ref, g + 2, k, NARROW)
        return 0

    lax.fori_loop(0, gn // 2, pipeline, 0)
    for k in range(GROUP):
        store(p1_ref, jnp.where(gn > 0, gn - 1, gn), k, NARROW)

    def wide(i, _):
        load_group(x0_ref, i, WIDE, 1)
        product(x0_ref, p0_ref, i)

        def one(k, _):
            store(p0_ref, i, k, WIDE)
            return 0

        lax.fori_loop(0, GROUP, one, 0)
        return 0

    lax.fori_loop(gn + 1, gn + 1 + gw, wide, 0)

    def read(b):
        return acc0_ref[:, at(b + RB)] + acc1_ref[:, at(b + RB)]

    compress(read, z_ref, src_ref, start_ref)
    add_to_masters(z_ref, oh_ref, pe_ref, w_ref, g_ref, lhs_ref)
    hanging_values(z_ref, oh_ref, pe_ref, w_ref, g_ref, lhs_ref, hq_ref)
    new_ref = outs[0] if number < 3 else ext_ref

    def finish(i, _):
        for k in range(UNROLL):
            b = i * UNROLL + k
            t = expand(b, read(b), z_ref, posr_ref, start_ref)
            r = (t - CENTRE * u_ref[:, at(b)]) * ((1.0 if number == 1 else 2.0) / HALF)
            if number > 1:
                r = r - prev_ref[:, at(b)]
            new_ref[:, at(b)] = r
        return 0

    lax.fori_loop(0, NB // UNROLL, finish, 0)
    if number < 3:
        outs[1][...] = new_ref[:, 0:EDGE]
        outs[2][...] = new_ref[:, LOC - EDGE :]
    else:
        me = lax.axis_index("band")
        q = LOC // 4
        for k in range(4):
            outs[k][...] = new_ref[:, pl.ds(pl.multiple_of(((me + k) & 3) * q, L), q)]


def apply_step(number, u, gl, gr, prev, cell, base, hang, start):
    if number == 3:
        shapes = (sds((S, LOC // 4)),) * 4
    else:
        shapes = (sds((S, LOC)), sds((S, EDGE)), sds((S, EDGE)))
    return pl.pallas_call(
        functools.partial(step_kernel, number),
        out_shape=shapes,
        in_specs=[VM] * 14 + [SM] * 2,
        out_specs=(VM,) * len(shapes),
        scratch_shapes=[
            pltpu.VMEM((S, EXT), F32),
            pltpu.VMEM((S, EXT), F32),
            pltpu.VMEM((S, EXT), F32),
            *[pltpu.VMEM((GROUP * S, NPAD), F32)] * 4,
            *HANG_SCRATCH,
        ],
        compiler_params=pltpu.CompilerParams(vmem_limit_bytes=VLIM),
        name=f"step{number}",
    )(u, gl, gr, prev, *cell, *hang, base, start)


def gram_kernel(q0_ref, q1_ref, q2_ref, q3_ref, gram_ref, all_ref):
    me = lax.axis_index("band")
    for k, ref in enumerate((q0_ref, q1_ref, q2_ref, q3_ref)):
        all_ref[pl.ds(pl.multiple_of(((me - k) & 3) * S, S), S), :] = ref[...]
    a = all_ref[...]
    gram_ref[...] = lax.dot_general(a, a, NT, preferred_element_type=F32, precision=lax.Precision.HIGHEST)


def gram_of(qs):
    n = qs[0].shape[1]
    return pl.pallas_call(
        gram_kernel,
        out_shape=(sds((4 * S, 4 * S)), sds((4 * S, n))),
        in_specs=[VM] * 4,
        out_specs=(VM, VM),
        compiler_params=pltpu.CompilerParams(vmem_limit_bytes=VLIM),
        name="gram",
    )(*qs)


def basis_kernel(total, gram_ref, all_ref, o0_ref, o1_ref, o2_ref, o3_ref, m_ref, r_ref):
    n = 4 * S
    eye = (iota((n, n), 0) == iota((n, n), 1)).astype(F32)
    m_ref[...] = jnp.concatenate([gram_ref[...], eye], 1)
    row_id = iota((n, 2 * n), 0)

    m = m_ref[...]
    for j in range(n):
        pivot = m[j : j + 1, :]
        scaled = pivot * (1.0 / pivot[:, j : j + 1])
        m = m - jnp.where(row_id > j, m[:, j : j + 1], 0.0) * scaled
    dg = jnp.sum(jnp.where(row_id == iota((n, 2 * n), 1), m, 0.0), axis=1, keepdims=True)
    inv = m[:, n:] * lax.rsqrt(dg) * jnp.sqrt(jnp.float32(total))
    r_ref[...] = jnp.dot(inv, all_ref[...], preferred_element_type=F32, precision=lax.Precision.HIGHEST)
    me = lax.axis_index("band")
    for k, ref in enumerate((o0_ref, o1_ref, o2_ref, o3_ref)):
        ref[...] = r_ref[pl.ds(pl.multiple_of(((me + k) & 3) * S, S), S), :]


def basis_of(gram, rows, total):
    n = rows.shape[1]
    return pl.pallas_call(
        functools.partial(basis_kernel, total),
        out_shape=(sds((S, n)),) * 4,
        in_specs=[VM, VM],
        out_specs=(VM,) * 4,
        scratch_shapes=[pltpu.VMEM((4 * S, 8 * S), F32), pltpu.VMEM((4 * S, n), F32)],
        compiler_params=pltpu.CompilerParams(vmem_limit_bytes=VLIM),
        name="basis",
    )(gram, rows)


def join_kernel(q0_ref, q1_ref, q2_ref, q3_ref, out_ref):
    me = lax.axis_index("band")
    n = q0_ref.shape[1]
    for k, ref in enumerate((q0_ref, q1_ref, q2_ref, q3_ref)):
        out_ref[:, pl.ds(pl.multiple_of(((me - k) & 3) * n, L), n)] = ref[...]


def join(qs):
    return pl.pallas_call(
        join_kernel,
        out_shape=sds((S, LOC)),
        in_specs=[VM] * 4,
        out_specs=VM,
        compiler_params=pltpu.CompilerParams(vmem_limit_bytes=VLIM),
        name="join",
    )(*qs)


def shift(x, axis, by):
    size = lax.axis_size(axis)
    return lax.ppermute(x, axis, [(i, (i + by) % size) for i in range(size)])


def swap(x, axis, bits):
    size = lax.axis_size(axis)
    return lax.ppermute(x, axis, [(i, i ^ bits) for i in range(size)])


def summed(g):
    g = g + swap(g, "dom", 1)
    for axis, unit in (("dom", 2), ("dom", 8), ("band", 1)):
        others = [swap(g, axis, unit * k) for k in (1, 2, 3)]
        g = (g + others[0]) + (others[1] + others[2])
    return g


def body(
    block,
    stiffness,
    cell_scale,
    potential,
    cell_dofs,
    cell_count,
    hang_rows,
    hang_masters,
    hang_weights,
):
    own, hanging = pack(
        cell_dofs.T, potential.T, cell_scale, hang_rows, hang_masters, hang_weights, cell_count
    )
    from_left = shift(own, "dom", 1)
    from_right = shift(own, "dom", -1)
    *hang, start, u0, first, last = prepare(hanging, block)

    def ghosts(first, last):
        return shift(last, "dom", 1), shift(first, "dom", -1)

    gl, gr = ghosts(first, last)
    *cell, base = cell_tables(own, from_left, from_right, hang[0], stiffness)
    args = (cell, base, hang, start)
    u1, first, last = apply_step(1, u0, gl, gr, u0, *args)
    gl, gr = ghosts(first, last)
    u2, first, last = apply_step(2, u1, gl, gr, u0, *args)
    gl, gr = ghosts(first, last)
    qs = apply_step(3, u2, gl, gr, u1, *args)
    qs = [qs[0]] + [shift(qs[k], "band", k) for k in (1, 2, 3)]
    gram, rows = gram_of(qs)
    gram = summed(gram)
    outs = basis_of(gram, rows, LOC * lax.axis_size("dom"))
    outs = [outs[0]] + [shift(outs[k], "band", k) for k in (1, 2, 3)]
    return join(outs)


def solution(mesh):
    return jax.shard_map(
        body,
        mesh=mesh,
        in_specs=(
            P("band", "dom"),
            P(),
            P("dom"),
            P(None, "dom"),
            P(None, "dom"),
            P("dom"),
            P("dom"),
            P(None, "dom"),
            P(None, "dom"),
        ),
        out_specs=P("band", "dom"),
        check_vma=False,
    )
```
